128 devices in a mesh: scen: 8 (over x, core), vec: 16 (over z, y).
Axes of the slice: x: 4, y: 4, z: 4, core: 2. Of those that a mesh axis runs over, the one named last changes fastest.
Arguments:
- rhs: float32 [1536, 128], P('vec'), may hold values from -6 to 6
- diag_cost: float32 [1536, 128], P('vec'), may hold values from 1 to 10
- couple: bfloat16 [128, 24, 128, 128], P(('scen', 'vec')), may hold values from -0.5 to 0.5
- couple_idx: int32 [128, 24], P(('scen', 'vec')), may hold values from 0 to 1535
- factor: bfloat16 [128, 24, 3, 128, 128], P(('scen', 'vec')), may hold values from -0.3125 to 0.3125
- pattern: int32 [128, 24, 2], P(('scen', 'vec')), may hold values 0 or 1
Outputs:
- solution: float32 [1536, 128], P('vec')
- residual: float32 [1536, 128], P('vec')
The draws below stay inside these ranges and needn't reach their ends.
Inputs may be any that keep to these rules, and one draw needn't show every extreme that they name: `couple_idx`: a first-section block index.
All inputs are finite; a program needn't handle non-finite values. No bound on the sum of `pattern` on one device may be relied on, other than what follows from the above.
Results may differ from the reference program's by a relative error of at most 0.017.
Values may be sent and summed in bfloat16 or wider, within the bound.
No kernel may reach another device: no remote copies, remote signals or barrier semaphores. Data moves between devices by JAX's collectives and lax.ppermute only.
A program may use at most 64 MiB of HBM per device.

```python
import math
import jax
import jax.numpy as jnp
from jax import lax

BLOCK = 128
ROWBLOCKS = 24
ITERS = 3
FBLOCKS = 1536
SCENARIOS = 128


def place_ends(drawn, own_key, least, largest):
    extent = drawn.shape
    place = [jax.random.randint(jax.random.fold_in(own_key, axis), (), 0, extent[axis]) for axis in range(len(extent))]
    drawn = drawn.at[tuple(place)].set(least)
    longest = extent.index(max(extent))
    place[longest] = (place[longest] + 1) % extent[longest]
    return drawn.at[tuple(place)].set(largest)


def level_of(rng, shape, split, least, top_value):
    gain, own = 1.0, jax.random.fold_in(rng, 6)
    for position, blocks in split:
        steps = jnp.exp(jax.random.uniform(jax.random.fold_in(own, position), (blocks,), jnp.float32, least / len(split), top_value / len(split)))
        gain = gain * jnp.repeat(steps, shape[position] // blocks).reshape([-1 if axis == position else 1 for axis in range(len(shape))])
    return gain


def noise(key, dims, spread, most, cuts=(), held_as=jnp.bfloat16):
    gain = level_of(key, dims, cuts, -0.22, 0.18) if cuts else 1.0
    drawn = jax.random.normal(key, dims, jnp.float32) * spread * gain
    return jnp.minimum(jnp.maximum(drawn, -most), most).astype(held_as)


def setup_inputs(seed: int = 0) -> dict:
    seeds = jax.random.split(jax.random.key(seed), 7)
    return {
        "rhs": noise(seeds[0], (FBLOCKS, BLOCK), 1.0, 6.0, ((0, 16),), jnp.float32),
        "diag_cost": jnp.clip(jnp.exp(math.log(10.0) - 2.3025851 * jax.random.uniform(seeds[1], (FBLOCKS, BLOCK), jnp.float32) ** level_of(seeds[1], (FBLOCKS, BLOCK), ((0, 16),), -0.2, 0.2)), 1.0, 10.0),
        "couple": noise(seeds[2], (SCENARIOS, ROWBLOCKS, BLOCK, BLOCK), BLOCK ** -0.5, 0.5, ((0, 128),)),
        "couple_idx": place_ends(jax.random.randint(seeds[3], (SCENARIOS, ROWBLOCKS), 0, FBLOCKS), jax.random.fold_in(seeds[3], 1), 0, FBLOCKS - 1).astype(jnp.int32),
        "factor": noise(seeds[4], (SCENARIOS, ROWBLOCKS, 3, BLOCK, BLOCK), (3 * BLOCK) ** -0.5, 0.3125, ((0, 128),)),
        "pattern": place_ends((jax.random.randint(seeds[5], (SCENARIOS, ROWBLOCKS, 2), 0, 2) < 1).astype(jnp.int32), jax.random.fold_in(seeds[5], 1), 0, 1),
    }


def slot_reach(pattern):
    places = jnp.arange(ROWBLOCKS)
    left_side = pattern[:, 0] * (places > 0).astype(jnp.int32)
    right_side = pattern[:, 1] * (places < ROWBLOCKS - 1).astype(jnp.int32)
    middle = jnp.ones((ROWBLOCKS,), jnp.int32)
    return jnp.stack([left_side, middle, right_side], axis=1).astype(jnp.float32)


def scenario_lift(full16, couple, couple_idx, factor, pattern):
    fetched = full16[couple_idx]
    coupled = jnp.einsum("rij,rj->ri", couple.astype(jnp.float32), fetched.astype(jnp.float32)).astype(jnp.bfloat16)
    reach = slot_reach(pattern)
    zero_row = jnp.zeros((1, BLOCK), jnp.bfloat16)
    padded = jnp.concatenate([zero_row, coupled, zero_row], axis=0)
    stacked = jnp.stack([padded[:-2], padded[1:-1], padded[2:]], axis=1).astype(jnp.float32)
    weighted = jnp.einsum("rkij,rkj->ri", factor.astype(jnp.float32), stacked * reach[:, :, None]).astype(jnp.bfloat16)
    spread_back = jnp.einsum("rkij,ri->rkj", factor.astype(jnp.float32), weighted.astype(jnp.float32)) * reach[:, :, None]
    zero_f = jnp.zeros((1, BLOCK), jnp.float32)
    returned = spread_back[:, 1] + jnp.concatenate([spread_back[1:, 0], zero_f], axis=0) + jnp.concatenate([zero_f, spread_back[:-1, 2]], axis=0)
    returned = returned.astype(jnp.bfloat16)
    return jnp.einsum("rij,ri->rj", couple.astype(jnp.float32), returned.astype(jnp.float32))


def schur_apply(direction, diag_cost, couple, couple_idx, factor, pattern):
    full16 = direction.astype(jnp.bfloat16)

    def one_scenario(total, pieces):
        lifted = scenario_lift(full16, pieces[0], pieces[1], pieces[2], pieces[3])
        return total.at[pieces[1]].add(lifted), None

    start_total = jnp.zeros((FBLOCKS, BLOCK), jnp.float32)
    total, unused = lax.scan(one_scenario, start_total, (couple, couple_idx, factor, pattern))
    return diag_cost * direction + total


def reference(rhs, diag_cost, couple, couple_idx, factor, pattern):
    inverse = 1.0 / diag_cost
    solution = jnp.zeros_like(rhs)
    residual = rhs
    precond = inverse * residual
    direction = precond
    rz_now = jnp.sum(residual * precond)
    for iteration in range(ITERS):
        image = schur_apply(direction, diag_cost, couple, couple_idx, factor, pattern)
        step_size = rz_now / jnp.sum(direction * image)
        solution = solution + step_size * direction
        residual = residual - step_size * image
        precond = inverse * residual
        rz_next = jnp.sum(residual * precond)
        direction = precond + (rz_next / rz_now) * direction
        rz_now = rz_next
    return solution, residual
```

```python
import functools

import jax
import jax.numpy as jnp
import numpy as np
from jax import lax
from jax.experimental import pallas as pl
from jax.experimental.pallas import tpu as pltpu
from jax.sharding import Mesh
from jax.sharding import PartitionSpec as P

ROWS = 24
PAD = 32
OWN = 96
WIDTH = 128
CHIPS = 64
GAMMA, DELTA = 4000, 4001
F32, BF16 = jnp.float32, jnp.bfloat16


def dot_nn(a, b):
    return lax.dot_general(a, b, (((1,), (0,)), ((), ())), preferred_element_type=F32)


def dot_nt(a, b):
    return lax.dot_general(a, b, (((1,), (1,)), ((), ())), preferred_element_type=F32)


def only_row(rows, values, r):
    return jnp.where(rows == r, values, 0.0).astype(BF16)


def split(values):
    high = values.astype(BF16).astype(F32)
    return high, values - high


def scenario_lift(y, couple, factor, reach):
    rows = lax.broadcasted_iota(jnp.int32, (PAD, WIDTH), 0)
    left, right = reach[:, 0:1], reach[:, 1:2]
    coupled = jnp.zeros((PAD, WIDTH), F32)
    for r in range(ROWS):
        coupled += dot_nt(only_row(rows, y, r), couple[r])
    coupled = coupled.astype(BF16).astype(F32)
    slots = (pltpu.roll(coupled, 1, 0) * left, coupled, pltpu.roll(coupled, PAD - 1, 0) * right)
    weighted = jnp.zeros((PAD, WIDTH), F32)
    for r in range(ROWS):
        for k in range(3):
            weighted += dot_nt(only_row(rows, slots[k], r), factor[r, k])
    weighted = weighted.astype(BF16).astype(F32)
    spread = [jnp.zeros((PAD, WIDTH), F32) for k in range(3)]
    for r in range(ROWS):
        row = only_row(rows, weighted, r)
        for k in range(3):
            spread[k] += dot_nn(row, factor[r, k])
    returned = (
        spread[1]
        + pltpu.roll(spread[0] * left, PAD - 1, 0)
        + pltpu.roll(spread[2] * right, 1, 0)
    )
    returned = returned.astype(BF16).astype(F32)
    lifted = jnp.zeros((PAD, WIDTH), F32)
    for r in range(ROWS):
        lifted += dot_nn(only_row(rows, returned, r), couple[r])
    return lifted


def message(lifted, gamma, delta, extra):
    rows = lax.broadcasted_iota(jnp.int32, (PAD, WIDTH), 0)
    out = jnp.where(rows < ROWS, lifted, 0.0)
    for place, line in enumerate(split(gamma) + split(delta) + tuple(extra)):
        out = jnp.where(rows == ROWS + place, jnp.broadcast_to(line, out.shape), out)
    return out.astype(BF16)


def column_sum(values):
    return jnp.sum(values, axis=0, keepdims=True)


def first_kernel(
    core_ref, near, far, tgt, label, reach, rhs, diag, share, couple, factor, msg_out, us_out
):
    half = OWN // 2
    core = core_ref[0]
    want = tgt[0:PAD, :]
    us = jnp.zeros((PAD, WIDTH), F32)
    for part, which in ((near, core), (far, 1 - core)):
        place = lax.broadcasted_iota(jnp.int32, (1, 16 * half), 1)
        shard = (place * 1366) >> 16
        block = place + half * shard + half * which
        us += dot_nn((want == block).astype(F32).astype(BF16), part[...])
    us_out[...] = us
    lifted = scenario_lift(us, couple, factor, reach[...])
    own = rhs[...]
    u = own * (1.0 / diag[...])
    gamma = column_sum(own * u) * 0.125
    delta = column_sum(diag[...] * u * u) * 0.125 + column_sum(us * lifted)
    msg_out[0:PAD, :] = message(lifted, gamma, delta, (label[0:1, :], label[1:2, :]))
    rows = lax.broadcasted_iota(jnp.int32, (PAD, WIDTH), 0)
    high, low = split(share[...])
    msg_out[PAD : 2 * PAD, :] = jnp.where(rows < 12, high, low).astype(BF16)


def advance(total, us, inv_s, ps, u, diag, q, d, x, r, gamma_old, alpha_old):
    gamma = jnp.sum(total[ROWS : ROWS + 1, :], axis=1, keepdims=True)
    delta = jnp.sum(total[ROWS + 1 : ROWS + 2, :], axis=1, keepdims=True)
    if gamma_old is None:
        alpha = gamma / delta
    else:
        beta = gamma / gamma_old
        alpha = gamma / (delta - beta * gamma / alpha_old)
    image = total[PAD:, :]
    s = diag * u + image
    if gamma_old is None:
        d, q = u, s
    else:
        d, q = u + beta * d, s + beta * q
    x = alpha * d if x is None else x + alpha * d
    r = r - alpha * q
    if us is not None:
        rows = lax.broadcasted_iota(jnp.int32, (PAD, WIDTH), 0)
        own = jnp.where(rows < ROWS, us + inv_s * total[0:PAD, :], 0.0)
        ps = own if ps is None else own + beta * ps
        us = us - alpha * ps
    return gamma, alpha, us, ps, d, q, x, r


def next_message(us, u, r, diag, couple, factor, reach):
    lifted = scenario_lift(us, couple, factor, reach)
    gamma = column_sum(r * u) * 0.125
    delta = column_sum(diag * u * u) * 0.125 + column_sum(us * lifted)
    return message(lifted, gamma, delta, ())


def second_kernel(
    core_ref, near, far, tgt, us, reach, rhs, diag, couple, factor,
    msg_out, hot_out, us_out, ps_out, inv_out, scal_out, d_out, q_out, x_out, r_out,
):
    core = core_ref[0]
    want = tgt[...]
    lane = lax.broadcasted_iota(jnp.int32, (1, WIDTH), 1)
    slot = lane & (PAD - 1)
    fixed = jnp.where(slot < ROWS + 2, GAMMA, jnp.where(slot < ROWS + 4, DELTA, -1))
    sums = []
    inverse = jnp.zeros((PAD, WIDTH), F32)
    for number, (part, which) in enumerate(((near, core), (far, 1 - core))):
        total = jnp.zeros((PAD + OWN, WIDTH), F32)
        for chunk in range(CHIPS // 4):
            tiles = [part[4 * chunk + m] for m in range(4)]
            ends = [t[ROWS:PAD, :].astype(F32) for t in tiles]
            ends = ends[0] + ends[1] + ends[2] + ends[3]
            found = (ends[4:5, :] * 64.0 + ends[5:6, :]).astype(jnp.int32)
            block = jnp.where(slot < ROWS, found, fixed)
            hot = (want == block).astype(F32).astype(BF16)
            hot_out[number, chunk] = hot
            total += dot_nn(hot, jnp.concatenate([t[0:PAD, :] for t in tiles], axis=0))
            place = chunk * 4 + (lane >> 5)
            member = jnp.where(slot < 12, slot, slot - 12)
            shard = (place & 15) * OWN + ((place >> 4) * 2 + which) * 12 + member
            shard = jnp.where(slot < 24, shard, -1)
            pick = (want[0:PAD, :] == shard).astype(F32).astype(BF16)
            inverse += dot_nn(pick, jnp.concatenate([t[PAD:, :] for t in tiles], axis=0))
        sums.append(total)
    total = sums[0] + sums[1]
    own = rhs[...]
    cost = diag[...]
    inv = 1.0 / cost
    gamma, alpha, u_s, p_s, d, q, x, r = advance(
        total, us[...], inverse, None, inv * own, cost, None, None, None, own, None, None
    )
    us_out[...], ps_out[...], inv_out[...] = u_s, p_s, inverse
    d_out[...], q_out[...], x_out[...], r_out[...] = d, q, x, r
    scal_out[0:1, :] = jnp.broadcast_to(gamma, (1, WIDTH))
    scal_out[1:2, :] = jnp.broadcast_to(alpha, (1, WIDTH))
    msg_out[...] = next_message(u_s, inv * r, r, cost, couple, factor, reach[...])


def gathered(near, far, hot):
    sums = []
    for number, part in enumerate((near, far)):
        total = jnp.zeros((PAD + OWN, WIDTH), F32)
        for chunk in range(CHIPS // 4):
            total += dot_nn(hot[number, chunk], part[128 * chunk : 128 * chunk + 128, :])
        sums.append(total)
    return sums[0] + sums[1]


def third_kernel(
    near, far, hot, us, ps, inv_s, scal, d, q, x, r, reach, diag, couple, factor,
    msg_out, us_out, ps_out, scal_out, d_out, q_out, x_out, r_out,
):
    total = gathered(near, far, hot)
    cost = diag[...]
    inv = 1.0 / cost
    gamma, alpha, u_s, p_s, dn, qn, xn, rn = advance(
        total, us[...], inv_s[...], ps[...], inv * r[...], cost, q[...], d[...], x[...], r[...],
        scal[0:1, 0:1], scal[1:2, 0:1],
    )
    us_out[...], ps_out[...] = u_s, p_s
    d_out[...], q_out[...], x_out[...], r_out[...] = dn, qn, xn, rn
    scal_out[0:1, :] = jnp.broadcast_to(gamma, (1, WIDTH))
    scal_out[1:2, :] = jnp.broadcast_to(alpha, (1, WIDTH))
    msg_out[...] = next_message(u_s, inv * rn, rn, cost, couple, factor, reach[...])


def last_kernel(near, far, hot, scal, d, q, x, r, diag, x_out, r_out):
    total = gathered(near, far, hot)
    cost = diag[...]
    found = advance(
        total, None, None, None, r[...] / cost, cost, q[...], d[...], x[...], r[...],
        scal[0:1, 0:1], scal[1:2, 0:1],
    )
    x_out[...], r_out[...] = found[6], found[7]


def call(kernel, shapes, *args, scalars=0):
    vmem = pl.BlockSpec(memory_space=pltpu.VMEM)
    specs = [pl.BlockSpec(memory_space=pltpu.SMEM)] * scalars + [vmem] * (len(args) - scalars)
    return pl.pallas_call(
        kernel,
        out_shape=[jax.ShapeDtypeStruct(s, t) for s, t in shapes],
        in_specs=specs,
        out_specs=[vmem] * len(shapes),
        compiler_params=pltpu.CompilerParams(vmem_limit_bytes=24 * 1024 * 1024),
    )(*args)


def share_out(block, axes, count):
    return lax.all_to_all(
        jnp.broadcast_to(block[None], (count,) + block.shape), axes, 0, 0, tiled=True
    )


def other_core(values):
    return lax.ppermute(values, "core", [(0, 1), (1, 0)])


def shards(rhs, diag, couple, couple_idx, factor, pattern):
    couple, factor = couple[0], factor[0]
    core = lax.axis_index("core")
    vec = lax.axis_index("z") * 4 + lax.axis_index("y")
    inv = 1.0 / diag
    half = OWN // 2
    sent = lax.dynamic_slice_in_dim((rhs * inv).astype(BF16), core * half, half, 0)
    near = share_out(sent, ("z", "y"), 16).reshape(16 * half, WIDTH)
    far = other_core(near)

    idx = couple_idx[0]
    tgt = jnp.concatenate(
        [idx, jnp.array([GAMMA, DELTA] + [-2] * 6, jnp.int32), vec * OWN + jnp.arange(OWN)]
    )[:, None]
    spaced = jnp.tile(jnp.pad(idx, (0, PAD - ROWS)), 4)
    spaced = jnp.where(jnp.arange(WIDTH) // PAD == lax.axis_index("y"), spaced, 0)
    label = jnp.stack([spaced >> 6, spaced & 63]).astype(F32)
    place = jnp.arange(ROWS)
    reach = jnp.stack(
        [pattern[0, :, 0] * (place > 0), pattern[0, :, 1] * (place < ROWS - 1)], axis=1
    ).astype(F32)
    reach = jnp.pad(reach, ((0, PAD - ROWS), (0, 0)))
    eighth = lax.dynamic_slice_in_dim(inv, (lax.axis_index("x") * 2 + core) * 12, 12, 0)
    share = jnp.concatenate([eighth, eighth, jnp.zeros((8, WIDTH), F32)], axis=0)
    core_arg = core[None]

    scen, own, msg = ((PAD, WIDTH), F32), ((OWN, WIDTH), F32), ((PAD, WIDTH), BF16)
    scal = ((2, WIDTH), F32)
    sent, us = call(
        first_kernel, [((2 * PAD, WIDTH), BF16), scen],
        core_arg, near, far, tgt, label, reach, rhs, diag, share, couple, factor, scalars=1,
    )
    near = share_out(sent, ("x", "z", "y"), CHIPS)
    far = other_core(near)
    sent, hot, us, ps, inv_s, sc, d, q, x, r = call(
        second_kernel,
        [msg, ((2, CHIPS // 4, PAD + OWN, WIDTH), BF16), scen, scen, scen, scal, own, own, own, own],
        core_arg, near, far, tgt, us, reach, rhs, diag, couple, factor, scalars=1,
    )
    near = share_out(sent, ("x", "z", "y"), CHIPS).reshape(CHIPS * PAD, WIDTH)
    far = other_core(near)
    sent, us, ps, sc, d, q, x, r = call(
        third_kernel, [msg, scen, scen, scal, own, own, own, own],
        near, far, hot, us, ps, inv_s, sc, d, q, x, r, reach, diag, couple, factor,
    )
    near = share_out(sent, ("x", "z", "y"), CHIPS).reshape(CHIPS * PAD, WIDTH)
    far = other_core(near)
    x, r = call(last_kernel, [own, own], near, far, hot, sc, d, q, x, r, diag)
    return x, r


def solution(mesh):
    fine = Mesh(np.array(mesh.devices).reshape(4, 2, 4, 4), ("x", "core", "z", "y"))
    vec, scen = ("z", "y"), ("x", "core", "z", "y")
    in_specs = (
        P(vec, None),
        P(vec, None),
        P(scen, None, None, None),
        P(scen, None),
        P(scen, None, None, None, None),
        P(scen, None, None),
    )
    out_specs = (P(vec, None), P(vec, None))
    return jax.shard_map(shards, mesh=fine, in_specs=in_specs, out_specs=out_specs, check_vma=False)
```

```python
import jax
import jax.numpy as jnp
import numpy as np
from jax import lax
from jax.experimental import pallas as pl
from jax.experimental.pallas import tpu as pltpu
from jax.sharding import Mesh
from jax.sharding import PartitionSpec as P

ROWS = 24
PAD = 32
OWN = 96
HALF = OWN // 2
WIDTH = 128
CHIPS = 64
PLANE = 16
GAMMA, DELTA = 4000, 4001
INVERSE = 2048
F32, BF16 = jnp.float32, jnp.bfloat16


def dot_nn(a, b):
    return lax.dot_general(a, b, (((1,), (0,)), ((), ())), preferred_element_type=F32)


def dot_nt(a, b):
    return lax.dot_general(a, b, (((1,), (1,)), ((), ())), preferred_element_type=F32)


def split(values):
    high = values.astype(BF16).astype(F32)
    return high, values - high


def hot_of(mask):
    return mask.astype(F32).astype(BF16)


def by_row(values):
    rows = lax.broadcasted_iota(jnp.int32, (PAD, WIDTH), 0)
    return jnp.concatenate(
        [jnp.where(rows == r, values, 0.0).astype(BF16) for r in range(ROWS)], axis=1
    )


def fetch(first_hbm, second_hbm, first, second, sems):
    copies = (
        pltpu.make_async_copy(first_hbm, first, sems.at[0]),
        pltpu.make_async_copy(second_hbm, second, sems.at[1]),
    )
    for copy in copies:
        copy.start()
    return copies


def scenario_lift(y, copies, couple, factor, reach):
    left, right = reach[:, 0:1], reach[:, 1:2]
    copies[0].wait()
    beside = jnp.concatenate([couple[r] for r in range(ROWS)], axis=1)
    coupled = dot_nt(by_row(y), beside).astype(BF16).astype(F32)
    slots = jnp.concatenate(
        [pltpu.roll(coupled, 1, 0) * left, coupled, pltpu.roll(coupled, PAD - 1, 0) * right], axis=1
    ).astype(BF16)
    copies[1].wait()
    lane = lax.broadcasted_iota(jnp.int32, (WIDTH, PAD), 1)
    weighted = jnp.zeros((WIDTH, PAD), F32)
    for r in range(ROWS):
        blocks = jnp.concatenate([factor[r, k] for k in range(3)], axis=1)
        weighted = jnp.where(lane == r, dot_nt(blocks, slots), weighted)
    weighted = weighted.T.astype(BF16).astype(F32)
    rows = lax.broadcasted_iota(jnp.int32, (PAD, WIDTH), 0)
    spread = jnp.zeros((PAD, 3 * WIDTH), F32)
    for r in range(0, ROWS, 2):
        pair = [jnp.where(rows == r + i, weighted, 0.0).astype(BF16) for i in range(2)]
        blocks = [factor[r : r + 2, k].reshape(2 * WIDTH, WIDTH) for k in range(3)]
        spread += dot_nn(jnp.concatenate(pair, axis=1), jnp.concatenate(blocks, axis=1))
    returned = (
        spread[:, WIDTH : 2 * WIDTH]
        + pltpu.roll(spread[:, :WIDTH] * left, PAD - 1, 0)
        + pltpu.roll(spread[:, 2 * WIDTH :] * right, 1, 0)
    )
    returned = returned.astype(BF16).astype(F32)
    return dot_nn(by_row(returned), couple[...].reshape(ROWS * WIDTH, WIDTH))


def message(lifted, gamma, delta, extra):
    rows = lax.broadcasted_iota(jnp.int32, (PAD, WIDTH), 0)
    out = jnp.where(rows < ROWS, lifted, 0.0)
    for place, line in enumerate(split(gamma) + split(delta) + tuple(extra)):
        out = jnp.where(rows == ROWS + place, jnp.broadcast_to(line, out.shape), out)
    return out.astype(BF16)


def column_sum(values):
    return jnp.sum(values, axis=0, keepdims=True)


def next_message(us, u, r, cost, copies, couple, factor, reach, extra=()):
    lifted = scenario_lift(us, copies, couple, factor, reach)
    gamma = column_sum(r * u) * 0.125
    delta = column_sum(cost * u * u) * 0.125 + column_sum(us * lifted)
    return message(lifted, gamma, delta, extra)


def opening_kernel(core_ref, rhs_hbm, diag_hbm, msg_out, r_out, cost_out, rhs, diag, sems):
    for copy in fetch(rhs_hbm, diag_hbm, rhs, diag, sems):
        copy.wait()
    r_out[...], cost_out[...] = rhs[...], diag[...]
    mine = pl.ds(pl.multiple_of(core_ref[0] * HALF, HALF), HALF)
    inverse = 1.0 / diag[mine, :]
    u = (rhs[mine, :] * inverse).astype(BF16)
    inverse = inverse.astype(BF16)
    for place in range(PLANE):
        msg_out[place, 0:HALF, :] = u
        msg_out[place, HALF:OWN, :] = inverse


def first_kernel(
    core_ref, near, far, tgt, label, reach, own, cost, couple_hbm, factor_hbm,
    msg_out, us_out, inv_out, couple, factor, sems,
):
    copies = fetch(couple_hbm, factor_hbm, couple, factor, sems)
    core = core_ref[0]
    want = tgt[0:PAD, :]
    want = jnp.concatenate([want, want + INVERSE], axis=0)
    found = jnp.zeros((2 * PAD, WIDTH), F32)
    for part, which in ((near, core), (far, 1 - core)):
        place = lax.broadcasted_iota(jnp.int32, (1, PLANE * OWN), 1)
        member = place - OWN * ((place * 683) >> 16)
        block = place + HALF * which + jnp.where(member < HALF, 0, INVERSE - HALF)
        found += dot_nn(hot_of(want == block), part[...])
    us = found[0:PAD, :]
    us_out[...], inv_out[...] = us, found[PAD:, :]
    r, d = own[...], cost[...]
    msg_out[...] = next_message(
        us, r * (1.0 / d), r, d, copies, couple, factor, reach[...], (label[0:1, :], label[1:2, :])
    )


def advance(total, us, inv_s, ps, u, cost, q, d, x, r, gamma_old, alpha_old):
    gamma = jnp.sum(total[ROWS : ROWS + 1, :], axis=1, keepdims=True)
    delta = jnp.sum(total[ROWS + 1 : ROWS + 2, :], axis=1, keepdims=True)
    if gamma_old is None:
        alpha = gamma / delta
    else:
        beta = gamma / gamma_old
        alpha = gamma / (delta - beta * gamma / alpha_old)
    s = cost * u + total[PAD:, :]
    if gamma_old is None:
        d, q = u, s
    else:
        d, q = u + beta * d, s + beta * q
    x = alpha * d if x is None else x + alpha * d
    r = r - alpha * q
    if us is not None:
        rows = lax.broadcasted_iota(jnp.int32, (PAD, WIDTH), 0)
        own = jnp.where(rows < ROWS, us + inv_s * total[0:PAD, :], 0.0)
        ps = own if ps is None else own + beta * ps
        us = us - alpha * ps
    return gamma, alpha, us, ps, d, q, x, r


def second_kernel(
    near, far, tgt, us, inv_s, reach, own, cost, couple_hbm, factor_hbm,
    msg_out, hot_out, us_out, ps_out, scal_out, d_out, q_out, x_out, r_out,
    couple, factor, sems,
):
    copies = fetch(couple_hbm, factor_hbm, couple, factor, sems)
    want = tgt[...]
    lane = lax.broadcasted_iota(jnp.int32, (1, WIDTH), 1)
    slot = lane & (PAD - 1)
    fixed = jnp.where(slot < ROWS + 2, GAMMA, jnp.where(slot < ROWS + 4, DELTA, -1))
    sums = []
    for number, part in enumerate((near, far)):
        for chunk in range(CHIPS // 4):
            start = WIDTH * chunk
            ends = [part[start + PAD * m + 16 : start + PAD * (m + 1), :].astype(F32) for m in range(4)]
            ends = ends[0] + ends[1] + ends[2] + ends[3]
            found = (ends[12:13, :] * 64.0 + ends[13:14, :]).astype(jnp.int32)
            block = jnp.where(slot < ROWS, found, fixed)
            hot_out[number, :, start : start + WIDTH] = hot_of(want == block)
        sums.append(dot_nn(hot_out[number], part[...]))
    total = sums[0] + sums[1]
    d = cost[...]
    inv = 1.0 / d
    r = own[...]
    gamma, alpha, u_s, p_s, dn, qn, xn, rn = advance(
        total, us[...], inv_s[...], None, inv * r, d, None, None, None, r, None, None
    )
    us_out[...], ps_out[...] = u_s, p_s
    d_out[...], q_out[...], x_out[...], r_out[...] = dn, qn, xn, rn
    scal_out[0:1, :] = jnp.broadcast_to(gamma, (1, WIDTH))
    scal_out[1:2, :] = jnp.broadcast_to(alpha, (1, WIDTH))
    msg_out[...] = next_message(u_s, inv * rn, rn, d, copies, couple, factor, reach[...])


def third_kernel(
    near, far, hot, us, ps, inv_s, scal, d, q, x, r, reach, cost, couple_hbm, factor_hbm,
    msg_out, scal_out, d_out, q_out, x_out, r_out,
    couple, factor, sems,
):
    copies = fetch(couple_hbm, factor_hbm, couple, factor, sems)
    total = dot_nn(hot[0], near[...]) + dot_nn(hot[1], far[...])
    c = cost[...]
    inv = 1.0 / c
    gamma, alpha, u_s, p_s, dn, qn, xn, rn = advance(
        total, us[...], inv_s[...], ps[...], inv * r[...], c, q[...], d[...], x[...], r[...],
        scal[0:1, 0:1], scal[1:2, 0:1],
    )
    d_out[...], q_out[...], x_out[...], r_out[...] = dn, qn, xn, rn
    scal_out[0:1, :] = jnp.broadcast_to(gamma, (1, WIDTH))
    scal_out[1:2, :] = jnp.broadcast_to(alpha, (1, WIDTH))
    msg_out[...] = next_message(u_s, inv * rn, rn, c, copies, couple, factor, reach[...])


def last_kernel(near, far, hot, scal, d, q, x, r, cost, x_out, r_out):
    total = dot_nn(hot[0], near[...]) + dot_nn(hot[1], far[...])
    c = cost[...]
    found = advance(
        total, None, None, None, r[...] / c, c, q[...], d[...], x[...], r[...],
        scal[0:1, 0:1], scal[1:2, 0:1],
    )
    x_out[...], r_out[...] = found[6], found[7]


def call(kernel, shapes, *args, scalars=0, weights=()):
    vmem = pl.BlockSpec(memory_space=pltpu.VMEM)
    specs = [pl.BlockSpec(memory_space=pltpu.SMEM)] * scalars + [vmem] * (len(args) - scalars)
    specs += [pl.BlockSpec(memory_space=pltpu.HBM)] * len(weights)
    scratch = [pltpu.VMEM(w.shape, w.dtype) for w in weights]
    if weights:
        scratch.append(pltpu.SemaphoreType.DMA((len(weights),)))
    return pl.pallas_call(
        kernel,
        out_shape=[jax.ShapeDtypeStruct(s, t) for s, t in shapes],
        in_specs=specs,
        out_specs=[vmem] * len(shapes),
        scratch_shapes=scratch,
        compiler_params=pltpu.CompilerParams(vmem_limit_bytes=48 * 1024 * 1024),
    )(*args, *weights)


def in_hbm(*arrays):
    return [pltpu.with_memory_space_constraint(a, pltpu.HBM) for a in arrays]


def other_core(values):
    return lax.ppermute(values, "core", [(0, 1), (1, 0)])


def exchange(sent):
    copies = jnp.broadcast_to(sent[None], (CHIPS,) + sent.shape)
    near = lax.all_to_all(copies, ("x", "z", "y"), 0, 0, tiled=True).reshape(CHIPS * PAD, WIDTH)
    return near, other_core(near)


def shards(rhs, diag, couple, couple_idx, factor, pattern):
    weights = in_hbm(couple[0], factor[0])
    scen, own, msg = ((PAD, WIDTH), F32), ((OWN, WIDTH), F32), ((PAD, WIDTH), BF16)
    scal = ((2, WIDTH), F32)
    core = lax.axis_index("core")[None]
    vec = lax.axis_index("z") * 4 + lax.axis_index("y")
    sent, r, cost = call(
        opening_kernel, [((PLANE, OWN, WIDTH), BF16), own, own], core, scalars=1, weights=in_hbm(rhs, diag)
    )
    near = lax.all_to_all(sent, ("z", "y"), 0, 0, tiled=True).reshape(PLANE * OWN, WIDTH)
    far = other_core(near)

    idx = couple_idx[0]
    tgt = jnp.concatenate(
        [idx, jnp.array([GAMMA, DELTA] + [-9] * 6, jnp.int32), vec * OWN + jnp.arange(OWN)]
    )[:, None]
    spaced = jnp.tile(jnp.pad(idx, (0, PAD - ROWS)), 4)
    spaced = jnp.where(jnp.arange(WIDTH) // PAD == lax.axis_index("y"), spaced, 0)
    label = jnp.stack([spaced >> 6, spaced & 63]).astype(F32)
    place = jnp.arange(ROWS)
    reach = jnp.stack(
        [pattern[0, :, 0] * (place > 0), pattern[0, :, 1] * (place < ROWS - 1)], axis=1
    ).astype(F32)
    reach = jnp.pad(reach, ((0, PAD - ROWS), (0, 0)))

    sent, us, inv_s = call(
        first_kernel, [msg, scen, scen],
        core, near, far, tgt, label, reach, r, cost, scalars=1, weights=weights,
    )
    near, far = exchange(sent)
    sent, hot, us, ps, sc, d, q, x, r = call(
        second_kernel,
        [msg, ((2, PAD + OWN, CHIPS * PAD), BF16), scen, scen, scal, own, own, own, own],
        near, far, tgt, us, inv_s, reach, r, cost, weights=weights,
    )
    near, far = exchange(sent)
    sent, sc, d, q, x, r = call(
        third_kernel, [msg, scal, own, own, own, own],
        near, far, hot, us, ps, inv_s, sc, d, q, x, r, reach, cost, weights=weights,
    )
    near, far = exchange(sent)
    return call(last_kernel, [own, own], near, far, hot, sc, d, q, x, r, cost)


def solution(mesh):
    fine = Mesh(np.array(mesh.devices).reshape(4, 2, 4, 4), ("x", "core", "z", "y"))
    vec, scen = ("z", "y"), ("x", "core", "z", "y")
    in_specs = (
        P(vec, None),
        P(vec, None),
        P(scen, None, None, None),
        P(scen, None),
        P(scen, None, None, None, None),
        P(scen, None, None),
    )
    out_specs = (P(vec, None), P(vec, None))
    return jax.shard_map(shards, mesh=fine, in_specs=in_specs, out_specs=out_specs, check_vma=False)
```

```python
import jax
import jax.numpy as jnp
import numpy as np
from jax import lax
from jax.experimental import pallas as pl
from jax.experimental.pallas import tpu as pltpu
from jax.sharding import Mesh
from jax.sharding import PartitionSpec as P

ROWS = 24
PAD = 32
OWN = 96
HALF = OWN // 2
WIDTH = 128
CHIPS = 64
PLANE = 16
BANDS = 5
GAMMA, DELTA = 4000, 4001
INVERSE = 2048
F32, BF16 = jnp.float32, jnp.bfloat16


def dot_nn(a, b):
    return lax.dot_general(a, b, (((1,), (0,)), ((), ())), preferred_element_type=F32)


def dot_nt(a, b):
    return lax.dot_general(a, b, (((1,), (1,)), ((), ())), preferred_element_type=F32)


def split(values):
    high = values.astype(BF16).astype(F32)
    return high, values - high


def hot_of(mask):
    return mask.astype(F32).astype(BF16)


def only_row(values, r):
    rows = lax.broadcasted_iota(jnp.int32, (PAD, WIDTH), 0)
    return jnp.where(rows == r, values, 0.0).astype(BF16)


def scenario_lift(y, normal):
    spread = jnp.zeros((PAD, BANDS * WIDTH), F32)
    for r in range(0, ROWS, 2):
        pair = jnp.concatenate([only_row(y, r), only_row(y, r + 1)], axis=1)
        spread += dot_nn(pair, normal[r : r + 2].reshape(2 * WIDTH, BANDS * WIDTH))
    lifted = spread[:, 2 * WIDTH : 3 * WIDTH]
    for band in (0, 1, 3, 4):
        part = spread[:, band * WIDTH : (band + 1) * WIDTH]
        lifted += pltpu.roll(part, (band - 2) % PAD, 0)
    return lifted


def message(lifted, gamma, delta, extra):
    rows = lax.broadcasted_iota(jnp.int32, (PAD, WIDTH), 0)
    out = jnp.where(rows < ROWS, lifted, 0.0)
    for place, line in enumerate(split(gamma) + split(delta) + tuple(extra)):
        out = jnp.where(rows == ROWS + place, jnp.broadcast_to(line, out.shape), out)
    return out.astype(BF16)


def column_sum(values):
    return jnp.sum(values, axis=0, keepdims=True)


def next_message(us, u, r, cost, normal, extra=()):
    lifted = scenario_lift(us, normal)
    gamma = column_sum(r * u) * 0.125
    delta = column_sum(cost * u * u) * 0.125 + column_sum(us * lifted)
    return message(lifted, gamma, delta, extra)


def opening_kernel(ids, rhs_hbm, diag_hbm, msg_out, r_out, cost_out, rhs, diag, sems):
    copies = (
        pltpu.make_async_copy(rhs_hbm, rhs, sems.at[0]),
        pltpu.make_async_copy(diag_hbm, diag, sems.at[1]),
    )
    for copy in copies:
        copy.start()
    for copy in copies:
        copy.wait()
    r_out[...], cost_out[...] = rhs[...], diag[...]
    mine = pl.ds(pl.multiple_of(ids[0] * HALF, HALF), HALF)
    inverse = 1.0 / diag[mine, :]
    u = (rhs[mine, :] * inverse).astype(BF16)
    inverse = inverse.astype(BF16)
    for place in range(PLANE):
        msg_out[place, 0:HALF, :] = u
        msg_out[place, HALF:OWN, :] = inverse


def normal_kernel(
    ids, idx, pattern, couple_hbm, factor_hbm, normal, tgt, label, couple, factor, prod, flip, sems
):
    third = ROWS // 3
    copies = [pltpu.make_async_copy(couple_hbm, couple, sems.at[0])]
    for part in range(3):
        rows = pl.ds(part * third, third)
        copies.append(
            pltpu.make_async_copy(factor_hbm.at[rows], factor.at[rows], sems.at[1 + part])
        )
    for copy in copies:
        copy.start()

    square = (ROWS, ROWS)
    same = lax.broadcasted_iota(jnp.int32, square, 0) == lax.broadcasted_iota(jnp.int32, square, 1)
    column = jnp.where(same, jnp.broadcast_to(idx[...], square), 0)
    column = jnp.sum(column.astype(F32), axis=1, keepdims=True).astype(jnp.int32)
    rows = lax.broadcasted_iota(jnp.int32, (PAD + OWN, WIDTH), 0)
    fixed = jnp.where(rows < ROWS + 2, rows - ROWS + GAMMA, -9)
    fixed = jnp.where(rows < PAD, fixed, rows - PAD + ids[2] * OWN)
    tgt[...] = fixed
    column = jnp.broadcast_to(column, (ROWS, WIDTH))
    tgt[0:ROWS, :] = column
    lanes = lax.broadcasted_iota(jnp.int32, (ROWS, WIDTH), 1)
    place = lax.broadcasted_iota(jnp.int32, (ROWS, WIDTH), 0) + PAD * ids[1]
    for line, values in enumerate((column >> 6, column & 63)):
        label[line : line + 1, :] = column_sum(jnp.where(lanes == place, values, 0).astype(F32))

    side = pattern[...].astype(F32)
    zeros = jnp.zeros((WIDTH, WIDTH), BF16)
    copies[0].wait()
    for r in range(ROWS):
        if r % third == 0:
            copies[1 + r // third].wait()
        for k in range(3):
            c = r + k - 1
            if not 0 <= c < ROWS:
                continue
            block = dot_nn(factor[r, k], couple[c])
            if k != 1:
                block = block * side[r : r + 1, k // 2 : k // 2 + 1]
            block = block.astype(BF16)
            prod[r, k] = block
            flip[c, :, (2 - k) * WIDTH : (3 - k) * WIDTH] = block.T
    for d in range(ROWS):
        for band in range(BANDS):
            c = d + band - 2
            if not 0 <= c < ROWS:
                normal[d, :, band * WIDTH : (band + 1) * WIDTH] = zeros
                continue
            if band < 2:
                continue
            terms = [r for r in (d - 1, d, d + 1) if 0 <= r < ROWS and abs(r - c) <= 1]
            first = terms[0] - d + 1
            left = flip[d, :, first * WIDTH : (first + len(terms)) * WIDTH]
            right = jnp.concatenate([prod[r, c - r + 1] for r in terms], axis=0)
            block = dot_nn(left, right).astype(BF16)
            normal[d, :, band * WIDTH : (band + 1) * WIDTH] = block
            if c != d:
                normal[c, :, (4 - band) * WIDTH : (5 - band) * WIDTH] = block.T


def first_kernel(ids, near, far, tgt, label, own, cost, normal, msg_out, us_out, inv_out):
    want = tgt[0:PAD, 0:1]
    want = jnp.concatenate([want, want + INVERSE], axis=0)
    found = jnp.zeros((2 * PAD, WIDTH), F32)
    for part, which in ((near, ids[0]), (far, 1 - ids[0])):
        place = lax.broadcasted_iota(jnp.int32, (1, PLANE * OWN), 1)
        member = place - OWN * ((place * 683) >> 16)
        block = place + HALF * which + jnp.where(member < HALF, 0, INVERSE - HALF)
        found += dot_nn(hot_of(want == block), part[...])
    us = found[0:PAD, :]
    us_out[...], inv_out[...] = us, found[PAD:, :]
    r, d = own[...], cost[...]
    msg_out[...] = next_message(us, r * (1.0 / d), r, d, normal, (label[0:1, :], label[1:2, :]))


def label_sum(part, tgt, hot_out, sum_out):
    want = tgt[...]
    lane = lax.broadcasted_iota(jnp.int32, (1, WIDTH), 1)
    slot = lane & (PAD - 1)
    fixed = jnp.where(slot < ROWS + 2, GAMMA, jnp.where(slot < ROWS + 4, DELTA, -1))
    for chunk in range(CHIPS // 4):
        start = WIDTH * chunk
        ends = [part[start + PAD * m + 16 : start + PAD * (m + 1), :].astype(F32) for m in range(4)]
        ends = ends[0] + ends[1] + ends[2] + ends[3]
        found = (ends[12:13, :] * 64.0 + ends[13:14, :]).astype(jnp.int32)
        block = jnp.where(slot < ROWS, found, fixed)
        hot_out[:, start : start + WIDTH] = hot_of(want == block)
    sum_out[...] = dot_nn(hot_out[...], part[...])


def near_sum(part, hot, sum_out):
    sum_out[...] = dot_nn(hot[...], part[...])


def advance(total, us, inv_s, ps, u, cost, q, d, x, r, gamma_old, alpha_old):
    gamma = jnp.sum(total[ROWS : ROWS + 1, :], axis=1, keepdims=True)
    delta = jnp.sum(total[ROWS + 1 : ROWS + 2, :], axis=1, keepdims=True)
    if gamma_old is None:
        alpha = gamma / delta
    else:
        beta = gamma / gamma_old
        alpha = gamma / (delta - beta * gamma / alpha_old)
    s = cost * u + total[PAD:, :]
    if gamma_old is None:
        d, q = u, s
    else:
        d, q = u + beta * d, s + beta * q
    x = alpha * d if x is None else x + alpha * d
    r = r - alpha * q
    if us is not None:
        rows = lax.broadcasted_iota(jnp.int32, (PAD, WIDTH), 0)
        own = jnp.where(rows < ROWS, us + inv_s * total[0:PAD, :], 0.0)
        ps = own if ps is None else own + beta * ps
        us = us - alpha * ps
    return gamma, alpha, us, ps, d, q, x, r


def second_kernel(
    far, tgt, half, us, inv_s, own, cost, normal,
    msg_out, hot_out, us_out, ps_out, scal_out, d_out, q_out, x_out, r_out, other,
):
    label_sum(far, tgt, hot_out, other)
    total = half[...] + other[...]
    d = cost[...]
    inv = 1.0 / d
    r = own[...]
    gamma, alpha, u_s, p_s, dn, qn, xn, rn = advance(
        total, us[...], inv_s[...], None, inv * r, d, None, None, None, r, None, None
    )
    us_out[...], ps_out[...] = u_s, p_s
    d_out[...], q_out[...], x_out[...], r_out[...] = dn, qn, xn, rn
    scal_out[0:1, :] = jnp.broadcast_to(gamma, (1, WIDTH))
    scal_out[1:2, :] = jnp.broadcast_to(alpha, (1, WIDTH))
    msg_out[...] = next_message(u_s, inv * rn, rn, d, normal)


def third_kernel(
    far, hot, half, us, ps, inv_s, scal, d, q, x, r, cost, normal,
    msg_out, scal_out, d_out, q_out, x_out, r_out,
):
    total = half[...] + dot_nn(hot[...], far[...])
    c = cost[...]
    inv = 1.0 / c
    gamma, alpha, u_s, p_s, dn, qn, xn, rn = advance(
        total, us[...], inv_s[...], ps[...], inv * r[...], c, q[...], d[...], x[...], r[...],
        scal[0:1, 0:1], scal[1:2, 0:1],
    )
    d_out[...], q_out[...], x_out[...], r_out[...] = dn, qn, xn, rn
    scal_out[0:1, :] = jnp.broadcast_to(gamma, (1, WIDTH))
    scal_out[1:2, :] = jnp.broadcast_to(alpha, (1, WIDTH))
    msg_out[...] = next_message(u_s, inv * rn, rn, c, normal)


def last_kernel(far, hot, half, scal, d, q, x, r, cost, x_out, r_out):
    total = half[...] + dot_nn(hot[...], far[...])
    c = cost[...]
    found = advance(
        total, None, None, None, r[...] / c, c, q[...], d[...], x[...], r[...],
        scal[0:1, 0:1], scal[1:2, 0:1],
    )
    x_out[...], r_out[...] = found[6], found[7]


def call(kernel, shapes, *args, scalars=0, weights=(), scratch=(), sems=0):
    vmem = pl.BlockSpec(memory_space=pltpu.VMEM)
    specs = [pl.BlockSpec(memory_space=pltpu.SMEM)] * scalars + [vmem] * (len(args) - scalars)
    specs += [pl.BlockSpec(memory_space=pltpu.HBM)] * len(weights)
    scratch = [pltpu.VMEM(s, t) for s, t in scratch]
    if sems:
        scratch.append(pltpu.SemaphoreType.DMA((sems,)))
    return pl.pallas_call(
        kernel,
        out_shape=[jax.ShapeDtypeStruct(s, t) for s, t in shapes],
        in_specs=specs,
        out_specs=[vmem] * len(shapes),
        scratch_shapes=scratch,
        compiler_params=pltpu.CompilerParams(vmem_limit_bytes=32 * 1024 * 1024),
    )(*args, *weights)


def in_hbm(*arrays):
    return [pltpu.with_memory_space_constraint(a, pltpu.HBM) for a in arrays]


def other_core(values):
    return lax.ppermute(values, "core", [(0, 1), (1, 0)])


def exchange(sent):
    copies = jnp.broadcast_to(sent[None], (CHIPS,) + sent.shape)
    near = lax.all_to_all(copies, ("x", "z", "y"), 0, 0, tiled=True).reshape(CHIPS * PAD, WIDTH)
    return near, other_core(near)


def shards(rhs, diag, couple, couple_idx, factor, pattern):
    scen, own, msg = ((PAD, WIDTH), F32), ((OWN, WIDTH), F32), ((PAD, WIDTH), BF16)
    scal, sums = ((2, WIDTH), F32), ((PAD + OWN, WIDTH), F32)
    hots = ((PAD + OWN, CHIPS * PAD), BF16)
    vec = lax.axis_index("z") * 4 + lax.axis_index("y")
    ids = jnp.stack([lax.axis_index("core"), lax.axis_index("y"), vec]).astype(jnp.int32)
    sent, r, cost = call(
        opening_kernel, [((PLANE, OWN, WIDTH), BF16), own, own],
        ids, scalars=1, weights=in_hbm(rhs, diag), scratch=[own, own], sems=2,
    )
    near = lax.all_to_all(sent, ("z", "y"), 0, 0, tiled=True).reshape(PLANE * OWN, WIDTH)
    far = other_core(near)
    block = (ROWS, WIDTH, WIDTH)
    triple, wide = (ROWS, 3, WIDTH, WIDTH), (ROWS, WIDTH, 3 * WIDTH)
    normal, tgt, label = call(
        normal_kernel,
        [((ROWS, WIDTH, BANDS * WIDTH), BF16), ((PAD + OWN, WIDTH), jnp.int32), scal],
        ids, couple_idx, pattern[0], scalars=1, weights=in_hbm(couple[0], factor[0]),
        scratch=[(block, BF16), (triple, BF16), (triple, BF16), (wide, BF16)], sems=4,
    )
    sent, us, inv_s = call(
        first_kernel, [msg, scen, scen], ids, near, far, tgt, label, r, cost, normal, scalars=1
    )

    near, far = exchange(sent)
    hot_near, half = call(label_sum, [hots, sums], near, tgt)
    sent, hot_far, us, ps, sc, d, q, x, r = call(
        second_kernel, [msg, hots, scen, scen, scal, own, own, own, own],
        far, tgt, half, us, inv_s, r, cost, normal, scratch=[sums],
    )
    near, far = exchange(sent)
    half = call(near_sum, [sums], near, hot_near)[0]
    sent, sc, d, q, x, r = call(
        third_kernel, [msg, scal, own, own, own, own],
        far, hot_far, half, us, ps, inv_s, sc, d, q, x, r, cost, normal,
    )
    near, far = exchange(sent)
    half = call(near_sum, [sums], near, hot_near)[0]
    return call(last_kernel, [own, own], far, hot_far, half, sc, d, q, x, r, cost)


def solution(mesh):
    fine = Mesh(np.array(mesh.devices).reshape(4, 2, 4, 4), ("x", "core", "z", "y"))
    vec, scen = ("z", "y"), ("x", "core", "z", "y")
    in_specs = (
        P(vec, None),
        P(vec, None),
        P(scen, None, None, None),
        P(scen, None),
        P(scen, None, None, None, None),
        P(scen, None, None),
    )
    out_specs = (P(vec, None), P(vec, None))
    return jax.shard_map(shards, mesh=fine, in_specs=in_specs, out_specs=out_specs, check_vma=False)
```

```python
import jax
import jax.numpy as jnp
import numpy as np
from jax import lax
from jax.experimental import pallas as pl
from jax.experimental.pallas import tpu as pltpu
from jax.sharding import Mesh
from jax.sharding import PartitionSpec as P

ROWS = 24
PAD = 32
OWN = 96
HALF = OWN // 2
WIDTH = 128
CHIPS = 64
PLANE = 16
BANDS = 5
GAMMA, DELTA = 4000, 4001
INVERSE = 2048
F32, BF16 = jnp.float32, jnp.bfloat16


def dot_nn(a, b):
    return lax.dot_general(a, b, (((1,), (0,)), ((), ())), preferred_element_type=F32)


def dot_nt(a, b):
    return lax.dot_general(a, b, (((1,), (1,)), ((), ())), preferred_element_type=F32)


def split(values):
    high = values.astype(BF16).astype(F32)
    return high, values - high


def hot_of(mask):
    return mask.astype(F32).astype(BF16)


def only_row(values, r):
    rows = lax.broadcasted_iota(jnp.int32, (PAD, WIDTH), 0)
    return jnp.where(rows == r, values, 0.0).astype(BF16)


def scenario_lift(y, normal):
    spread = jnp.zeros((PAD, BANDS * WIDTH), F32)
    for r in range(0, ROWS, 2):
        pair = jnp.concatenate([only_row(y, r), only_row(y, r + 1)], axis=1)
        spread += dot_nn(pair, normal[r : r + 2].reshape(2 * WIDTH, BANDS * WIDTH))
    lifted = spread[:, 2 * WIDTH : 3 * WIDTH]
    for band in (0, 1, 3, 4):
        part = spread[:, band * WIDTH : (band + 1) * WIDTH]
        lifted += pltpu.roll(part, (band - 2) % PAD, 0)
    return lifted


def message(lifted, gamma, delta, extra):
    rows = lax.broadcasted_iota(jnp.int32, (PAD, WIDTH), 0)
    out = jnp.where(rows < ROWS, lifted, 0.0)
    for place, line in enumerate(split(gamma) + split(delta) + tuple(extra)):
        out = jnp.where(rows == ROWS + place, jnp.broadcast_to(line, out.shape), out)
    return out.astype(BF16)


def column_sum(values):
    return jnp.sum(values, axis=0, keepdims=True)


def next_message(us, u, r, cost, normal, extra=()):
    lifted = scenario_lift(us, normal)
    gamma = column_sum(r * u) * 0.125
    delta = column_sum(cost * u * u) * 0.125 + column_sum(us * lifted)
    return message(lifted, gamma, delta, extra)


def as_column(row):
    square = (ROWS, ROWS)
    same = lax.broadcasted_iota(jnp.int32, square, 0) == lax.broadcasted_iota(jnp.int32, square, 1)
    found = jnp.where(same, jnp.broadcast_to(row, square), 0).astype(F32)
    return jnp.broadcast_to(jnp.sum(found, axis=1, keepdims=True), (ROWS, WIDTH))


def opening_kernel(
    ids, rhs_hbm, diag_hbm, idx_hbm, pattern_hbm,
    msg_out, r_out, cost_out, scen_tgt, own_tgt, label, side,
    rhs, diag, idx, pattern, sems,
):
    pairs = ((rhs_hbm, rhs), (diag_hbm, diag), (idx_hbm, idx), (pattern_hbm, pattern))
    copies = [pltpu.make_async_copy(a, b, sems.at[i]) for i, (a, b) in enumerate(pairs)]
    for copy in copies:
        copy.start()
    for copy in copies:
        copy.wait()
    r_out[...], cost_out[...] = rhs[...], diag[...]
    mine = pl.ds(pl.multiple_of(ids[0] * HALF, HALF), HALF)
    inverse = 1.0 / diag[mine, :]
    msg_out[0:HALF, :] = (rhs[mine, :] * inverse).astype(BF16)
    msg_out[HALF:OWN, :] = inverse.astype(BF16)

    column = as_column(idx[...]).astype(jnp.int32)
    rows = lax.broadcasted_iota(jnp.int32, (PAD, WIDTH), 0)
    scen_tgt[...] = jnp.where(rows < ROWS + 2, rows - ROWS + GAMMA, -9)
    scen_tgt[0:ROWS, :] = column
    own_tgt[...] = lax.broadcasted_iota(jnp.int32, (OWN, WIDTH), 0) + ids[2] * OWN
    lanes = lax.broadcasted_iota(jnp.int32, (ROWS, WIDTH), 1)
    place = lax.broadcasted_iota(jnp.int32, (ROWS, WIDTH), 0) + PAD * ids[1]
    for line, values in enumerate((column >> 6, column & 63)):
        label[line : line + 1, :] = column_sum(jnp.where(lanes == place, values, 0).astype(F32))
    for k in range(2):
        side[k] = as_column(pattern[k : k + 1, :])


def copy_parts(source, target, sems, first, parts):
    step = source.shape[0] // parts
    copies = []
    for part in range(parts):
        rows = pl.ds(part * step, step)
        copies.append(
            pltpu.make_async_copy(source.at[rows], target.at[rows], sems.at[first + part])
        )
    return copies


def normal_kernel(
    side, couple_hbm, factor_hbm, normal_hbm, couple, factor, prod, flip, normal, sems
):
    couples = copy_parts(couple_hbm, couple, sems, 0, 3)
    factors = copy_parts(factor_hbm, factor, sems, 3, 6)
    outs = copy_parts(normal, normal_hbm, sems, 9, 6)
    for part in range(3):
        for copy in (couples[part], factors[2 * part], factors[2 * part + 1]):
            copy.start()
    zeros = jnp.zeros((WIDTH, WIDTH), BF16)

    def product_row(r):
        for k in range(3):
            c = r + k - 1
            if not 0 <= c < ROWS:
                continue
            block = dot_nn(factor[r, k], couple[c])
            if k != 1:
                block = block * side[k // 2, r : r + 1, :]
            block = block.astype(BF16)
            prod[r, k] = block
            flip[c, :, (2 - k) * WIDTH : (3 - k) * WIDTH] = block.T

    def normal_row(d):
        for band in range(BANDS):
            c = d + band - 2
            if not 0 <= c < ROWS:
                normal[d, :, band * WIDTH : (band + 1) * WIDTH] = zeros
                continue
            if band < 2:
                continue
            terms = [r for r in (d - 1, d, d + 1) if 0 <= r < ROWS and abs(r - c) <= 1]
            first = terms[0] - d + 1
            left = flip[d, :, first * WIDTH : (first + len(terms)) * WIDTH]
            right = jnp.concatenate([prod[r, c - r + 1] for r in terms], axis=0)
            block = dot_nn(left, right).astype(BF16)
            normal[d, :, band * WIDTH : (band + 1) * WIDTH] = block
            if c != d:
                normal[c, :, (4 - band) * WIDTH : (5 - band) * WIDTH] = block.T

    for copy in couples[:2] + factors[:2]:
        copy.wait()
    for r in range(8):
        product_row(r)
    for copy in couples[2:] + factors[2:4]:
        copy.wait()
    for r in range(8, 16):
        product_row(r)
    for d in range(7):
        normal_row(d)
    outs[0].start()
    for copy in factors[4:]:
        copy.wait()
    for r in range(16, 24):
        product_row(r)
    for d in range(7, 12):
        normal_row(d)
    outs[1].start()
    outs[2].start()
    for d in range(12, 18):
        normal_row(d)
    outs[3].start()
    for d in range(18, 24):
        normal_row(d)
    outs[4].start()
    outs[5].start()
    for copy in outs:
        copy.wait()


def load_kernel(normal_hbm, normal, sems):
    copies = copy_parts(normal_hbm, normal, sems, 0, 6)
    for copy in copies:
        copy.start()
    for copy in copies:
        copy.wait()


def first_kernel(ids, near, far, scen_tgt, label, own, cost, normal, msg_out, us_out, inv_out):
    want = scen_tgt[:, 0:1]
    want = jnp.concatenate([want, want + INVERSE], axis=0)
    found = jnp.zeros((2 * PAD, WIDTH), F32)
    for part, which in ((near, ids[0]), (far, 1 - ids[0])):
        place = lax.broadcasted_iota(jnp.int32, (1, PLANE * OWN), 1)
        member = place - OWN * ((place * 683) >> 16)
        block = place + HALF * which + jnp.where(member < HALF, 0, INVERSE - HALF)
        found += dot_nn(hot_of(want == block), part[...])
    us = found[0:PAD, :]
    us_out[...], inv_out[...] = us, found[PAD:, :]
    r, d = own[...], cost[...]
    msg_out[...] = next_message(us, r * (1.0 / d), r, d, normal, (label[0:1, :], label[1:2, :]))


def give_and_keep(found, keep, give):
    keep[...] = found[0 : PAD + OWN, :]
    give[0:PAD, :] = found[PAD + OWN :, :]
    give[PAD:, :] = found[PAD : PAD + OWN, :]


def label_sum(part, scen_tgt, own_tgt, other_tgt, hot, keep, give):
    want = jnp.concatenate([scen_tgt[...], own_tgt[...], other_tgt[...]], axis=0)
    lane = lax.broadcasted_iota(jnp.int32, (1, WIDTH), 1)
    slot = lane & (PAD - 1)
    fixed = jnp.where(slot < ROWS + 2, GAMMA, jnp.where(slot < ROWS + 4, DELTA, -1))
    for chunk in range(CHIPS // 4):
        start = WIDTH * chunk
        ends = [part[start + PAD * m + 16 : start + PAD * (m + 1), :].astype(F32) for m in range(4)]
        ends = ends[0] + ends[1] + ends[2] + ends[3]
        found = (ends[12:13, :] * 64.0 + ends[13:14, :]).astype(jnp.int32)
        block = jnp.where(slot < ROWS, found, fixed)
        hot[:, start : start + WIDTH] = hot_of(want == block)
    give_and_keep(dot_nn(hot[...], part[...]), keep, give)


def message_sum(part, hot, keep, give):
    give_and_keep(dot_nn(hot[...], part[...]), keep, give)


def advance(total, us, inv_s, ps, u, cost, q, d, x, r, gamma_old, alpha_old):
    gamma = jnp.sum(total[ROWS : ROWS + 1, :], axis=1, keepdims=True)
    delta = jnp.sum(total[ROWS + 1 : ROWS + 2, :], axis=1, keepdims=True)
    if gamma_old is None:
        alpha = gamma / delta
    else:
        beta = gamma / gamma_old
        alpha = gamma / (delta - beta * gamma / alpha_old)
    s = cost * u + total[PAD:, :]
    if gamma_old is None:
        d, q = u, s
    else:
        d, q = u + beta * d, s + beta * q
    x = alpha * d if x is None else x + alpha * d
    r = r - alpha * q
    if us is not None:
        rows = lax.broadcasted_iota(jnp.int32, (PAD, WIDTH), 0)
        own = jnp.where(rows < ROWS, us + inv_s * total[0:PAD, :], 0.0)
        ps = own if ps is None else own + beta * ps
        us = us - alpha * ps
    return gamma, alpha, us, ps, d, q, x, r


def second_kernel(
    keep, got, us, inv_s, own, cost, normal,
    msg_out, us_out, ps_out, scal_out, d_out, q_out, x_out, r_out,
):
    total = keep[...] + got[...]
    d = cost[...]
    inv = 1.0 / d
    r = own[...]
    gamma, alpha, u_s, p_s, dn, qn, xn, rn = advance(
        total, us[...], inv_s[...], None, inv * r, d, None, None, None, r, None, None
    )
    us_out[...], ps_out[...] = u_s, p_s
    d_out[...], q_out[...], x_out[...], r_out[...] = dn, qn, xn, rn
    scal_out[0:1, :] = jnp.broadcast_to(gamma, (1, WIDTH))
    scal_out[1:2, :] = jnp.broadcast_to(alpha, (1, WIDTH))
    msg_out[...] = next_message(u_s, inv * rn, rn, d, normal)


def third_kernel(
    keep, got, us, ps, inv_s, scal, d, q, x, r, cost, normal,
    msg_out, scal_out, d_out, q_out, x_out, r_out,
):
    total = keep[...] + got[...]
    c = cost[...]
    inv = 1.0 / c
    gamma, alpha, u_s, p_s, dn, qn, xn, rn = advance(
        total, us[...], inv_s[...], ps[...], inv * r[...], c, q[...], d[...], x[...], r[...],
        scal[0:1, 0:1], scal[1:2, 0:1],
    )
    d_out[...], q_out[...], x_out[...], r_out[...] = dn, qn, xn, rn
    scal_out[0:1, :] = jnp.broadcast_to(gamma, (1, WIDTH))
    scal_out[1:2, :] = jnp.broadcast_to(alpha, (1, WIDTH))
    msg_out[...] = next_message(u_s, inv * rn, rn, c, normal)


def last_kernel(keep, got, scal, d, q, x, r, cost, x_out, r_out):
    total = keep[...] + got[...]
    c = cost[...]
    found = advance(
        total, None, None, None, r[...] / c, c, q[...], d[...], x[...], r[...],
        scal[0:1, 0:1], scal[1:2, 0:1],
    )
    x_out[...], r_out[...] = found[6], found[7]


def call(kernel, shapes, *args, scalars=0, weights=(), scratch=(), sems=0, hbm_out=False):
    vmem = pl.BlockSpec(memory_space=pltpu.VMEM)
    specs = [pl.BlockSpec(memory_space=pltpu.SMEM)] * scalars + [vmem] * (len(args) - scalars)
    specs += [pl.BlockSpec(memory_space=pltpu.HBM)] * len(weights)
    scratch = [pltpu.VMEM(s, t) for s, t in scratch]
    if sems:
        scratch.append(pltpu.SemaphoreType.DMA((sems,)))
    return pl.pallas_call(
        kernel,
        out_shape=[(pltpu.HBM if hbm_out else jax.ShapeDtypeStruct)(s, t) for s, t in shapes],
        in_specs=specs,
        out_specs=[pl.BlockSpec(memory_space=pltpu.HBM) if hbm_out else vmem] * len(shapes),
        scratch_shapes=scratch,
        compiler_params=pltpu.CompilerParams(vmem_limit_bytes=32 * 1024 * 1024),
    )(*args, *weights)


def in_hbm(*arrays):
    return [pltpu.with_memory_space_constraint(a, pltpu.HBM) for a in arrays]


def other_core(values):
    return lax.ppermute(values, "core", [(0, 1), (1, 0)])


def to_all(sent, axes, count):
    copies = jnp.broadcast_to(sent[None], (count,) + sent.shape)
    return lax.all_to_all(copies, axes, 0, 0, tiled=True).reshape(-1, WIDTH)


def shards(rhs, diag, couple, couple_idx, factor, pattern):
    scen, own, msg = ((PAD, WIDTH), F32), ((OWN, WIDTH), F32), ((PAD, WIDTH), BF16)
    scal, sums = ((2, WIDTH), F32), ((PAD + OWN, WIDTH), F32)
    hots = ((PAD + OWN + PAD, CHIPS * PAD), BF16)
    vec = lax.axis_index("z") * 4 + lax.axis_index("y")
    ids = jnp.stack([lax.axis_index("core"), lax.axis_index("y"), vec]).astype(jnp.int32)
    sent, r, cost, scen_tgt, own_tgt, label, side = call(
        opening_kernel,
        [
            ((OWN, WIDTH), BF16), own, own, ((PAD, WIDTH), jnp.int32), ((OWN, WIDTH), jnp.int32),
            scal, ((2, ROWS, WIDTH), F32),
        ],
        ids, scalars=1, weights=in_hbm(rhs, diag, couple_idx, pattern[0].T),
        scratch=[own, own, ((1, ROWS), jnp.int32), ((2, ROWS), jnp.int32)], sems=4,
    )
    near = to_all(sent, ("z", "y"), PLANE)
    other_tgt = other_core(scen_tgt)
    triple, wide = (ROWS, 3, WIDTH, WIDTH), (ROWS, WIDTH, 3 * WIDTH)
    bands = ((ROWS, WIDTH, BANDS * WIDTH), BF16)
    normal = call(
        normal_kernel, [bands], side, weights=in_hbm(couple[0], factor[0]), hbm_out=True,
        scratch=[((ROWS, WIDTH, WIDTH), BF16), (triple, BF16), (triple, BF16), (wide, BF16), bands],
        sems=15,
    )[0]
    near, normal, other_tgt = lax.optimization_barrier((near, normal, other_tgt))
    far = other_core(near)
    normal = call(load_kernel, [bands], weights=in_hbm(normal), sems=6)[0]
    sent, us, inv_s = call(
        first_kernel, [msg, scen, scen], ids, near, far, scen_tgt, label, r, cost, normal, scalars=1
    )

    near = to_all(sent, ("x", "z", "y"), CHIPS)
    hot, keep, give = call(label_sum, [hots, sums, sums], near, scen_tgt, own_tgt, other_tgt)
    sent, us, ps, sc, d, q, x, r = call(
        second_kernel, [msg, scen, scen, scal, own, own, own, own],
        keep, other_core(give), us, inv_s, r, cost, normal,
    )
    near = to_all(sent, ("x", "z", "y"), CHIPS)
    keep, give = call(message_sum, [sums, sums], near, hot)
    sent, sc, d, q, x, r = call(
        third_kernel, [msg, scal, own, own, own, own],
        keep, other_core(give), us, ps, inv_s, sc, d, q, x, r, cost, normal,
    )
    near = to_all(sent, ("x", "z", "y"), CHIPS)
    keep, give = call(message_sum, [sums, sums], near, hot)
    return call(last_kernel, [own, own], keep, other_core(give), sc, d, q, x, r, cost)


def solution(mesh):
    fine = Mesh(np.array(mesh.devices).reshape(4, 2, 4, 4), ("x", "core", "z", "y"))
    vec, scen = ("z", "y"), ("x", "core", "z", "y")
    in_specs = (
        P(vec, None),
        P(vec, None),
        P(scen, None, None, None),
        P(scen, None),
        P(scen, None, None, None, None),
        P(scen, None, None),
    )
    out_specs = (P(vec, None), P(vec, None))
    return jax.shard_map(shards, mesh=fine, in_specs=in_specs, out_specs=out_specs, check_vma=False)
```

```python
import jax
import jax.numpy as jnp
import numpy as np
from jax import lax
from jax.experimental import pallas as pl
from jax.experimental.pallas import tpu as pltpu
from jax.sharding import Mesh
from jax.sharding import PartitionSpec as P

ROWS = 24
PAD = 32
SENT = 26
OWN = 96
HALF = OWN // 2
WIDTH = 128
CHIPS = 64
PLANE = 16
BANDS = 5
GAMMA, DELTA = 4000, 4001
F32, BF16 = jnp.float32, jnp.bfloat16


def dot_nn(a, b):
    return lax.dot_general(a, b, (((1,), (0,)), ((), ())), preferred_element_type=F32)


def dot_nt(a, b):
    return lax.dot_general(a, b, (((1,), (1,)), ((), ())), preferred_element_type=F32)


def split(values):
    high = values.astype(BF16).astype(F32)
    return high, values - high


def hot_of(mask):
    return mask.astype(F32).astype(BF16)


def only_row(values, r):
    rows = lax.broadcasted_iota(jnp.int32, (PAD, WIDTH), 0)
    return jnp.where(rows == r, values, 0.0).astype(BF16)


def scenario_lift(y, normal):
    spread = jnp.zeros((PAD, BANDS * WIDTH), F32)
    for r in range(0, ROWS, 2):
        pair = jnp.concatenate([only_row(y, r), only_row(y, r + 1)], axis=1)
        spread += dot_nn(pair, normal[r : r + 2].reshape(2 * WIDTH, BANDS * WIDTH))
    lifted = spread[:, 2 * WIDTH : 3 * WIDTH]
    for band in (0, 1, 3, 4):
        part = spread[:, band * WIDTH : (band + 1) * WIDTH]
        lifted += pltpu.roll(part, (band - 2) % PAD, 0)
    return lifted


def write_message(msg_out, lifted, lines):
    rows = lax.broadcasted_iota(jnp.int32, (PAD, WIDTH), 0)
    out = lifted
    for place, line in enumerate(lines):
        out = jnp.where(rows == ROWS + place, jnp.broadcast_to(line, out.shape), out)
    for pair in range(SENT // 2):
        msg_out[pair] = out[2 * pair : 2 * pair + 2, :].astype(BF16)


def column_sum(values):
    return jnp.sum(values, axis=0, keepdims=True)


def products(us, lifted, ru, cuu):
    return column_sum(ru) * 0.125, column_sum(cuu) * 0.125 + column_sum(us * lifted)


def folded(values):
    lane = lax.broadcasted_iota(jnp.int32, (1, WIDTH), 1)
    high, low = split(values + pltpu.roll(values, WIDTH // 2, 1))
    return jnp.where(lane < WIDTH // 2, high, low)


def next_message(msg_out, us, u, r, cost, normal):
    lifted = scenario_lift(us, normal)
    write_message(msg_out, lifted, [folded(v) for v in products(us, lifted, r * u, cost * u * u)])


def as_column(row):
    square = (ROWS, ROWS)
    same = lax.broadcasted_iota(jnp.int32, square, 0) == lax.broadcasted_iota(jnp.int32, square, 1)
    found = jnp.where(same, jnp.broadcast_to(row, square), 0).astype(F32)
    return jnp.broadcast_to(jnp.sum(found, axis=1, keepdims=True), (ROWS, WIDTH))


def scenario_targets(idx):
    rows = lax.broadcasted_iota(jnp.int32, (PAD - ROWS, WIDTH), 0)
    rest = jnp.where(rows < 2, rows + GAMMA, -9)
    return jnp.concatenate([as_column(idx).astype(jnp.int32), rest], axis=0)


def opening_kernel(ids, rhs_hbm, diag_hbm, msg_hbm, rhs, diag, msg, sems):
    copies = (
        pltpu.make_async_copy(rhs_hbm, rhs, sems.at[0]),
        pltpu.make_async_copy(diag_hbm, diag, sems.at[1]),
    )
    for copy in copies:
        copy.start()
    for copy in copies:
        copy.wait()
    mine = pl.ds(pl.multiple_of(ids[0] * HALF, HALF), HALF)
    inverse = 1.0 / diag[mine, :]
    msg[:, 0:WIDTH] = (rhs[mine, :] * inverse).astype(BF16)
    msg[:, WIDTH:] = inverse.astype(BF16)
    copies = [
        pltpu.make_async_copy(msg, msg_hbm.at[place], sems.at[2 + place]) for place in range(PLANE)
    ]
    for copy in copies:
        copy.start()
    for copy in copies:
        copy.wait()


def copy_parts(source, target, sems, first, parts):
    step = source.shape[0] // parts
    copies = []
    for part in range(parts):
        rows = pl.ds(part * step, step)
        copies.append(
            pltpu.make_async_copy(source.at[rows], target.at[rows], sems.at[first + part])
        )
    return copies


def normal_kernel(
    pattern_hbm, couple_hbm, factor_hbm, normal_hbm,
    pattern, couple, factor, prod, flip, normal, sems,
):
    couples = copy_parts(couple_hbm, couple, sems, 0, 3)
    factors = copy_parts(factor_hbm, factor, sems, 3, 6)
    outs = copy_parts(normal, normal_hbm, sems, 9, 6)
    for part in range(3):
        for copy in (couples[part], factors[2 * part], factors[2 * part + 1]):
            copy.start()
    copy = pltpu.make_async_copy(pattern_hbm, pattern, sems.at[15])
    copy.start()
    copy.wait()
    side = [as_column(pattern[k : k + 1, :]) for k in range(2)]
    zeros = jnp.zeros((WIDTH, WIDTH), BF16)

    def product_row(r):
        for k in range(3):
            c = r + k - 1
            if not 0 <= c < ROWS:
                continue
            block = dot_nn(factor[r, k], couple[c])
            if k != 1:
                block = block * side[k // 2][r : r + 1, :]
            block = block.astype(BF16)
            prod[r, k] = block
            flip[c, :, (2 - k) * WIDTH : (3 - k) * WIDTH] = block.T

    def normal_row(d):
        for band in range(BANDS):
            c = d + band - 2
            if not 0 <= c < ROWS:
                normal[d, :, band * WIDTH : (band + 1) * WIDTH] = zeros
                continue
            if band < 2:
                continue
            terms = [r for r in (d - 1, d, d + 1) if 0 <= r < ROWS and abs(r - c) <= 1]
            first = terms[0] - d + 1
            left = flip[d, :, first * WIDTH : (first + len(terms)) * WIDTH]
            right = jnp.concatenate([prod[r, c - r + 1] for r in terms], axis=0)
            block = dot_nn(left, right).astype(BF16)
            normal[d, :, band * WIDTH : (band + 1) * WIDTH] = block
            if c != d:
                normal[c, :, (4 - band) * WIDTH : (5 - band) * WIDTH] = block.T

    for copy in couples[:2] + factors[:2]:
        copy.wait()
    for r in range(8):
        product_row(r)
    for copy in couples[2:] + factors[2:4]:
        copy.wait()
    for r in range(8, 16):
        product_row(r)
    for d in range(7):
        normal_row(d)
    outs[0].start()
    for copy in factors[4:]:
        copy.wait()
    for r in range(16, 24):
        product_row(r)
    for d in range(7, 12):
        normal_row(d)
    outs[1].start()
    outs[2].start()
    for d in range(12, 18):
        normal_row(d)
    outs[3].start()
    for d in range(18, 24):
        normal_row(d)
    outs[4].start()
    outs[5].start()
    for copy in outs:
        copy.wait()


def load_kernel(normal_hbm, rhs_hbm, diag_hbm, idx_hbm, normal, rhs, diag, idx, sems):
    copies = copy_parts(normal_hbm, normal, sems, 0, 6)
    for place, pair in enumerate(((rhs_hbm, rhs), (diag_hbm, diag), (idx_hbm, idx))):
        copies.append(pltpu.make_async_copy(*pair, sems.at[6 + place]))
    for copy in copies:
        copy.start()
    for copy in copies:
        copy.wait()


def first_kernel(ids, near, far, idx, own, cost, normal, msg_out, us_out, inv_out):
    want = scenario_targets(idx[...])
    found = jnp.zeros((PAD, 2 * WIDTH), F32)
    for part, which in ((near, ids[0]), (far, 1 - ids[0])):
        place = lax.broadcasted_iota(jnp.int32, (1, PLANE * HALF), 1)
        block = place + HALF * ((place * 1366) >> 16) + HALF * which
        found += dot_nn(hot_of(want[:, 0:1] == block), part[...])
    us = found[:, 0:WIDTH]
    us_out[...], inv_out[...] = us, found[:, WIDTH:]
    lifted = scenario_lift(us, normal)
    r = own[...]
    ru = r * (r * (1.0 / cost[...]))
    lane = lax.broadcasted_iota(jnp.int32, (1, WIDTH), 1)
    turned = (lane - SENT * ids[1]) & (WIDTH - 1)
    parts = []
    for line in products(us, lifted, ru, ru):
        high, low = split(jnp.sum(line, axis=1, keepdims=True))
        parts.append(jnp.where(turned == ROWS, high, jnp.where(turned == ROWS + 1, low, 0.0)))
    rows = lax.broadcasted_iota(jnp.int32, (ROWS, WIDTH), 0)
    column = want[0:ROWS, :]
    for line, values in enumerate((column >> 8, column & 255)):
        parts[line] += column_sum(jnp.where(rows == turned, values, 0).astype(F32))
    write_message(msg_out, lifted, parts)


def give_and_keep(found, keep, give):
    keep[...] = found[0 : PAD + OWN, :]
    give[0:PAD, :] = found[PAD + OWN :, :]
    give[PAD:, :] = found[PAD : PAD + OWN, :]


def label_sum(ids, part, idx, other_idx, hot, keep, give):
    own = lax.broadcasted_iota(jnp.int32, (OWN, WIDTH), 0) + ids[2] * OWN
    want = [scenario_targets(idx[...]), own, scenario_targets(other_idx[...])]
    want = jnp.concatenate(want, axis=0)
    row = lax.broadcasted_iota(jnp.int32, (2 * CHIPS, CHIPS * SENT), 0)
    place = lax.broadcasted_iota(jnp.int32, (2 * CHIPS, CHIPS * SENT), 1)
    line = SENT * (row & (CHIPS - 1)) + ROWS + jnp.where(row < CHIPS, 0, 1)
    ends = dot_nn(hot_of(place == line), part[...])
    first, second = ends[0:CHIPS, :], ends[CHIPS:, :]
    message = lax.broadcasted_iota(jnp.int32, (CHIPS, WIDTH), 0) * SENT
    lane = lax.broadcasted_iota(jnp.int32, (CHIPS, WIDTH), 1)
    turned = (lane - message) & (WIDTH - 1)
    inner = [
        column_sum(jnp.where((turned >= ROWS) & (turned < SENT), e, 0.0)) for e in (first, second)
    ]
    labels = jnp.where(turned < ROWS, first * 256.0 + second, 0.0)
    at_chunk = (message + turned) >> 7
    for chunk in range(CHIPS * SENT // WIDTH):
        start = WIDTH * chunk
        found = column_sum(jnp.where(at_chunk == chunk, labels, 0.0)).astype(jnp.int32)
        place = lax.broadcasted_iota(jnp.int32, (1, WIDTH), 1) + start
        slot = place - SENT * ((place * 2521) >> 16)
        block = jnp.where(slot < ROWS, found, slot - ROWS + GAMMA)
        hot[:, start : start + WIDTH] = hot_of(want == block)
    give_and_keep(dot_nn(hot[...], part[...]), keep, give)
    for ref in (keep, give):
        for k in range(2):
            ref[ROWS + k : ROWS + k + 1, :] = inner[k]


def message_sum(part, hot, keep, give):
    give_and_keep(dot_nn(hot[...], part[...]), keep, give)


def advance(total, us, inv_s, ps, u, cost, q, d, x, r, gamma_old, alpha_old):
    gamma = jnp.sum(total[ROWS : ROWS + 1, :], axis=1, keepdims=True)
    delta = jnp.sum(total[ROWS + 1 : ROWS + 2, :], axis=1, keepdims=True)
    if gamma_old is None:
        alpha = gamma / delta
    else:
        beta = gamma / gamma_old
        alpha = gamma / (delta - beta * gamma / alpha_old)
    s = cost * u + total[PAD:, :]
    if gamma_old is None:
        d, q = u, s
    else:
        d, q = u + beta * d, s + beta * q
    x = alpha * d if x is None else x + alpha * d
    r = r - alpha * q
    if us is not None:
        rows = lax.broadcasted_iota(jnp.int32, (PAD, WIDTH), 0)
        own = jnp.where(rows < ROWS, us + inv_s * total[0:PAD, :], 0.0)
        ps = own if ps is None else own + beta * ps
        us = us - alpha * ps
    return gamma, alpha, us, ps, d, q, x, r


def second_kernel(
    keep, got, us, inv_s, own, cost, normal,
    msg_out, us_out, ps_out, scal_out, d_out, q_out, x_out, r_out,
):
    total = keep[...] + got[...]
    d = cost[...]
    inv = 1.0 / d
    r = own[...]
    gamma, alpha, u_s, p_s, dn, qn, xn, rn = advance(
        total, us[...], inv_s[...], None, inv * r, d, None, None, None, r, None, None
    )
    us_out[...], ps_out[...] = u_s, p_s
    d_out[...], q_out[...], x_out[...], r_out[...] = dn, qn, xn, rn
    scal_out[0:1, :] = jnp.broadcast_to(gamma, (1, WIDTH))
    scal_out[1:2, :] = jnp.broadcast_to(alpha, (1, WIDTH))
    next_message(msg_out, u_s, inv * rn, rn, d, normal)


def third_kernel(
    keep, got, us, ps, inv_s, scal, d, q, x, r, cost, normal,
    msg_out, scal_out, d_out, q_out, x_out, r_out,
):
    total = keep[...] + got[...]
    c = cost[...]
    inv = 1.0 / c
    gamma, alpha, u_s, p_s, dn, qn, xn, rn = advance(
        total, us[...], inv_s[...], ps[...], inv * r[...], c, q[...], d[...], x[...], r[...],
        scal[0:1, 0:1], scal[1:2, 0:1],
    )
    d_out[...], q_out[...], x_out[...], r_out[...] = dn, qn, xn, rn
    scal_out[0:1, :] = jnp.broadcast_to(gamma, (1, WIDTH))
    scal_out[1:2, :] = jnp.broadcast_to(alpha, (1, WIDTH))
    next_message(msg_out, u_s, inv * rn, rn, c, normal)


def last_kernel(keep, got, scal, d, q, x, r, cost, x_out, r_out):
    total = keep[...] + got[...]
    c = cost[...]
    found = advance(
        total, None, None, None, r[...] / c, c, q[...], d[...], x[...], r[...],
        scal[0:1, 0:1], scal[1:2, 0:1],
    )
    x_out[...], r_out[...] = found[6], found[7]


def call(kernel, shapes, *args, scalars=0, weights=(), scratch=(), sems=0, hbm_out=False):
    vmem = pl.BlockSpec(memory_space=pltpu.VMEM)
    specs = [pl.BlockSpec(memory_space=pltpu.SMEM)] * scalars + [vmem] * (len(args) - scalars)
    specs += [pl.BlockSpec(memory_space=pltpu.HBM)] * len(weights)
    scratch = [pltpu.VMEM(s, t) for s, t in scratch]
    if sems:
        scratch.append(pltpu.SemaphoreType.DMA((sems,)))
    return pl.pallas_call(
        kernel,
        out_shape=[(pltpu.HBM if hbm_out else jax.ShapeDtypeStruct)(s, t) for s, t in shapes],
        in_specs=specs,
        out_specs=[pl.BlockSpec(memory_space=pltpu.HBM) if hbm_out else vmem] * len(shapes),
        scratch_shapes=scratch,
        compiler_params=pltpu.CompilerParams(vmem_limit_bytes=32 * 1024 * 1024),
    )(*args, *weights)


def in_hbm(*arrays):
    return [pltpu.with_memory_space_constraint(a, pltpu.HBM) for a in arrays]


def other_core(values):
    return lax.ppermute(values, "core", [(0, 1), (1, 0)])


def to_all(sent):
    copies = jnp.broadcast_to(sent[None], (CHIPS,) + sent.shape)
    near = lax.all_to_all(copies, ("x", "z", "y"), 0, 0, tiled=True)
    return near.reshape(CHIPS * SENT, WIDTH)


def shards(rhs, diag, couple, couple_idx, factor, pattern):
    scen, own, msg = ((PAD, WIDTH), F32), ((OWN, WIDTH), F32), ((SENT // 2, 2, WIDTH), BF16)
    scal, sums = ((2, WIDTH), F32), ((PAD + OWN, WIDTH), F32)
    hots = ((PAD + OWN + PAD, CHIPS * SENT), BF16)
    index = ((1, ROWS), jnp.int32)
    vec = lax.axis_index("z") * 4 + lax.axis_index("y")
    ids = [lax.axis_index("core"), lax.axis_index("x") * PLANE + vec, vec]
    ids = jnp.stack(ids).astype(jnp.int32)
    sent = call(
        opening_kernel, [((PLANE, HALF, 2 * WIDTH), BF16)], ids, scalars=1, hbm_out=True,
        weights=in_hbm(rhs, diag), scratch=[own, own, ((HALF, 2 * WIDTH), BF16)], sems=2 + PLANE,
    )[0]
    near = lax.all_to_all(sent, ("z", "y"), 0, 0, tiled=True).reshape(PLANE * HALF, 2 * WIDTH)
    other_idx = other_core(couple_idx)
    triple, wide = (ROWS, 3, WIDTH, WIDTH), (ROWS, WIDTH, 3 * WIDTH)
    bands = ((ROWS, WIDTH, BANDS * WIDTH), BF16)
    normal = call(
        normal_kernel, [bands], hbm_out=True, sems=16,
        weights=in_hbm(pattern[0].T, couple[0], factor[0]),
        scratch=[
            ((2, ROWS), jnp.int32), ((ROWS, WIDTH, WIDTH), BF16), (triple, BF16),
            (triple, BF16), (wide, BF16), bands,
        ],
    )[0]
    near, normal, other_idx = lax.optimization_barrier((near, normal, other_idx))
    far = other_core(near)
    normal, r, cost, idx = call(
        load_kernel, [bands, own, own, index], sems=9,
        weights=in_hbm(normal, rhs, diag, couple_idx),
    )
    sent, us, inv_s = call(
        first_kernel, [msg, scen, scen], ids, near, far, idx, r, cost, normal, scalars=1
    )

    near = to_all(sent)
    hot, keep, give = call(
        label_sum, [hots, sums, sums], ids, near, idx, other_idx, scalars=1
    )
    sent, us, ps, sc, d, q, x, r = call(
        second_kernel, [msg, scen, scen, scal, own, own, own, own],
        keep, other_core(give), us, inv_s, r, cost, normal,
    )
    near = to_all(sent)
    keep, give = call(message_sum, [sums, sums], near, hot)
    sent, sc, d, q, x, r = call(
        third_kernel, [msg, scal, own, own, own, own],
        keep, other_core(give), us, ps, inv_s, sc, d, q, x, r, cost, normal,
    )
    near = to_all(sent)
    keep, give = call(message_sum, [sums, sums], near, hot)
    return call(last_kernel, [own, own], keep, other_core(give), sc, d, q, x, r, cost)


def solution(mesh):
    fine = Mesh(np.array(mesh.devices).reshape(4, 2, 4, 4), ("x", "core", "z", "y"))
    vec, scen = ("z", "y"), ("x", "core", "z", "y")
    in_specs = (
        P(vec, None),
        P(vec, None),
        P(scen, None, None, None),
        P(scen, None),
        P(scen, None, None, None, None),
        P(scen, None, None),
    )
    out_specs = (P(vec, None), P(vec, None))
    return jax.shard_map(shards, mesh=fine, in_specs=in_specs, out_specs=out_specs, check_vma=False)
```

```python
import jax
import jax.numpy as jnp
import numpy as np
from jax import lax
from jax.experimental import pallas as pl
from jax.experimental.pallas import tpu as pltpu
from jax.sharding import Mesh
from jax.sharding import PartitionSpec as P

ROWS = 24
PAD = 32
SENT = 26
OWN = 96
HALF = OWN // 2
WIDTH = 128
CHIPS = 64
PLANE = 16
BANDS = 5
COPIES = 8
GAMMA, DELTA = 4000, 4001
F32, BF16 = jnp.float32, jnp.bfloat16


def dot_nn(a, b):
    return lax.dot_general(a, b, (((1,), (0,)), ((), ())), preferred_element_type=F32)


def dot_nt(a, b):
    return lax.dot_general(a, b, (((1,), (1,)), ((), ())), preferred_element_type=F32)


def split(values):
    high = values.astype(BF16).astype(F32)
    return high, values - high


def hot_of(mask):
    return mask.astype(F32).astype(BF16)


def only_row(values, r):
    rows = lax.broadcasted_iota(jnp.int32, (PAD, WIDTH), 0)
    return jnp.where(rows == r, values, 0.0).astype(BF16)


def scenario_lift(y, normal):
    spread = jnp.zeros((PAD, BANDS * WIDTH), F32)
    for r in range(0, ROWS, 2):
        pair = jnp.concatenate([only_row(y, r), only_row(y, r + 1)], axis=1)
        spread += dot_nn(pair, normal[r : r + 2].reshape(2 * WIDTH, BANDS * WIDTH))
    lifted = spread[:, 2 * WIDTH : 3 * WIDTH]
    for band in (0, 1, 3, 4):
        part = spread[:, band * WIDTH : (band + 1) * WIDTH]
        lifted += pltpu.roll(part, (band - 2) % PAD, 0)
    return lifted


def write_message(msg_out, lifted, lines):
    rows = lax.broadcasted_iota(jnp.int32, (PAD, WIDTH), 0)
    out = lifted
    for place, line in enumerate(lines):
        out = jnp.where(rows == ROWS + place, jnp.broadcast_to(line, out.shape), out)
    row = lax.broadcasted_iota(jnp.int32, (COPIES * SENT, PAD), 0)
    column = lax.broadcasted_iota(jnp.int32, (COPIES * SENT, PAD), 1)
    again = hot_of(row - SENT * ((row * 2521) >> 16) == column)
    block = dot_nn(again, out.astype(BF16)).astype(BF16)
    for start in range(0, CHIPS * SENT, COPIES * SENT):
        msg_out[start : start + COPIES * SENT, :] = block


def column_sum(values):
    return jnp.sum(values, axis=0, keepdims=True)


def products(us, lifted, ru, cuu):
    return column_sum(ru) * 0.125, column_sum(cuu) * 0.125 + column_sum(us * lifted)


def folded(values):
    lane = lax.broadcasted_iota(jnp.int32, (1, WIDTH), 1)
    high, low = split(values + pltpu.roll(values, WIDTH // 2, 1))
    return jnp.where(lane < WIDTH // 2, high, low)


def next_message(msg_out, us, u, r, cost, normal):
    lifted = scenario_lift(us, normal)
    write_message(msg_out, lifted, [folded(v) for v in products(us, lifted, r * u, cost * u * u)])


def as_column(row):
    square = (ROWS, ROWS)
    same = lax.broadcasted_iota(jnp.int32, square, 0) == lax.broadcasted_iota(jnp.int32, square, 1)
    found = jnp.where(same, jnp.broadcast_to(row, square), 0).astype(F32)
    return jnp.broadcast_to(jnp.sum(found, axis=1, keepdims=True), (ROWS, WIDTH))


def scenario_targets(idx):
    rows = lax.broadcasted_iota(jnp.int32, (PAD - ROWS, WIDTH), 0)
    rest = jnp.where(rows < 2, rows + GAMMA, -9)
    return jnp.concatenate([as_column(idx).astype(jnp.int32), rest], axis=0)


def here():
    vec = lax.axis_index("z") * 4 + lax.axis_index("y")
    return lax.axis_index("core"), lax.axis_index("x") * PLANE + vec, vec


def opening_kernel(rhs_hbm, diag_hbm, msg_hbm, rhs, diag, msg, sems):
    copies = (
        pltpu.make_async_copy(rhs_hbm, rhs, sems.at[0]),
        pltpu.make_async_copy(diag_hbm, diag, sems.at[1]),
    )
    for copy in copies:
        copy.start()
    for copy in copies:
        copy.wait()
    mine = pl.ds(pl.multiple_of(here()[0] * HALF, HALF), HALF)
    inverse = 1.0 / diag[mine, :]
    msg[:, 0:WIDTH] = (rhs[mine, :] * inverse).astype(BF16)
    msg[:, WIDTH:] = inverse.astype(BF16)
    copies = [
        pltpu.make_async_copy(msg, msg_hbm.at[place], sems.at[2 + place]) for place in range(PLANE)
    ]
    for copy in copies:
        copy.start()
    for copy in copies:
        copy.wait()


def copy_parts(source, target, sems, first, parts):
    step = source.shape[0] // parts
    copies = []
    for part in range(parts):
        rows = pl.ds(part * step, step)
        copies.append(
            pltpu.make_async_copy(source.at[rows], target.at[rows], sems.at[first + part])
        )
    return copies


def normal_kernel(
    pattern_hbm, couple_hbm, factor_hbm, normal_hbm,
    pattern, couple, factor, prod, flip, normal, sems,
):
    couples = copy_parts(couple_hbm, couple, sems, 0, 3)
    factors = copy_parts(factor_hbm, factor, sems, 3, 6)
    outs = copy_parts(normal, normal_hbm, sems, 9, 6)
    for part in range(3):
        for copy in (couples[part], factors[2 * part], factors[2 * part + 1]):
            copy.start()
    copy = pltpu.make_async_copy(pattern_hbm, pattern, sems.at[15])
    copy.start()
    copy.wait()
    side = [as_column(pattern[k : k + 1, :]) for k in range(2)]
    zeros = jnp.zeros((WIDTH, WIDTH), BF16)

    def product_row(r):
        for k in range(3):
            c = r + k - 1
            if not 0 <= c < ROWS:
                continue
            block = dot_nn(factor[r, k], couple[c])
            if k != 1:
                block = block * side[k // 2][r : r + 1, :]
            block = block.astype(BF16)
            prod[r, k] = block
            flip[c, :, (2 - k) * WIDTH : (3 - k) * WIDTH] = block.T

    def normal_row(d):
        for band in range(BANDS):
            c = d + band - 2
            if not 0 <= c < ROWS:
                normal[d, :, band * WIDTH : (band + 1) * WIDTH] = zeros
                continue
            if band < 2:
                continue
            terms = [r for r in (d - 1, d, d + 1) if 0 <= r < ROWS and abs(r - c) <= 1]
            first = terms[0] - d + 1
            left = flip[d, :, first * WIDTH : (first + len(terms)) * WIDTH]
            right = jnp.concatenate([prod[r, c - r + 1] for r in terms], axis=0)
            block = dot_nn(left, right).astype(BF16)
            normal[d, :, band * WIDTH : (band + 1) * WIDTH] = block
            if c != d:
                normal[c, :, (4 - band) * WIDTH : (5 - band) * WIDTH] = block.T

    for copy in couples[:2] + factors[:2]:
        copy.wait()
    for r in range(8):
        product_row(r)
    for copy in couples[2:] + factors[2:4]:
        copy.wait()
    for r in range(8, 16):
        product_row(r)
    for d in range(7):
        normal_row(d)
    outs[0].start()
    for copy in factors[4:]:
        copy.wait()
    for r in range(16, 24):
        product_row(r)
    for d in range(7, 12):
        normal_row(d)
    outs[1].start()
    outs[2].start()
    for d in range(12, 18):
        normal_row(d)
    outs[3].start()
    for d in range(18, 24):
        normal_row(d)
    outs[4].start()
    outs[5].start()
    for copy in outs:
        copy.wait()


def fetched(part, which, want):
    place = lax.broadcasted_iota(jnp.int32, (1, PLANE * HALF), 1)
    block = place + HALF * ((place * 1366) >> 16) + HALF * which
    return dot_nn(hot_of(want[:, 0:1] == block), part[...])


def load_kernel(
    near, normal_hbm, rhs_hbm, diag_hbm, idx_hbm, other_hbm,
    normal, rhs, diag, targets, labels, selector, found, idx, sems,
):
    core, chip, vec = here()
    index = [
        pltpu.make_async_copy(hbm, idx.at[k], sems.at[8 + k])
        for k, hbm in enumerate((idx_hbm, other_hbm))
    ]
    copies = [
        pltpu.make_async_copy(rhs_hbm, rhs, sems.at[6]),
        pltpu.make_async_copy(diag_hbm, diag, sems.at[7]),
    ]
    copies += copy_parts(normal_hbm, normal, sems, 0, 6)
    for copy in index + copies:
        copy.start()
    row = lax.broadcasted_iota(jnp.int32, (2 * CHIPS, CHIPS * SENT), 0)
    place = lax.broadcasted_iota(jnp.int32, (2 * CHIPS, CHIPS * SENT), 1)
    line = SENT * (row & (CHIPS - 1)) + ROWS + jnp.where(row < CHIPS, 0, 1)
    selector[...] = hot_of(place == line)
    for copy in index:
        copy.wait()
    want = scenario_targets(idx[0])
    targets[0:PAD, :] = want
    targets[PAD : PAD + OWN, :] = lax.broadcasted_iota(jnp.int32, (OWN, WIDTH), 0) + vec * OWN
    targets[PAD + OWN :, :] = scenario_targets(idx[1])
    found[...] = fetched(near, core, want)
    lane = lax.broadcasted_iota(jnp.int32, (ROWS, WIDTH), 1)
    rows = lax.broadcasted_iota(jnp.int32, (ROWS, WIDTH), 0)
    mine = rows == (lane - SENT * chip) & (WIDTH - 1)
    column = want[0:ROWS, :]
    for line, values in enumerate((column >> 8, column & 255)):
        labels[line : line + 1, :] = column_sum(jnp.where(mine, values, 0).astype(F32))
    for copy in copies:
        copy.wait()


def first_kernel(
    far, targets, labels, found, own, cost, normal, msg_out, us_out, inv_out
):
    core, chip, _ = here()
    total = found[...] + fetched(far, 1 - core, targets[0:PAD, :])
    us = total[:, 0:WIDTH]
    us_out[...], inv_out[...] = us, total[:, WIDTH:]
    lifted = scenario_lift(us, normal)
    r = own[...]
    ru = r * (r * (1.0 / cost[...]))
    lane = lax.broadcasted_iota(jnp.int32, (1, WIDTH), 1)
    turned = (lane - SENT * chip) & (WIDTH - 1)
    parts = []
    for k, line in enumerate(products(us, lifted, ru, ru)):
        high, low = split(jnp.sum(line, axis=1, keepdims=True))
        line = labels[k : k + 1, :]
        parts.append(jnp.where(turned == ROWS, high, jnp.where(turned == ROWS + 1, low, line)))
    write_message(msg_out, lifted, parts)


def give_and_keep(found, keep, give):
    keep[...] = found[0 : PAD + OWN, :]
    give[0:PAD, :] = found[PAD + OWN :, :]
    give[PAD:, :] = found[PAD : PAD + OWN, :]


def label_sum(part, targets, selector, hot, keep, give):
    want = targets[...]
    ends = dot_nn(selector[...], part[...])
    first, second = ends[0:CHIPS, :], ends[CHIPS:, :]
    message = lax.broadcasted_iota(jnp.int32, (CHIPS, WIDTH), 0) * SENT
    lane = lax.broadcasted_iota(jnp.int32, (CHIPS, WIDTH), 1)
    turned = (lane - message) & (WIDTH - 1)
    inner = [
        column_sum(jnp.where((turned >= ROWS) & (turned < SENT), e, 0.0)) for e in (first, second)
    ]
    labels = jnp.where(turned < ROWS, first * 256.0 + second, 0.0)
    at_chunk = (message + turned) >> 7
    for chunk in range(CHIPS * SENT // WIDTH):
        start = WIDTH * chunk
        found = column_sum(jnp.where(at_chunk == chunk, labels, 0.0)).astype(jnp.int32)
        place = lax.broadcasted_iota(jnp.int32, (1, WIDTH), 1) + start
        slot = place - SENT * ((place * 2521) >> 16)
        block = jnp.where(slot < ROWS, found, slot - ROWS + GAMMA)
        hot[:, start : start + WIDTH] = hot_of(want == block)
    give_and_keep(dot_nn(hot[...], part[...]), keep, give)
    for ref in (keep, give):
        for k in range(2):
            ref[ROWS + k : ROWS + k + 1, :] = inner[k]


def message_sum(part, hot, keep, give):
    give_and_keep(dot_nn(hot[...], part[...]), keep, give)


def advance(total, us, inv_s, ps, u, cost, q, d, x, r, gamma_old, alpha_old):
    gamma = jnp.sum(total[ROWS : ROWS + 1, :], axis=1, keepdims=True)
    delta = jnp.sum(total[ROWS + 1 : ROWS + 2, :], axis=1, keepdims=True)
    if gamma_old is None:
        alpha = gamma / delta
    else:
        beta = gamma / gamma_old
        alpha = gamma / (delta - beta * gamma / alpha_old)
    s = cost * u + total[PAD:, :]
    if gamma_old is None:
        d, q = u, s
    else:
        d, q = u + beta * d, s + beta * q
    x = alpha * d if x is None else x + alpha * d
    r = r - alpha * q
    if us is not None:
        rows = lax.broadcasted_iota(jnp.int32, (PAD, WIDTH), 0)
        own = jnp.where(rows < ROWS, us + inv_s * total[0:PAD, :], 0.0)
        ps = own if ps is None else own + beta * ps
        us = us - alpha * ps
    return gamma, alpha, us, ps, d, q, x, r


def second_kernel(
    keep, got, us, inv_s, own, cost, normal,
    msg_out, us_out, ps_out, scal_out, d_out, q_out, x_out, r_out,
):
    total = keep[...] + got[...]
    d = cost[...]
    inv = 1.0 / d
    r = own[...]
    gamma, alpha, u_s, p_s, dn, qn, xn, rn = advance(
        total, us[...], inv_s[...], None, inv * r, d, None, None, None, r, None, None
    )
    us_out[...], ps_out[...] = u_s, p_s
    d_out[...], q_out[...], x_out[...], r_out[...] = dn, qn, xn, rn
    scal_out[0:1, :] = jnp.broadcast_to(gamma, (1, WIDTH))
    scal_out[1:2, :] = jnp.broadcast_to(alpha, (1, WIDTH))
    next_message(msg_out, u_s, inv * rn, rn, d, normal)


def third_kernel(
    keep, got, us, ps, inv_s, scal, d, q, x, r, cost, normal,
    msg_out, scal_out, d_out, q_out, x_out, r_out,
):
    total = keep[...] + got[...]
    c = cost[...]
    inv = 1.0 / c
    gamma, alpha, u_s, p_s, dn, qn, xn, rn = advance(
        total, us[...], inv_s[...], ps[...], inv * r[...], c, q[...], d[...], x[...], r[...],
        scal[0:1, 0:1], scal[1:2, 0:1],
    )
    d_out[...], q_out[...], x_out[...], r_out[...] = dn, qn, xn, rn
    scal_out[0:1, :] = jnp.broadcast_to(gamma, (1, WIDTH))
    scal_out[1:2, :] = jnp.broadcast_to(alpha, (1, WIDTH))
    next_message(msg_out, u_s, inv * rn, rn, c, normal)


def last_kernel(keep, got, scal, d, q, x, r, cost, x_out, r_out):
    total = keep[...] + got[...]
    c = cost[...]
    found = advance(
        total, None, None, None, r[...] / c, c, q[...], d[...], x[...], r[...],
        scal[0:1, 0:1], scal[1:2, 0:1],
    )
    x_out[...], r_out[...] = found[6], found[7]


def call(kernel, shapes, *args, weights=(), scratch=(), sems=0, hbm_out=False):
    vmem = pl.BlockSpec(memory_space=pltpu.VMEM)
    specs = [vmem] * len(args) + [pl.BlockSpec(memory_space=pltpu.HBM)] * len(weights)
    scratch = [pltpu.VMEM(s, t) for s, t in scratch]
    if sems:
        scratch.append(pltpu.SemaphoreType.DMA((sems,)))
    return pl.pallas_call(
        kernel,
        out_shape=[(pltpu.HBM if hbm_out else jax.ShapeDtypeStruct)(s, t) for s, t in shapes],
        in_specs=specs,
        out_specs=[pl.BlockSpec(memory_space=pltpu.HBM) if hbm_out else vmem] * len(shapes),
        scratch_shapes=scratch,
        compiler_params=pltpu.CompilerParams(vmem_limit_bytes=32 * 1024 * 1024),
    )(*args, *weights)


def in_hbm(*arrays):
    return [pltpu.with_memory_space_constraint(a, pltpu.HBM) for a in arrays]


def other_core(values):
    return lax.ppermute(values, "core", [(0, 1), (1, 0)])


def to_all(sent):
    sent = sent.reshape(CHIPS, SENT // 2, 2, WIDTH)
    near = lax.all_to_all(sent, ("x", "z", "y"), 0, 0, tiled=True)
    return near.reshape(CHIPS * SENT, WIDTH)


def shards(rhs, diag, couple, couple_idx, factor, pattern):
    scen, own, msg = ((PAD, WIDTH), F32), ((OWN, WIDTH), F32), ((CHIPS * SENT, WIDTH), BF16)
    scal, sums = ((2, WIDTH), F32), ((PAD + OWN, WIDTH), F32)
    hots = ((PAD + OWN + PAD, CHIPS * SENT), BF16)
    aims = ((PAD + OWN + PAD, WIDTH), jnp.int32)
    selectors = ((2 * CHIPS, CHIPS * SENT), BF16)
    sent = call(
        opening_kernel, [((PLANE, HALF, 2 * WIDTH), BF16)], hbm_out=True,
        weights=in_hbm(rhs, diag), scratch=[own, own, ((HALF, 2 * WIDTH), BF16)], sems=2 + PLANE,
    )[0]
    near = lax.all_to_all(sent, ("z", "y"), 0, 0, tiled=True).reshape(PLANE * HALF, 2 * WIDTH)
    other_idx = other_core(couple_idx)
    triple, wide = (ROWS, 3, WIDTH, WIDTH), (ROWS, WIDTH, 3 * WIDTH)
    bands = ((ROWS, WIDTH, BANDS * WIDTH), BF16)
    normal = call(
        normal_kernel, [bands], hbm_out=True, sems=16,
        weights=in_hbm(pattern[0].T, couple[0], factor[0]),
        scratch=[
            ((2, ROWS), jnp.int32), ((ROWS, WIDTH, WIDTH), BF16), (triple, BF16),
            (triple, BF16), (wide, BF16), bands,
        ],
    )[0]
    near, normal, other_idx = lax.optimization_barrier((near, normal, other_idx))
    far = other_core(near)
    normal, r, cost, targets, labels, selector, found = call(
        load_kernel, [bands, own, own, aims, scal, selectors, ((PAD, 2 * WIDTH), F32)],
        near, weights=in_hbm(normal, rhs, diag, couple_idx, other_idx),
        scratch=[((2, 1, ROWS), jnp.int32)], sems=10,
    )
    sent, us, inv_s = call(
        first_kernel, [msg, scen, scen],
        far, targets, labels, found, r, cost, normal,
    )

    near = to_all(sent)
    hot, keep, give = call(label_sum, [hots, sums, sums], near, targets, selector)
    sent, us, ps, sc, d, q, x, r = call(
        second_kernel, [msg, scen, scen, scal, own, own, own, own],
        keep, other_core(give), us, inv_s, r, cost, normal,
    )
    near = to_all(sent)
    keep, give = call(message_sum, [sums, sums], near, hot)
    sent, sc, d, q, x, r = call(
        third_kernel, [msg, scal, own, own, own, own],
        keep, other_core(give), us, ps, inv_s, sc, d, q, x, r, cost, normal,
    )
    near = to_all(sent)
    keep, give = call(message_sum, [sums, sums], near, hot)
    return call(last_kernel, [own, own], keep, other_core(give), sc, d, q, x, r, cost)


def solution(mesh):
    fine = Mesh(np.array(mesh.devices).reshape(4, 2, 4, 4), ("x", "core", "z", "y"))
    vec, scen = ("z", "y"), ("x", "core", "z", "y")
    in_specs = (
        P(vec, None),
        P(vec, None),
        P(scen, None, None, None),
        P(scen, None),
        P(scen, None, None, None, None),
        P(scen, None, None),
    )
    out_specs = (P(vec, None), P(vec, None))
    return jax.shard_map(shards, mesh=fine, in_specs=in_specs, out_specs=out_specs, check_vma=False)
```

```python
import jax
import jax.numpy as jnp
import numpy as np
from jax import lax
from jax.experimental import pallas as pl
from jax.experimental.pallas import tpu as pltpu
from jax.sharding import Mesh
from jax.sharding import PartitionSpec as P

ROWS = 24
PAD = 32
SENT = 26
OWN = 96
HALF = OWN // 2
WIDTH = 128
CHIPS = 64
PLANE = 16
UPPER, LOWER = 3, 2
COPIES = 8
GAMMA, DELTA = 4000, 4001
F32, BF16 = jnp.float32, jnp.bfloat16


def dot_nn(a, b):
    return lax.dot_general(a, b, (((1,), (0,)), ((), ())), preferred_element_type=F32)


def dot_nt(a, b):
    return lax.dot_general(a, b, (((1,), (1,)), ((), ())), preferred_element_type=F32)


def split(values):
    high = values.astype(BF16).astype(F32)
    return high, values - high


def hot_of(mask):
    return mask.astype(F32).astype(BF16)


def only_row(values, r):
    rows = lax.broadcasted_iota(jnp.int32, (PAD, WIDTH), 0)
    return jnp.where(rows == r, values, 0.0).astype(BF16)


def scenario_lift(y, upper, lower):
    spread = jnp.zeros((PAD, (LOWER + UPPER) * WIDTH), F32)
    for r in range(0, ROWS, 2):
        pair = jnp.concatenate([only_row(y, r), only_row(y, r + 1)], axis=1)
        blocks = [m[r : r + 2].reshape(2 * WIDTH, m.shape[2]) for m in (lower, upper)]
        spread += dot_nn(pair, jnp.concatenate(blocks, axis=1))
    lifted = spread[:, LOWER * WIDTH : (LOWER + 1) * WIDTH]
    for band in (0, 1, 3, 4):
        part = spread[:, band * WIDTH : (band + 1) * WIDTH]
        lifted += pltpu.roll(part, (band - LOWER) % PAD, 0)
    return lifted


def write_message(msg_out, lifted, lines):
    rows = lax.broadcasted_iota(jnp.int32, (PAD, WIDTH), 0)
    out = lifted
    for place, line in enumerate(lines):
        out = jnp.where(rows == ROWS + place, jnp.broadcast_to(line, out.shape), out)
    row = lax.broadcasted_iota(jnp.int32, (COPIES * SENT, PAD), 0)
    column = lax.broadcasted_iota(jnp.int32, (COPIES * SENT, PAD), 1)
    again = hot_of(row - SENT * ((row * 2521) >> 16) == column)
    block = dot_nn(again, out.astype(BF16)).astype(BF16)
    for start in range(0, CHIPS * SENT, COPIES * SENT):
        msg_out[start : start + COPIES * SENT, :] = block


def column_sum(values):
    return jnp.sum(values, axis=0, keepdims=True)


def products(us, lifted, ru, cuu):
    return column_sum(ru) * 0.125, column_sum(cuu) * 0.125 + column_sum(us * lifted)


def folded(values):
    lane = lax.broadcasted_iota(jnp.int32, (1, WIDTH), 1)
    high, low = split(values + pltpu.roll(values, WIDTH // 2, 1))
    return jnp.where(lane < WIDTH // 2, high, low)


def next_message(msg_out, us, u, r, cost, upper, lower):
    lifted = scenario_lift(us, upper, lower)
    write_message(msg_out, lifted, [folded(v) for v in products(us, lifted, r * u, cost * u * u)])


def as_column(row):
    square = (ROWS, ROWS)
    same = lax.broadcasted_iota(jnp.int32, square, 0) == lax.broadcasted_iota(jnp.int32, square, 1)
    found = jnp.where(same, jnp.broadcast_to(row, square), 0).astype(F32)
    return jnp.broadcast_to(jnp.sum(found, axis=1, keepdims=True), (ROWS, WIDTH))


def scenario_targets(idx):
    rows = lax.broadcasted_iota(jnp.int32, (PAD - ROWS, WIDTH), 0)
    rest = jnp.where(rows < 2, rows + GAMMA, -9)
    return jnp.concatenate([as_column(idx).astype(jnp.int32), rest], axis=0)


def here():
    vec = lax.axis_index("z") * 4 + lax.axis_index("y")
    return lax.axis_index("core"), lax.axis_index("x") * PLANE + vec, vec


def copy_parts(source, target, sems, first, parts):
    step = source.shape[0] // parts
    copies = []
    for part in range(parts):
        rows = pl.ds(part * step, step)
        copies.append(
            pltpu.make_async_copy(source.at[rows], target.at[rows], sems.at[first + part])
        )
    return copies


def normal_kernel(
    pattern_hbm, couple_hbm, factor_hbm, upper_hbm,
    pattern, couple, factor, prod, flip, upper, sems,
):
    couples = copy_parts(couple_hbm, couple, sems, 0, 3)
    factors = copy_parts(factor_hbm, factor, sems, 3, 6)
    outs = copy_parts(upper, upper_hbm, sems, 9, 6)
    for part in range(3):
        for copy in (couples[part], factors[2 * part], factors[2 * part + 1]):
            copy.start()
    copy = pltpu.make_async_copy(pattern_hbm, pattern, sems.at[15])
    copy.start()
    copy.wait()
    side = [as_column(pattern[k : k + 1, :]) for k in range(2)]
    zeros = jnp.zeros((WIDTH, WIDTH), BF16)

    def product_row(r):
        for k in range(3):
            c = r + k - 1
            if not 0 <= c < ROWS:
                continue
            block = dot_nn(factor[r, k], couple[c])
            if k != 1:
                block = block * side[k // 2][r : r + 1, :]
            block = block.astype(BF16)
            prod[r, k] = block
            flip[c, :, (2 - k) * WIDTH : (3 - k) * WIDTH] = block.T

    def normal_row(d):
        for band in range(UPPER):
            c = d + band
            at = slice(band * WIDTH, (band + 1) * WIDTH)
            if c >= ROWS:
                upper[d, :, at] = zeros
                continue
            terms = [r for r in (d - 1, d, d + 1) if 0 <= r < ROWS and abs(r - c) <= 1]
            first = terms[0] - d + 1
            left = flip[d, :, first * WIDTH : (first + len(terms)) * WIDTH]
            right = jnp.concatenate([prod[r, c - r + 1] for r in terms], axis=0)
            upper[d, :, at] = dot_nn(left, right).astype(BF16)

    for copy in couples[:2] + factors[:2]:
        copy.wait()
    for r in range(8):
        product_row(r)
    for copy in couples[2:] + factors[2:4]:
        copy.wait()
    for r in range(8, 16):
        product_row(r)
    for d in range(7):
        normal_row(d)
    outs[0].start()
    for copy in factors[4:]:
        copy.wait()
    for r in range(16, 24):
        product_row(r)
    for d in range(7, 12):
        normal_row(d)
    outs[1].start()
    outs[2].start()
    for d in range(12, 18):
        normal_row(d)
    outs[3].start()
    for d in range(18, 24):
        normal_row(d)
    outs[4].start()
    outs[5].start()
    for copy in outs:
        copy.wait()


def fetched(part, which, want):
    place = lax.broadcasted_iota(jnp.int32, (1, PLANE * HALF), 1)
    block = place + HALF * ((place * 1366) >> 16) + HALF * which
    starts = range(0, PLANE * OWN, OWN)
    start = jnp.concatenate([part[k : k + HALF, :] for k in starts], axis=0)
    inverse = jnp.concatenate([part[k + HALF : k + OWN, :] for k in starts], axis=0)
    return dot_nn(hot_of(want[:, 0:1] == block), jnp.concatenate([start, inverse], axis=1))


def load_kernel(
    near, upper_hbm, rhs_hbm, diag_hbm, idx_hbm, other_hbm,
    upper, lower, rhs, diag, targets, labels, selector, found, idx, sems,
):
    core, chip, vec = here()
    index = [
        pltpu.make_async_copy(hbm, idx.at[k], sems.at[8 + k])
        for k, hbm in enumerate((idx_hbm, other_hbm))
    ]
    copies = [
        pltpu.make_async_copy(rhs_hbm, rhs, sems.at[6]),
        pltpu.make_async_copy(diag_hbm, diag, sems.at[7]),
    ]
    parts = copy_parts(upper_hbm, upper, sems, 0, 6)
    for copy in index + copies + parts:
        copy.start()
    row = lax.broadcasted_iota(jnp.int32, (2 * CHIPS, CHIPS * SENT), 0)
    place = lax.broadcasted_iota(jnp.int32, (2 * CHIPS, CHIPS * SENT), 1)
    line = SENT * (row & (CHIPS - 1)) + ROWS + jnp.where(row < CHIPS, 0, 1)
    selector[...] = hot_of(place == line)
    for copy in index:
        copy.wait()
    want = scenario_targets(idx[0])
    targets[0:PAD, :] = want
    targets[PAD : PAD + OWN, :] = lax.broadcasted_iota(jnp.int32, (OWN, WIDTH), 0) + vec * OWN
    targets[PAD + OWN :, :] = scenario_targets(idx[1])
    found[...] = fetched(near, core, want)
    lane = lax.broadcasted_iota(jnp.int32, (ROWS, WIDTH), 1)
    rows = lax.broadcasted_iota(jnp.int32, (ROWS, WIDTH), 0)
    mine = rows == (lane - SENT * chip) & (WIDTH - 1)
    column = want[0:ROWS, :]
    for line, values in enumerate((column >> 8, column & 255)):
        labels[line : line + 1, :] = column_sum(jnp.where(mine, values, 0).astype(F32))
    lower[0, :, :] = jnp.zeros((WIDTH, LOWER * WIDTH), BF16)
    lower[1, :, 0:WIDTH] = jnp.zeros((WIDTH, WIDTH), BF16)
    for d in range(ROWS):
        if d % 4 == 0:
            parts[d // 4].wait()
        for band in range(1, UPPER):
            if d + band < ROWS:
                at = (LOWER - band) * WIDTH
                block = upper[d, :, band * WIDTH : (band + 1) * WIDTH]
                lower[d + band, :, at : at + WIDTH] = block.T
    for copy in copies:
        copy.wait()


def first_kernel(
    far, targets, labels, found, own, cost, upper, lower, msg_out, us_out, inv_out
):
    core, chip, _ = here()
    total = found[...] + fetched(far, 1 - core, targets[0:PAD, :])
    us = total[:, 0:WIDTH]
    us_out[...], inv_out[...] = us, total[:, WIDTH:]
    lifted = scenario_lift(us, upper, lower)
    r = own[...]
    ru = r * (r * (1.0 / cost[...]))
    lane = lax.broadcasted_iota(jnp.int32, (1, WIDTH), 1)
    turned = (lane - SENT * chip) & (WIDTH - 1)
    parts = []
    for k, line in enumerate(products(us, lifted, ru, ru)):
        high, low = split(jnp.sum(line, axis=1, keepdims=True))
        line = labels[k : k + 1, :]
        parts.append(jnp.where(turned == ROWS, high, jnp.where(turned == ROWS + 1, low, line)))
    write_message(msg_out, lifted, parts)


def give_and_keep(found, keep, give):
    keep[...] = found[0 : PAD + OWN, :]
    give[0:PAD, :] = found[PAD + OWN :, :]
    give[PAD:, :] = found[PAD : PAD + OWN, :]


def label_sum(part, targets, selector, hot, keep, give):
    want = targets[...]
    ends = dot_nn(selector[...], part[...])
    first, second = ends[0:CHIPS, :], ends[CHIPS:, :]
    message = lax.broadcasted_iota(jnp.int32, (CHIPS, WIDTH), 0) * SENT
    lane = lax.broadcasted_iota(jnp.int32, (CHIPS, WIDTH), 1)
    turned = (lane - message) & (WIDTH - 1)
    inner = [
        column_sum(jnp.where((turned >= ROWS) & (turned < SENT), e, 0.0)) for e in (first, second)
    ]
    labels = jnp.where(turned < ROWS, first * 256.0 + second, 0.0)
    at_chunk = (message + turned) >> 7
    for chunk in range(CHIPS * SENT // WIDTH):
        start = WIDTH * chunk
        found = column_sum(jnp.where(at_chunk == chunk, labels, 0.0)).astype(jnp.int32)
        place = lax.broadcasted_iota(jnp.int32, (1, WIDTH), 1) + start
        slot = place - SENT * ((place * 2521) >> 16)
        block = jnp.where(slot < ROWS, found, slot - ROWS + GAMMA)
        hot[:, start : start + WIDTH] = hot_of(want == block)
    give_and_keep(dot_nn(hot[...], part[...]), keep, give)
    for ref in (keep, give):
        for k in range(2):
            ref[ROWS + k : ROWS + k + 1, :] = inner[k]


def message_sum(part, hot, keep, give):
    give_and_keep(dot_nn(hot[...], part[...]), keep, give)


def advance(total, us, inv_s, ps, u, cost, q, d, x, r, gamma_old, alpha_old):
    gamma = jnp.sum(total[ROWS : ROWS + 1, :], axis=1, keepdims=True)
    delta = jnp.sum(total[ROWS + 1 : ROWS + 2, :], axis=1, keepdims=True)
    if gamma_old is None:
        alpha = gamma / delta
    else:
        beta = gamma / gamma_old
        alpha = gamma / (delta - beta * gamma / alpha_old)
    s = cost * u + total[PAD:, :]
    if gamma_old is None:
        d, q = u, s
    else:
        d, q = u + beta * d, s + beta * q
    x = alpha * d if x is None else x + alpha * d
    r = r - alpha * q
    if us is not None:
        rows = lax.broadcasted_iota(jnp.int32, (PAD, WIDTH), 0)
        own = jnp.where(rows < ROWS, us + inv_s * total[0:PAD, :], 0.0)
        ps = own if ps is None else own + beta * ps
        us = us - alpha * ps
    return gamma, alpha, us, ps, d, q, x, r


def second_kernel(
    keep, got, us, inv_s, own, cost, upper, lower,
    msg_out, us_out, ps_out, scal_out, d_out, q_out, x_out, r_out,
):
    total = keep[...] + got[...]
    d = cost[...]
    inv = 1.0 / d
    r = own[...]
    gamma, alpha, u_s, p_s, dn, qn, xn, rn = advance(
        total, us[...], inv_s[...], None, inv * r, d, None, None, None, r, None, None
    )
    us_out[...], ps_out[...] = u_s, p_s
    d_out[...], q_out[...], x_out[...], r_out[...] = dn, qn, xn, rn
    scal_out[0:1, :] = jnp.broadcast_to(gamma, (1, WIDTH))
    scal_out[1:2, :] = jnp.broadcast_to(alpha, (1, WIDTH))
    next_message(msg_out, u_s, inv * rn, rn, d, upper, lower)


def third_kernel(
    keep, got, us, ps, inv_s, scal, d, q, x, r, cost, upper, lower,
    msg_out, scal_out, d_out, q_out, x_out, r_out,
):
    total = keep[...] + got[...]
    c = cost[...]
    inv = 1.0 / c
    gamma, alpha, u_s, p_s, dn, qn, xn, rn = advance(
        total, us[...], inv_s[...], ps[...], inv * r[...], c, q[...], d[...], x[...], r[...],
        scal[0:1, 0:1], scal[1:2, 0:1],
    )
    d_out[...], q_out[...], x_out[...], r_out[...] = dn, qn, xn, rn
    scal_out[0:1, :] = jnp.broadcast_to(gamma, (1, WIDTH))
    scal_out[1:2, :] = jnp.broadcast_to(alpha, (1, WIDTH))
    next_message(msg_out, u_s, inv * rn, rn, c, upper, lower)


def last_kernel(keep, got, scal, d, q, x, r, cost, x_out, r_out):
    total = keep[...] + got[...]
    c = cost[...]
    found = advance(
        total, None, None, None, r[...] / c, c, q[...], d[...], x[...], r[...],
        scal[0:1, 0:1], scal[1:2, 0:1],
    )
    x_out[...], r_out[...] = found[6], found[7]


def call(kernel, shapes, *args, weights=(), scratch=(), sems=0, hbm_out=False):
    vmem = pl.BlockSpec(memory_space=pltpu.VMEM)
    specs = [vmem] * len(args) + [pl.BlockSpec(memory_space=pltpu.HBM)] * len(weights)
    scratch = [pltpu.VMEM(s, t) for s, t in scratch]
    if sems:
        scratch.append(pltpu.SemaphoreType.DMA((sems,)))
    return pl.pallas_call(
        kernel,
        out_shape=[(pltpu.HBM if hbm_out else jax.ShapeDtypeStruct)(s, t) for s, t in shapes],
        in_specs=specs,
        out_specs=[pl.BlockSpec(memory_space=pltpu.HBM) if hbm_out else vmem] * len(shapes),
        scratch_shapes=scratch,
        compiler_params=pltpu.CompilerParams(vmem_limit_bytes=32 * 1024 * 1024),
    )(*args, *weights)


def in_hbm(*arrays):
    return [pltpu.with_memory_space_constraint(a, pltpu.HBM) for a in arrays]


def other_core(values):
    return lax.ppermute(values, "core", [(0, 1), (1, 0)])


def to_all(sent):
    sent = sent.reshape(CHIPS, SENT // 2, 2, WIDTH)
    near = lax.all_to_all(sent, ("x", "z", "y"), 0, 0, tiled=True)
    return near.reshape(CHIPS * SENT, WIDTH)


def shards(rhs, diag, couple, couple_idx, factor, pattern):
    scen, own, msg = ((PAD, WIDTH), F32), ((OWN, WIDTH), F32), ((CHIPS * SENT, WIDTH), BF16)
    scal, sums = ((2, WIDTH), F32), ((PAD + OWN, WIDTH), F32)
    hots = ((PAD + OWN + PAD, CHIPS * SENT), BF16)
    aims = ((PAD + OWN + PAD, WIDTH), jnp.int32)
    selectors = ((2 * CHIPS, CHIPS * SENT), BF16)
    first = lax.axis_index("core") * HALF
    inverse = 1.0 / lax.dynamic_slice_in_dim(diag, first, HALF, 0)
    start = lax.dynamic_slice_in_dim(rhs, first, HALF, 0) * inverse
    sent = jnp.concatenate([start.astype(BF16), inverse.astype(BF16)], axis=0)
    sent = jnp.broadcast_to(sent[None], (PLANE, OWN, WIDTH))
    near = lax.all_to_all(sent, ("z", "y"), 0, 0, tiled=True)
    near = near.reshape(PLANE * OWN, WIDTH)
    other_idx = other_core(couple_idx)
    triple, wide = (ROWS, 3, WIDTH, WIDTH), (ROWS, WIDTH, 3 * WIDTH)
    bands, below = [((ROWS, WIDTH, n * WIDTH), BF16) for n in (UPPER, LOWER)]
    upper = call(
        normal_kernel, [bands], hbm_out=True, sems=16,
        weights=in_hbm(pattern[0].T, couple[0], factor[0]),
        scratch=[
            ((2, ROWS), jnp.int32), ((ROWS, WIDTH, WIDTH), BF16), (triple, BF16),
            (triple, BF16), (wide, BF16), bands,
        ],
    )[0]
    near, upper, other_idx = lax.optimization_barrier((near, upper, other_idx))
    far = other_core(near)
    upper, lower, r, cost, targets, labels, selector, found = call(
        load_kernel, [bands, below, own, own, aims, scal, selectors, ((PAD, 2 * WIDTH), F32)],
        near, weights=in_hbm(upper, rhs, diag, couple_idx, other_idx),
        scratch=[((2, 1, ROWS), jnp.int32)], sems=10,
    )
    sent, us, inv_s = call(
        first_kernel, [msg, scen, scen],
        far, targets, labels, found, r, cost, upper, lower,
    )

    near = to_all(sent)
    hot, keep, give = call(label_sum, [hots, sums, sums], near, targets, selector)
    sent, us, ps, sc, d, q, x, r = call(
        second_kernel, [msg, scen, scen, scal, own, own, own, own],
        keep, other_core(give), us, inv_s, r, cost, upper, lower,
    )
    near = to_all(sent)
    keep, give = call(message_sum, [sums, sums], near, hot)
    sent, sc, d, q, x, r = call(
        third_kernel, [msg, scal, own, own, own, own],
        keep, other_core(give), us, ps, inv_s, sc, d, q, x, r, cost, upper, lower,
    )
    near = to_all(sent)
    keep, give = call(message_sum, [sums, sums], near, hot)
    return call(last_kernel, [own, own], keep, other_core(give), sc, d, q, x, r, cost)


def solution(mesh):
    fine = Mesh(np.array(mesh.devices).reshape(4, 2, 4, 4), ("x", "core", "z", "y"))
    vec, scen = ("z", "y"), ("x", "core", "z", "y")
    in_specs = (
        P(vec, None),
        P(vec, None),
        P(scen, None, None, None),
        P(scen, None),
        P(scen, None, None, None, None),
        P(scen, None, None),
    )
    out_specs = (P(vec, None), P(vec, None))
    return jax.shard_map(shards, mesh=fine, in_specs=in_specs, out_specs=out_specs, check_vma=False)
```

```python
import jax
import jax.numpy as jnp
import numpy as np
from jax import lax
from jax.experimental import pallas as pl
from jax.experimental.pallas import tpu as pltpu
from jax.sharding import Mesh
from jax.sharding import PartitionSpec as P

ROWS = 24
PAD = 32
SENT = 26
OWN = 96
HALF = OWN // 2
WIDTH = 128
CHIPS = 64
PLANE = 16
UPPER, LOWER = 3, 2
COPIES = 8
GAMMA, DELTA = 4000, 4001
F32, BF16 = jnp.float32, jnp.bfloat16


def dot_nn(a, b):
    return lax.dot_general(a, b, (((1,), (0,)), ((), ())), preferred_element_type=F32)


def dot_nt(a, b):
    return lax.dot_general(a, b, (((1,), (1,)), ((), ())), preferred_element_type=F32)


def split(values):
    high = values.astype(BF16).astype(F32)
    return high, values - high


def hot_of(mask):
    return mask.astype(F32).astype(BF16)


def only_row(values, r):
    rows = lax.broadcasted_iota(jnp.int32, (PAD, WIDTH), 0)
    return jnp.where(rows == r, values, 0.0).astype(BF16)


def scenario_lift(y, upper, lower):
    spread = jnp.zeros((PAD, (LOWER + UPPER) * WIDTH), F32)
    for r in range(0, ROWS, 2):
        pair = jnp.concatenate([only_row(y, r), only_row(y, r + 1)], axis=1)
        blocks = [m[r : r + 2].reshape(2 * WIDTH, m.shape[2]) for m in (lower, upper)]
        spread += dot_nn(pair, jnp.concatenate(blocks, axis=1))
    lifted = spread[:, LOWER * WIDTH : (LOWER + 1) * WIDTH]
    for band in (0, 1, 3, 4):
        part = spread[:, band * WIDTH : (band + 1) * WIDTH]
        lifted += pltpu.roll(part, (band - LOWER) % PAD, 0)
    return lifted


def write_message(msg_out, lifted, lines):
    rows = lax.broadcasted_iota(jnp.int32, (PAD, WIDTH), 0)
    out = lifted
    for place, line in enumerate(lines):
        out = jnp.where(rows == ROWS + place, jnp.broadcast_to(line, out.shape), out)
    row = lax.broadcasted_iota(jnp.int32, (COPIES * SENT, PAD), 0)
    column = lax.broadcasted_iota(jnp.int32, (COPIES * SENT, PAD), 1)
    again = hot_of(row - SENT * ((row * 2521) >> 16) == column)
    block = dot_nn(again, out.astype(BF16)).astype(BF16)
    for start in range(0, CHIPS * SENT, COPIES * SENT):
        msg_out[start : start + COPIES * SENT, :] = block


def column_sum(values):
    return jnp.sum(values, axis=0, keepdims=True)


def products(us, lifted, ru, cuu):
    return column_sum(ru) * 0.125, column_sum(cuu) * 0.125 + column_sum(us * lifted)


def folded(values):
    lane = lax.broadcasted_iota(jnp.int32, (1, WIDTH), 1)
    high, low = split(values + pltpu.roll(values, WIDTH // 2, 1))
    return jnp.where(lane < WIDTH // 2, high, low)


def next_message(msg_out, us, u, r, cost, upper, lower):
    lifted = scenario_lift(us, upper, lower)
    write_message(msg_out, lifted, [folded(v) for v in products(us, lifted, r * u, cost * u * u)])


def as_column(row):
    square = (ROWS, ROWS)
    same = lax.broadcasted_iota(jnp.int32, square, 0) == lax.broadcasted_iota(jnp.int32, square, 1)
    found = jnp.where(same, jnp.broadcast_to(row, square), 0).astype(F32)
    return jnp.broadcast_to(jnp.sum(found, axis=1, keepdims=True), (ROWS, WIDTH))


def scenario_targets(idx):
    rows = lax.broadcasted_iota(jnp.int32, (PAD - ROWS, WIDTH), 0)
    rest = jnp.where(rows < 2, rows + GAMMA, -9)
    return jnp.concatenate([as_column(idx).astype(jnp.int32), rest], axis=0)


def here():
    vec = lax.axis_index("z") * 4 + lax.axis_index("y")
    return lax.axis_index("core"), lax.axis_index("x") * PLANE + vec, vec


def copy_parts(source, target, sems, first, parts):
    step = source.shape[0] // parts
    copies = []
    for part in range(parts):
        rows = pl.ds(part * step, step)
        copies.append(
            pltpu.make_async_copy(source.at[rows], target.at[rows], sems.at[first + part])
        )
    return copies


def normal_kernel(
    pattern_hbm, couple_hbm, factor_hbm, upper, pattern, couple, factor, prod, flip, sems
):
    couples = copy_parts(couple_hbm, couple, sems, 0, 3)
    factors = copy_parts(factor_hbm, factor, sems, 3, 6)
    for part in range(3):
        for copy in (couples[part], factors[2 * part], factors[2 * part + 1]):
            copy.start()
    copy = pltpu.make_async_copy(pattern_hbm, pattern, sems.at[9])
    copy.start()
    copy.wait()
    side = [as_column(pattern[k : k + 1, :]) for k in range(2)]
    zeros = jnp.zeros((WIDTH, WIDTH), BF16)

    def product_row(r):
        for k in range(3):
            c = r + k - 1
            if not 0 <= c < ROWS:
                continue
            block = dot_nn(factor[r, k], couple[c])
            if k != 1:
                block = block * side[k // 2][r : r + 1, :]
            block = block.astype(BF16)
            prod[r, k] = block
            flip[c, :, (2 - k) * WIDTH : (3 - k) * WIDTH] = block.T

    def normal_row(d):
        for band in range(UPPER):
            c = d + band
            at = slice(band * WIDTH, (band + 1) * WIDTH)
            if c >= ROWS:
                upper[d, :, at] = zeros
                continue
            terms = [r for r in (d - 1, d, d + 1) if 0 <= r < ROWS and abs(r - c) <= 1]
            first = terms[0] - d + 1
            left = flip[d, :, first * WIDTH : (first + len(terms)) * WIDTH]
            right = jnp.concatenate([prod[r, c - r + 1] for r in terms], axis=0)
            upper[d, :, at] = dot_nn(left, right).astype(BF16)

    for copy in couples[:2] + factors[:2]:
        copy.wait()
    for r in range(8):
        product_row(r)
    for copy in couples[2:] + factors[2:4]:
        copy.wait()
    for r in range(8, 16):
        product_row(r)
    for d in range(7):
        normal_row(d)
    for copy in factors[4:]:
        copy.wait()
    for r in range(16, 24):
        product_row(r)
    for d in range(7, 12):
        normal_row(d)
    for d in range(12, 18):
        normal_row(d)
    for d in range(18, 24):
        normal_row(d)


def fetched(part, which, want):
    place = lax.broadcasted_iota(jnp.int32, (1, PLANE * HALF), 1)
    block = place + HALF * ((place * 1366) >> 16) + HALF * which
    starts = range(0, PLANE * OWN, OWN)
    start = jnp.concatenate([part[k : k + HALF, :] for k in starts], axis=0)
    inverse = jnp.concatenate([part[k + HALF : k + OWN, :] for k in starts], axis=0)
    return dot_nn(hot_of(want[:, 0:1] == block), jnp.concatenate([start, inverse], axis=1))


def load_kernel(
    near, upper, rhs_hbm, diag_hbm, idx_hbm, other_hbm,
    lower, rhs, diag, targets, labels, selector, found, idx, sems,
):
    core, chip, vec = here()
    index = [
        pltpu.make_async_copy(hbm, idx.at[k], sems.at[2 + k])
        for k, hbm in enumerate((idx_hbm, other_hbm))
    ]
    copies = [
        pltpu.make_async_copy(rhs_hbm, rhs, sems.at[0]),
        pltpu.make_async_copy(diag_hbm, diag, sems.at[1]),
    ]
    for copy in index + copies:
        copy.start()
    row = lax.broadcasted_iota(jnp.int32, (2 * CHIPS, CHIPS * SENT), 0)
    place = lax.broadcasted_iota(jnp.int32, (2 * CHIPS, CHIPS * SENT), 1)
    line = SENT * (row & (CHIPS - 1)) + ROWS + jnp.where(row < CHIPS, 0, 1)
    selector[...] = hot_of(place == line)
    for copy in index:
        copy.wait()
    want = scenario_targets(idx[0])
    targets[0:PAD, :] = want
    targets[PAD : PAD + OWN, :] = lax.broadcasted_iota(jnp.int32, (OWN, WIDTH), 0) + vec * OWN
    targets[PAD + OWN :, :] = scenario_targets(idx[1])
    found[...] = fetched(near, core, want)
    lane = lax.broadcasted_iota(jnp.int32, (ROWS, WIDTH), 1)
    rows = lax.broadcasted_iota(jnp.int32, (ROWS, WIDTH), 0)
    mine = rows == (lane - SENT * chip) & (WIDTH - 1)
    column = want[0:ROWS, :]
    for line, values in enumerate((column >> 8, column & 255)):
        labels[line : line + 1, :] = column_sum(jnp.where(mine, values, 0).astype(F32))
    lower[0, :, :] = jnp.zeros((WIDTH, LOWER * WIDTH), BF16)
    lower[1, :, 0:WIDTH] = jnp.zeros((WIDTH, WIDTH), BF16)
    for d in range(ROWS):
        for band in range(1, UPPER):
            if d + band < ROWS:
                at = (LOWER - band) * WIDTH
                block = upper[d, :, band * WIDTH : (band + 1) * WIDTH]
                lower[d + band, :, at : at + WIDTH] = block.T
    for copy in copies:
        copy.wait()


def first_kernel(
    far, targets, labels, found, own, cost, upper, lower, msg_out, us_out, inv_out
):
    core, chip, _ = here()
    total = found[...] + fetched(far, 1 - core, targets[0:PAD, :])
    us = total[:, 0:WIDTH]
    us_out[...], inv_out[...] = us, total[:, WIDTH:]
    lifted = scenario_lift(us, upper, lower)
    r = own[...]
    ru = r * (r * (1.0 / cost[...]))
    lane = lax.broadcasted_iota(jnp.int32, (1, WIDTH), 1)
    turned = (lane - SENT * chip) & (WIDTH - 1)
    parts = []
    for k, line in enumerate(products(us, lifted, ru, ru)):
        high, low = split(jnp.sum(line, axis=1, keepdims=True))
        line = labels[k : k + 1, :]
        parts.append(jnp.where(turned == ROWS, high, jnp.where(turned == ROWS + 1, low, line)))
    write_message(msg_out, lifted, parts)


def give_and_keep(found, keep, give):
    keep[...] = found[0 : PAD + OWN, :]
    give[0:PAD, :] = found[PAD + OWN :, :]
    give[PAD:, :] = found[PAD : PAD + OWN, :]


def label_sum(part, targets, selector, hot, keep, give):
    want = targets[...]
    ends = dot_nn(selector[...], part[...])
    first, second = ends[0:CHIPS, :], ends[CHIPS:, :]
    message = lax.broadcasted_iota(jnp.int32, (CHIPS, WIDTH), 0) * SENT
    lane = lax.broadcasted_iota(jnp.int32, (CHIPS, WIDTH), 1)
    turned = (lane - message) & (WIDTH - 1)
    inner = [
        column_sum(jnp.where((turned >= ROWS) & (turned < SENT), e, 0.0)) for e in (first, second)
    ]
    labels = jnp.where(turned < ROWS, first * 256.0 + second, 0.0)
    at_chunk = (message + turned) >> 7
    for chunk in range(CHIPS * SENT // WIDTH):
        start = WIDTH * chunk
        found = column_sum(jnp.where(at_chunk == chunk, labels, 0.0)).astype(jnp.int32)
        place = lax.broadcasted_iota(jnp.int32, (1, WIDTH), 1) + start
        slot = place - SENT * ((place * 2521) >> 16)
        block = jnp.where(slot < ROWS, found, slot - ROWS + GAMMA)
        hot[:, start : start + WIDTH] = hot_of(want == block)
    give_and_keep(dot_nn(hot[...], part[...]), keep, give)
    for ref in (keep, give):
        for k in range(2):
            ref[ROWS + k : ROWS + k + 1, :] = inner[k]


def message_sum(part, hot, keep, give):
    give_and_keep(dot_nn(hot[...], part[...]), keep, give)


def advance(total, us, inv_s, ps, u, cost, q, d, x, r, gamma_old, alpha_old):
    gamma = jnp.sum(total[ROWS : ROWS + 1, :], axis=1, keepdims=True)
    delta = jnp.sum(total[ROWS + 1 : ROWS + 2, :], axis=1, keepdims=True)
    if gamma_old is None:
        alpha = gamma / delta
    else:
        beta = gamma / gamma_old
        alpha = gamma / (delta - beta * gamma / alpha_old)
    s = cost * u + total[PAD:, :]
    if gamma_old is None:
        d, q = u, s
    else:
        d, q = u + beta * d, s + beta * q
    x = alpha * d if x is None else x + alpha * d
    r = r - alpha * q
    if us is not None:
        rows = lax.broadcasted_iota(jnp.int32, (PAD, WIDTH), 0)
        own = jnp.where(rows < ROWS, us + inv_s * total[0:PAD, :], 0.0)
        ps = own if ps is None else own + beta * ps
        us = us - alpha * ps
    return gamma, alpha, us, ps, d, q, x, r


def second_kernel(
    keep, got, us, inv_s, own, cost, upper, lower,
    msg_out, us_out, ps_out, scal_out, d_out, q_out, x_out, r_out,
):
    total = keep[...] + got[...]
    d = cost[...]
    inv = 1.0 / d
    r = own[...]
    gamma, alpha, u_s, p_s, dn, qn, xn, rn = advance(
        total, us[...], inv_s[...], None, inv * r, d, None, None, None, r, None, None
    )
    us_out[...], ps_out[...] = u_s, p_s
    d_out[...], q_out[...], x_out[...], r_out[...] = dn, qn, xn, rn
    scal_out[0:1, :] = jnp.broadcast_to(gamma, (1, WIDTH))
    scal_out[1:2, :] = jnp.broadcast_to(alpha, (1, WIDTH))
    next_message(msg_out, u_s, inv * rn, rn, d, upper, lower)


def third_kernel(
    keep, got, us, ps, inv_s, scal, d, q, x, r, cost, upper, lower,
    msg_out, scal_out, d_out, q_out, x_out, r_out,
):
    total = keep[...] + got[...]
    c = cost[...]
    inv = 1.0 / c
    gamma, alpha, u_s, p_s, dn, qn, xn, rn = advance(
        total, us[...], inv_s[...], ps[...], inv * r[...], c, q[...], d[...], x[...], r[...],
        scal[0:1, 0:1], scal[1:2, 0:1],
    )
    d_out[...], q_out[...], x_out[...], r_out[...] = dn, qn, xn, rn
    scal_out[0:1, :] = jnp.broadcast_to(gamma, (1, WIDTH))
    scal_out[1:2, :] = jnp.broadcast_to(alpha, (1, WIDTH))
    next_message(msg_out, u_s, inv * rn, rn, c, upper, lower)


def last_kernel(keep, got, scal, d, q, x, r, cost, x_out, r_out):
    total = keep[...] + got[...]
    c = cost[...]
    found = advance(
        total, None, None, None, r[...] / c, c, q[...], d[...], x[...], r[...],
        scal[0:1, 0:1], scal[1:2, 0:1],
    )
    x_out[...], r_out[...] = found[6], found[7]


def call(kernel, shapes, *args, weights=(), scratch=(), sems=0, hbm_out=False):
    vmem = pl.BlockSpec(memory_space=pltpu.VMEM)
    specs = [vmem] * len(args) + [pl.BlockSpec(memory_space=pltpu.HBM)] * len(weights)
    scratch = [pltpu.VMEM(s, t) for s, t in scratch]
    if sems:
        scratch.append(pltpu.SemaphoreType.DMA((sems,)))
    return pl.pallas_call(
        kernel,
        out_shape=[(pltpu.HBM if hbm_out else jax.ShapeDtypeStruct)(s, t) for s, t in shapes],
        in_specs=specs,
        out_specs=[pl.BlockSpec(memory_space=pltpu.HBM) if hbm_out else vmem] * len(shapes),
        scratch_shapes=scratch,
        compiler_params=pltpu.CompilerParams(vmem_limit_bytes=32 * 1024 * 1024),
    )(*args, *weights)


def in_hbm(*arrays):
    return [pltpu.with_memory_space_constraint(a, pltpu.HBM) for a in arrays]


def other_core(values):
    return lax.ppermute(values, "core", [(0, 1), (1, 0)])


def to_all(sent):
    sent = sent.reshape(CHIPS, SENT // 2, 2, WIDTH)
    near = lax.all_to_all(sent, ("x", "z", "y"), 0, 0, tiled=True)
    return near.reshape(CHIPS * SENT, WIDTH)


def shards(rhs, diag, couple, couple_idx, factor, pattern):
    scen, own, msg = ((PAD, WIDTH), F32), ((OWN, WIDTH), F32), ((CHIPS * SENT, WIDTH), BF16)
    scal, sums = ((2, WIDTH), F32), ((PAD + OWN, WIDTH), F32)
    hots = ((PAD + OWN + PAD, CHIPS * SENT), BF16)
    aims = ((PAD + OWN + PAD, WIDTH), jnp.int32)
    selectors = ((2 * CHIPS, CHIPS * SENT), BF16)
    first = lax.axis_index("core") * HALF
    inverse = 1.0 / lax.dynamic_slice_in_dim(diag, first, HALF, 0)
    start = lax.dynamic_slice_in_dim(rhs, first, HALF, 0) * inverse
    sent = jnp.concatenate([start.astype(BF16), inverse.astype(BF16)], axis=0)
    sent = jnp.broadcast_to(sent[None], (PLANE, OWN, WIDTH))
    near = lax.all_to_all(sent, ("z", "y"), 0, 0, tiled=True)
    near = near.reshape(PLANE * OWN, WIDTH)
    other_idx = other_core(couple_idx)
    triple, wide = (ROWS, 3, WIDTH, WIDTH), (ROWS, WIDTH, 3 * WIDTH)
    bands, below = [((ROWS, WIDTH, n * WIDTH), BF16) for n in (UPPER, LOWER)]
    upper = call(
        normal_kernel, [bands], sems=10,
        weights=in_hbm(pattern[0].T, couple[0], factor[0]),
        scratch=[
            ((2, ROWS), jnp.int32), ((ROWS, WIDTH, WIDTH), BF16), (triple, BF16),
            (triple, BF16), (wide, BF16),
        ],
    )[0]
    near, upper, other_idx = lax.optimization_barrier((near, upper, other_idx))
    far = other_core(near)
    lower, r, cost, targets, labels, selector, found = call(
        load_kernel, [below, own, own, aims, scal, selectors, ((PAD, 2 * WIDTH), F32)],
        near, upper, weights=in_hbm(rhs, diag, couple_idx, other_idx),
        scratch=[((2, 1, ROWS), jnp.int32)], sems=4,
    )
    sent, us, inv_s = call(
        first_kernel, [msg, scen, scen],
        far, targets, labels, found, r, cost, upper, lower,
    )

    near = to_all(sent)
    hot, keep, give = call(label_sum, [hots, sums, sums], near, targets, selector)
    sent, us, ps, sc, d, q, x, r = call(
        second_kernel, [msg, scen, scen, scal, own, own, own, own],
        keep, other_core(give), us, inv_s, r, cost, upper, lower,
    )
    near = to_all(sent)
    keep, give = call(message_sum, [sums, sums], near, hot)
    sent, sc, d, q, x, r = call(
        third_kernel, [msg, scal, own, own, own, own],
        keep, other_core(give), us, ps, inv_s, sc, d, q, x, r, cost, upper, lower,
    )
    near = to_all(sent)
    keep, give = call(message_sum, [sums, sums], near, hot)
    return call(last_kernel, [own, own], keep, other_core(give), sc, d, q, x, r, cost)


def solution(mesh):
    fine = Mesh(np.array(mesh.devices).reshape(4, 2, 4, 4), ("x", "core", "z", "y"))
    vec, scen = ("z", "y"), ("x", "core", "z", "y")
    in_specs = (
        P(vec, None),
        P(vec, None),
        P(scen, None, None, None),
        P(scen, None),
        P(scen, None, None, None, None),
        P(scen, None, None),
    )
    out_specs = (P(vec, None), P(vec, None))
    return jax.shard_map(shards, mesh=fine, in_specs=in_specs, out_specs=out_specs, check_vma=False)
```

```python
import jax
import jax.numpy as jnp
import numpy as np
from jax import lax
from jax.experimental import pallas as pl
from jax.experimental.pallas import tpu as pltpu
from jax.sharding import Mesh
from jax.sharding import PartitionSpec as P

ROWS = 24
PAD = 32
SENT = 26
OWN = 96
HALF = OWN // 2
WIDTH = 128
CHIPS = 64
PLANE = 16
UPPER, LOWER = 3, 2
COPIES = 8
GAMMA, DELTA = 4000, 4001
F32, BF16 = jnp.float32, jnp.bfloat16


def dot_nn(a, b):
    return lax.dot_general(a, b, (((1,), (0,)), ((), ())), preferred_element_type=F32)


def dot_nt(a, b):
    return lax.dot_general(a, b, (((1,), (1,)), ((), ())), preferred_element_type=F32)


def split(values):
    high = values.astype(BF16).astype(F32)
    return high, values - high


def hot_of(mask):
    return mask.astype(F32).astype(BF16)


def only_row(values, r):
    rows = lax.broadcasted_iota(jnp.int32, (PAD, WIDTH), 0)
    return jnp.where(rows == r, values, 0.0).astype(BF16)


def scenario_lift(y, upper, lower):
    spread = jnp.zeros((PAD, (LOWER + UPPER) * WIDTH), F32)
    for r in range(0, ROWS, 2):
        pair = jnp.concatenate([only_row(y, r), only_row(y, r + 1)], axis=1)
        blocks = [m[r : r + 2].reshape(2 * WIDTH, m.shape[2]) for m in (lower, upper)]
        spread += dot_nn(pair, jnp.concatenate(blocks, axis=1))
    lifted = spread[:, LOWER * WIDTH : (LOWER + 1) * WIDTH]
    for band in (0, 1, 3, 4):
        part = spread[:, band * WIDTH : (band + 1) * WIDTH]
        lifted += pltpu.roll(part, (band - LOWER) % PAD, 0)
    return lifted


def write_message(msg_out, lifted, lines):
    rows = lax.broadcasted_iota(jnp.int32, (PAD, WIDTH), 0)
    out = lifted
    for place, line in enumerate(lines):
        out = jnp.where(rows == ROWS + place, jnp.broadcast_to(line, out.shape), out)
    row = lax.broadcasted_iota(jnp.int32, (COPIES * SENT, PAD), 0)
    column = lax.broadcasted_iota(jnp.int32, (COPIES * SENT, PAD), 1)
    again = hot_of(row - SENT * ((row * 2521) >> 16) == column)
    block = dot_nn(again, out.astype(BF16)).astype(BF16)
    for start in range(0, CHIPS * SENT, COPIES * SENT):
        msg_out[start : start + COPIES * SENT, :] = block


def column_sum(values):
    return jnp.sum(values, axis=0, keepdims=True)


def products(us, lifted, ru, cuu):
    return column_sum(ru) * 0.125, column_sum(cuu) * 0.125 + column_sum(us * lifted)


def folded(values):
    lane = lax.broadcasted_iota(jnp.int32, (1, WIDTH), 1)
    high, low = split(values + pltpu.roll(values, WIDTH // 2, 1))
    return jnp.where(lane < WIDTH // 2, high, low)


def next_message(msg_out, us, u, r, cost, upper, lower):
    lifted = scenario_lift(us, upper, lower)
    write_message(msg_out, lifted, [folded(v) for v in products(us, lifted, r * u, cost * u * u)])


def as_column(row):
    square = (ROWS, ROWS)
    same = lax.broadcasted_iota(jnp.int32, square, 0) == lax.broadcasted_iota(jnp.int32, square, 1)
    found = jnp.where(same, jnp.broadcast_to(row, square), 0).astype(F32)
    return jnp.broadcast_to(jnp.sum(found, axis=1, keepdims=True), (ROWS, WIDTH))


def scenario_targets(idx):
    rows = lax.broadcasted_iota(jnp.int32, (PAD - ROWS, WIDTH), 0)
    rest = jnp.where(rows < 2, rows + GAMMA, -9)
    return jnp.concatenate([as_column(idx).astype(jnp.int32), rest], axis=0)


def here():
    vec = lax.axis_index("z") * 4 + lax.axis_index("y")
    return lax.axis_index("core"), lax.axis_index("x") * PLANE + vec, vec


def copy_parts(source, target, sems, first, parts):
    step = source.shape[0] // parts
    copies = []
    for part in range(parts):
        rows = pl.ds(part * step, step)
        copies.append(
            pltpu.make_async_copy(source.at[rows], target.at[rows], sems.at[first + part])
        )
    return copies


def normal_kernel(
    pattern_hbm, couple_hbm, factor_hbm, upper, pattern, couple, factor, prod, flip, sems
):
    couples = copy_parts(couple_hbm, couple, sems, 0, 3)
    factors = copy_parts(factor_hbm, factor, sems, 3, 6)
    for part in range(3):
        for copy in (couples[part], factors[2 * part], factors[2 * part + 1]):
            copy.start()
    copy = pltpu.make_async_copy(pattern_hbm, pattern, sems.at[9])
    copy.start()
    copy.wait()
    side = [as_column(pattern[k : k + 1, :]) for k in range(2)]
    zeros = jnp.zeros((WIDTH, WIDTH), BF16)

    def product_row(r):
        for k in range(3):
            c = r + k - 1
            if not 0 <= c < ROWS:
                continue
            block = dot_nn(factor[r, k], couple[c])
            if k != 1:
                block = block * side[k // 2][r : r + 1, :]
            block = block.astype(BF16)
            prod[r, k] = block
            flip[c, :, (2 - k) * WIDTH : (3 - k) * WIDTH] = block.T

    def normal_row(d):
        for band in range(UPPER):
            c = d + band
            at = slice(band * WIDTH, (band + 1) * WIDTH)
            if c >= ROWS:
                upper[d, :, at] = zeros
                continue
            terms = [r for r in (d - 1, d, d + 1) if 0 <= r < ROWS and abs(r - c) <= 1]
            first = terms[0] - d + 1
            left = flip[d, :, first * WIDTH : (first + len(terms)) * WIDTH]
            right = jnp.concatenate([prod[r, c - r + 1] for r in terms], axis=0)
            upper[d, :, at] = dot_nn(left, right).astype(BF16)

    for copy in couples[:2] + factors[:2]:
        copy.wait()
    for r in range(8):
        product_row(r)
    for copy in couples[2:] + factors[2:4]:
        copy.wait()
    for r in range(8, 16):
        product_row(r)
    for d in range(7):
        normal_row(d)
    for copy in factors[4:]:
        copy.wait()
    for r in range(16, 24):
        product_row(r)
    for d in range(7, 12):
        normal_row(d)
    for d in range(12, 18):
        normal_row(d)
    for d in range(18, 24):
        normal_row(d)


def fetched(part, which, want):
    place = lax.broadcasted_iota(jnp.int32, (1, PLANE * HALF), 1)
    block = place + HALF * ((place * 1366) >> 16) + HALF * which
    starts = range(0, PLANE * OWN, OWN)
    start = jnp.concatenate([part[k : k + HALF, :] for k in starts], axis=0)
    inverse = jnp.concatenate([part[k + HALF : k + OWN, :] for k in starts], axis=0)
    return dot_nn(hot_of(want[:, 0:1] == block), jnp.concatenate([start, inverse], axis=1))


def index_kernel(
    other_idx, rhs_hbm, diag_hbm, idx_hbm, rhs, diag, targets, labels, selector, idx, sems
):
    _, chip, vec = here()
    index = pltpu.make_async_copy(idx_hbm, idx, sems.at[2])
    index.start()
    copies = [
        pltpu.make_async_copy(rhs_hbm, rhs, sems.at[0]),
        pltpu.make_async_copy(diag_hbm, diag, sems.at[1]),
    ]
    for copy in copies:
        copy.start()
    row = lax.broadcasted_iota(jnp.int32, (2 * CHIPS, CHIPS * SENT), 0)
    place = lax.broadcasted_iota(jnp.int32, (2 * CHIPS, CHIPS * SENT), 1)
    line = SENT * (row & (CHIPS - 1)) + ROWS + jnp.where(row < CHIPS, 0, 1)
    selector[...] = hot_of(place == line)
    targets[PAD + OWN :, :] = scenario_targets(other_idx[...])
    index.wait()
    want = scenario_targets(idx[...])
    targets[0:PAD, :] = want
    targets[PAD : PAD + OWN, :] = lax.broadcasted_iota(jnp.int32, (OWN, WIDTH), 0) + vec * OWN
    lane = lax.broadcasted_iota(jnp.int32, (ROWS, WIDTH), 1)
    rows = lax.broadcasted_iota(jnp.int32, (ROWS, WIDTH), 0)
    mine = rows == (lane - SENT * chip) & (WIDTH - 1)
    column = want[0:ROWS, :]
    for line, values in enumerate((column >> 8, column & 255)):
        labels[line : line + 1, :] = column_sum(jnp.where(mine, values, 0).astype(F32))
    for copy in copies:
        copy.wait()


def fetch_kernel(near, targets, keep, give):
    want = jnp.concatenate([targets[0:PAD, 0:1], targets[PAD + OWN :, 0:1]], axis=0)
    place = lax.broadcasted_iota(jnp.int32, (1, PLANE * HALF), 1)
    block = place + HALF * ((place * 1366) >> 16) + HALF * lax.axis_index("core")
    starts = range(0, PLANE * OWN, OWN)
    start = jnp.concatenate([near[k : k + HALF, :] for k in starts], axis=0)
    inverse = jnp.concatenate([near[k + HALF : k + OWN, :] for k in starts], axis=0)
    found = dot_nn(hot_of(want == block), jnp.concatenate([start, inverse], axis=1))
    keep[...] = found[0:PAD, :]
    give[...] = found[PAD:, :].astype(BF16)


def lower_kernel(upper, lower):
    lower[0, :, :] = jnp.zeros((WIDTH, LOWER * WIDTH), BF16)
    lower[1, :, 0:WIDTH] = jnp.zeros((WIDTH, WIDTH), BF16)
    for d in range(ROWS):
        for band in range(1, UPPER):
            if d + band < ROWS:
                at = (LOWER - band) * WIDTH
                block = upper[d, :, band * WIDTH : (band + 1) * WIDTH]
                lower[d + band, :, at : at + WIDTH] = block.T


def first_kernel(keep, got, labels, own, cost, upper, lower, msg_out, us_out, inv_out):
    chip = here()[1]
    total = keep[...] + got[...].astype(F32)
    us = total[:, 0:WIDTH]
    us_out[...], inv_out[...] = us, total[:, WIDTH:]
    lifted = scenario_lift(us, upper, lower)
    r = own[...]
    ru = r * (r * (1.0 / cost[...]))
    lane = lax.broadcasted_iota(jnp.int32, (1, WIDTH), 1)
    turned = (lane - SENT * chip) & (WIDTH - 1)
    parts = []
    for k, line in enumerate(products(us, lifted, ru, ru)):
        high, low = split(jnp.sum(line, axis=1, keepdims=True))
        line = labels[k : k + 1, :]
        parts.append(jnp.where(turned == ROWS, high, jnp.where(turned == ROWS + 1, low, line)))
    write_message(msg_out, lifted, parts)


def give_and_keep(found, keep, give):
    keep[...] = found[0 : PAD + OWN, :]
    give[0:PAD, :] = found[PAD + OWN :, :]
    give[PAD:, :] = found[PAD : PAD + OWN, :]


def label_sum(part, targets, selector, hot, keep, give):
    want = targets[...]
    ends = dot_nn(selector[...], part[...])
    first, second = ends[0:CHIPS, :], ends[CHIPS:, :]
    message = lax.broadcasted_iota(jnp.int32, (CHIPS, WIDTH), 0) * SENT
    lane = lax.broadcasted_iota(jnp.int32, (CHIPS, WIDTH), 1)
    turned = (lane - message) & (WIDTH - 1)
    inner = [
        column_sum(jnp.where((turned >= ROWS) & (turned < SENT), e, 0.0)) for e in (first, second)
    ]
    labels = jnp.where(turned < ROWS, first * 256.0 + second, 0.0)
    at_chunk = (message + turned) >> 7
    for chunk in range(CHIPS * SENT // WIDTH):
        start = WIDTH * chunk
        found = column_sum(jnp.where(at_chunk == chunk, labels, 0.0)).astype(jnp.int32)
        place = lax.broadcasted_iota(jnp.int32, (1, WIDTH), 1) + start
        slot = place - SENT * ((place * 2521) >> 16)
        block = jnp.where(slot < ROWS, found, slot - ROWS + GAMMA)
        hot[:, start : start + WIDTH] = hot_of(want == block)
    give_and_keep(dot_nn(hot[...], part[...]), keep, give)
    for ref in (keep, give):
        for k in range(2):
            ref[ROWS + k : ROWS + k + 1, :] = inner[k]


def message_sum(part, hot, keep, give):
    give_and_keep(dot_nn(hot[...], part[...]), keep, give)


def advance(total, us, inv_s, ps, u, cost, q, d, x, r, gamma_old, alpha_old):
    gamma = jnp.sum(total[ROWS : ROWS + 1, :], axis=1, keepdims=True)
    delta = jnp.sum(total[ROWS + 1 : ROWS + 2, :], axis=1, keepdims=True)
    if gamma_old is None:
        alpha = gamma / delta
    else:
        beta = gamma / gamma_old
        alpha = gamma / (delta - beta * gamma / alpha_old)
    s = cost * u + total[PAD:, :]
    if gamma_old is None:
        d, q = u, s
    else:
        d, q = u + beta * d, s + beta * q
    x = alpha * d if x is None else x + alpha * d
    r = r - alpha * q
    if us is not None:
        rows = lax.broadcasted_iota(jnp.int32, (PAD, WIDTH), 0)
        own = jnp.where(rows < ROWS, us + inv_s * total[0:PAD, :], 0.0)
        ps = own if ps is None else own + beta * ps
        us = us - alpha * ps
    return gamma, alpha, us, ps, d, q, x, r


def second_kernel(
    keep, got, us, inv_s, own, cost, upper, lower,
    msg_out, us_out, ps_out, scal_out, d_out, q_out, x_out, r_out,
):
    total = keep[...] + got[...]
    d = cost[...]
    inv = 1.0 / d
    r = own[...]
    gamma, alpha, u_s, p_s, dn, qn, xn, rn = advance(
        total, us[...], inv_s[...], None, inv * r, d, None, None, None, r, None, None
    )
    us_out[...], ps_out[...] = u_s, p_s
    d_out[...], q_out[...], x_out[...], r_out[...] = dn, qn, xn, rn
    scal_out[0:1, :] = jnp.broadcast_to(gamma, (1, WIDTH))
    scal_out[1:2, :] = jnp.broadcast_to(alpha, (1, WIDTH))
    next_message(msg_out, u_s, inv * rn, rn, d, upper, lower)


def third_kernel(
    keep, got, us, ps, inv_s, scal, d, q, x, r, cost, upper, lower,
    msg_out, scal_out, d_out, q_out, x_out, r_out,
):
    total = keep[...] + got[...]
    c = cost[...]
    inv = 1.0 / c
    gamma, alpha, u_s, p_s, dn, qn, xn, rn = advance(
        total, us[...], inv_s[...], ps[...], inv * r[...], c, q[...], d[...], x[...], r[...],
        scal[0:1, 0:1], scal[1:2, 0:1],
    )
    d_out[...], q_out[...], x_out[...], r_out[...] = dn, qn, xn, rn
    scal_out[0:1, :] = jnp.broadcast_to(gamma, (1, WIDTH))
    scal_out[1:2, :] = jnp.broadcast_to(alpha, (1, WIDTH))
    next_message(msg_out, u_s, inv * rn, rn, c, upper, lower)


def last_kernel(keep, got, scal, d, q, x, r, cost, x_out, r_out):
    total = keep[...] + got[...]
    c = cost[...]
    found = advance(
        total, None, None, None, r[...] / c, c, q[...], d[...], x[...], r[...],
        scal[0:1, 0:1], scal[1:2, 0:1],
    )
    x_out[...], r_out[...] = found[6], found[7]


def call(kernel, shapes, *args, weights=(), scratch=(), sems=0, hbm_out=False):
    vmem = pl.BlockSpec(memory_space=pltpu.VMEM)
    specs = [vmem] * len(args) + [pl.BlockSpec(memory_space=pltpu.HBM)] * len(weights)
    scratch = [pltpu.VMEM(s, t) for s, t in scratch]
    if sems:
        scratch.append(pltpu.SemaphoreType.DMA((sems,)))
    return pl.pallas_call(
        kernel,
        out_shape=[(pltpu.HBM if hbm_out else jax.ShapeDtypeStruct)(s, t) for s, t in shapes],
        in_specs=specs,
        out_specs=[pl.BlockSpec(memory_space=pltpu.HBM) if hbm_out else vmem] * len(shapes),
        scratch_shapes=scratch,
        compiler_params=pltpu.CompilerParams(vmem_limit_bytes=32 * 1024 * 1024),
    )(*args, *weights)


def in_hbm(*arrays):
    return [pltpu.with_memory_space_constraint(a, pltpu.HBM) for a in arrays]


def other_core(values):
    return lax.ppermute(values, "core", [(0, 1), (1, 0)])


def to_all(sent):
    sent = sent.reshape(CHIPS, SENT // 2, 2, WIDTH)
    near = lax.all_to_all(sent, ("x", "z", "y"), 0, 0, tiled=True)
    return near.reshape(CHIPS * SENT, WIDTH)


def shards(rhs, diag, couple, couple_idx, factor, pattern):
    scen, own, msg = ((PAD, WIDTH), F32), ((OWN, WIDTH), F32), ((CHIPS * SENT, WIDTH), BF16)
    scal, sums = ((2, WIDTH), F32), ((PAD + OWN, WIDTH), F32)
    hots = ((PAD + OWN + PAD, CHIPS * SENT), BF16)
    aims = ((PAD + OWN + PAD, WIDTH), jnp.int32)
    selectors = ((2 * CHIPS, CHIPS * SENT), BF16)
    first = lax.axis_index("core") * HALF
    inverse = 1.0 / lax.dynamic_slice_in_dim(diag, first, HALF, 0)
    start = lax.dynamic_slice_in_dim(rhs, first, HALF, 0) * inverse
    sent = jnp.concatenate([start.astype(BF16), inverse.astype(BF16)], axis=0)
    sent = jnp.broadcast_to(sent[None], (PLANE, OWN, WIDTH))
    near = lax.all_to_all(sent, ("z", "y"), 0, 0, tiled=True)
    near = near.reshape(PLANE * OWN, WIDTH)
    other_idx = other_core(couple_idx)
    triple, wide = (ROWS, 3, WIDTH, WIDTH), (ROWS, WIDTH, 3 * WIDTH)
    bands, below = [((ROWS, WIDTH, n * WIDTH), BF16) for n in (UPPER, LOWER)]
    upper = call(
        normal_kernel, [bands], sems=10,
        weights=in_hbm(pattern[0].T, couple[0], factor[0]),
        scratch=[
            ((2, ROWS), jnp.int32), ((ROWS, WIDTH, WIDTH), BF16), (triple, BF16),
            (triple, BF16), (wide, BF16),
        ],
    )[0]
    r, cost, targets, labels, selector = call(
        index_kernel, [own, own, aims, scal, selectors],
        other_idx, weights=in_hbm(rhs, diag, couple_idx),
        scratch=[((1, ROWS), jnp.int32)], sems=3,
    )
    near, upper, r, cost, targets, labels, selector = lax.optimization_barrier(
        (near, upper, r, cost, targets, labels, selector)
    )
    pair = (PAD, 2 * WIDTH)
    keep, give = call(fetch_kernel, [(pair, F32), (pair, BF16)], near, targets)
    lower = call(lower_kernel, [below], upper)[0]
    sent, us, inv_s = call(
        first_kernel, [msg, scen, scen], keep, other_core(give), labels, r, cost, upper, lower
    )

    near = to_all(sent)
    hot, keep, give = call(label_sum, [hots, sums, sums], near, targets, selector)
    sent, us, ps, sc, d, q, x, r = call(
        second_kernel, [msg, scen, scen, scal, own, own, own, own],
        keep, other_core(give), us, inv_s, r, cost, upper, lower,
    )
    near = to_all(sent)
    keep, give = call(message_sum, [sums, sums], near, hot)
    sent, sc, d, q, x, r = call(
        third_kernel, [msg, scal, own, own, own, own],
        keep, other_core(give), us, ps, inv_s, sc, d, q, x, r, cost, upper, lower,
    )
    near = to_all(sent)
    keep, give = call(message_sum, [sums, sums], near, hot)
    return call(last_kernel, [own, own], keep, other_core(give), sc, d, q, x, r, cost)


def solution(mesh):
    fine = Mesh(np.array(mesh.devices).reshape(4, 2, 4, 4), ("x", "core", "z", "y"))
    vec, scen = ("z", "y"), ("x", "core", "z", "y")
    in_specs = (
        P(vec, None),
        P(vec, None),
        P(scen, None, None, None),
        P(scen, None),
        P(scen, None, None, None, None),
        P(scen, None, None),
    )
    out_specs = (P(vec, None), P(vec, None))
    return jax.shard_map(shards, mesh=fine, in_specs=in_specs, out_specs=out_specs, check_vma=False)
```

```python
import jax
import jax.numpy as jnp
import numpy as np
from jax import lax
from jax.experimental import pallas as pl
from jax.experimental.pallas import tpu as pltpu
from jax.sharding import Mesh
from jax.sharding import PartitionSpec as P

ROWS = 24
PAD = 32
SENT = 26
OWN = 96
HALF = OWN // 2
WIDTH = 128
CHIPS = 64
PLANE = 16
UPPER, LOWER = 3, 2
COPIES = 8
GAMMA, DELTA = 4000, 4001
F32, BF16 = jnp.float32, jnp.bfloat16


def dot_nn(a, b):
    return lax.dot_general(a, b, (((1,), (0,)), ((), ())), preferred_element_type=F32)


def dot_nt(a, b):
    return lax.dot_general(a, b, (((1,), (1,)), ((), ())), preferred_element_type=F32)


def split(values):
    high = values.astype(BF16).astype(F32)
    return high, values - high


def hot_of(mask):
    return mask.astype(F32).astype(BF16)


def only_row(values, r):
    rows = lax.broadcasted_iota(jnp.int32, (PAD, WIDTH), 0)
    return jnp.where(rows == r, values, 0.0).astype(BF16)


def scenario_lift(y, upper, lower):
    rows = lax.broadcasted_iota(jnp.int32, (PAD, WIDTH), 0)
    exact = y.astype(BF16).astype(F32)
    columns = jnp.concatenate([exact] * (WIDTH // PAD), axis=0).T
    spread = jnp.zeros((PAD, UPPER * WIDTH), F32)
    below = [jnp.zeros((PAD, WIDTH), F32) for band in range(LOWER)]
    for r in range(0, ROWS, 2):
        pair = jnp.concatenate([only_row(y, r), only_row(y, r + 1)], axis=1)
        spread += dot_nn(pair, upper[r : r + 2].reshape(2 * WIDTH, UPPER * WIDTH))
        for d in (r, r + 1):
            for band in range(LOWER):
                c = d + band - LOWER
                if c >= 0:
                    block = lower[d, :, band * WIDTH : (band + 1) * WIDTH].astype(F32)
                    line = column_sum(block * columns[:, d : d + 1])
                    below[band] = jnp.where(rows == c, line, below[band])
    lifted = spread[:, 0:WIDTH] + below[0] + below[1]
    for band in range(1, UPPER):
        lifted += pltpu.roll(spread[:, band * WIDTH : (band + 1) * WIDTH], band, 0)
    return lifted


def write_message(msg_out, lifted, lines):
    rows = lax.broadcasted_iota(jnp.int32, (PAD, WIDTH), 0)
    out = lifted
    for place, line in enumerate(lines):
        out = jnp.where(rows == ROWS + place, jnp.broadcast_to(line, out.shape), out)
    row = lax.broadcasted_iota(jnp.int32, (COPIES * SENT, PAD), 0)
    column = lax.broadcasted_iota(jnp.int32, (COPIES * SENT, PAD), 1)
    again = hot_of(row - SENT * ((row * 2521) >> 16) == column)
    block = dot_nn(again, out.astype(BF16)).astype(BF16)
    for start in range(0, CHIPS * SENT, COPIES * SENT):
        msg_out[start : start + COPIES * SENT, :] = block


def column_sum(values):
    return jnp.sum(values, axis=0, keepdims=True)


def products(us, lifted, ru, cuu):
    return column_sum(ru) * 0.125, column_sum(cuu) * 0.125 + column_sum(us * lifted)


def folded(values):
    lane = lax.broadcasted_iota(jnp.int32, (1, WIDTH), 1)
    high, low = split(values + pltpu.roll(values, WIDTH // 2, 1))
    return jnp.where(lane < WIDTH // 2, high, low)


def next_message(msg_out, us, u, r, cost, upper, lower):
    lifted = scenario_lift(us, upper, lower)
    write_message(msg_out, lifted, [folded(v) for v in products(us, lifted, r * u, cost * u * u)])


def as_column(row):
    square = (ROWS, ROWS)
    same = lax.broadcasted_iota(jnp.int32, square, 0) == lax.broadcasted_iota(jnp.int32, square, 1)
    found = jnp.where(same, jnp.broadcast_to(row, square), 0).astype(F32)
    return jnp.broadcast_to(jnp.sum(found, axis=1, keepdims=True), (ROWS, WIDTH))


def scenario_targets(idx):
    rows = lax.broadcasted_iota(jnp.int32, (PAD - ROWS, WIDTH), 0)
    rest = jnp.where(rows < 2, rows + GAMMA, -9)
    return jnp.concatenate([as_column(idx).astype(jnp.int32), rest], axis=0)


def here():
    vec = lax.axis_index("z") * 4 + lax.axis_index("y")
    return lax.axis_index("core"), lax.axis_index("x") * PLANE + vec, vec


def copy_parts(source, target, sems, first, parts):
    step = source.shape[0] // parts
    copies = []
    for part in range(parts):
        rows = pl.ds(part * step, step)
        copies.append(
            pltpu.make_async_copy(source.at[rows], target.at[rows], sems.at[first + part])
        )
    return copies


def normal_kernel(
    pattern_hbm, couple_hbm, factor_hbm, upper, pattern, couple, factor, prod, flip, sems
):
    couples = copy_parts(couple_hbm, couple, sems, 0, 3)
    factors = copy_parts(factor_hbm, factor, sems, 3, 6)
    for part in range(3):
        for copy in (couples[part], factors[2 * part], factors[2 * part + 1]):
            copy.start()
    copy = pltpu.make_async_copy(pattern_hbm, pattern, sems.at[9])
    copy.start()
    copy.wait()
    side = [as_column(pattern[k : k + 1, :]) for k in range(2)]
    zeros = jnp.zeros((WIDTH, WIDTH), BF16)

    def product_row(r):
        for k in range(3):
            c = r + k - 1
            if not 0 <= c < ROWS:
                continue
            block = dot_nn(factor[r, k], couple[c])
            if k != 1:
                block = block * side[k // 2][r : r + 1, :]
            block = block.astype(BF16)
            prod[r, k] = block
            flip[c, :, (2 - k) * WIDTH : (3 - k) * WIDTH] = block.T

    def normal_row(d):
        for band in range(UPPER):
            c = d + band
            at = slice(band * WIDTH, (band + 1) * WIDTH)
            if c >= ROWS:
                upper[d, :, at] = zeros
                continue
            terms = [r for r in (d - 1, d, d + 1) if 0 <= r < ROWS and abs(r - c) <= 1]
            first = terms[0] - d + 1
            left = flip[d, :, first * WIDTH : (first + len(terms)) * WIDTH]
            right = jnp.concatenate([prod[r, c - r + 1] for r in terms], axis=0)
            upper[d, :, at] = dot_nn(left, right).astype(BF16)

    for copy in couples[:2] + factors[:2]:
        copy.wait()
    for r in range(8):
        product_row(r)
    for copy in couples[2:] + factors[2:4]:
        copy.wait()
    for r in range(8, 16):
        product_row(r)
    for d in range(7):
        normal_row(d)
    for copy in factors[4:]:
        copy.wait()
    for r in range(16, 24):
        product_row(r)
    for d in range(7, 12):
        normal_row(d)
    for d in range(12, 18):
        normal_row(d)
    for d in range(18, 24):
        normal_row(d)


def fetched(part, which, want):
    place = lax.broadcasted_iota(jnp.int32, (1, PLANE * HALF), 1)
    block = place + HALF * ((place * 1366) >> 16) + HALF * which
    starts = range(0, PLANE * OWN, OWN)
    start = jnp.concatenate([part[k : k + HALF, :] for k in starts], axis=0)
    inverse = jnp.concatenate([part[k + HALF : k + OWN, :] for k in starts], axis=0)
    return dot_nn(hot_of(want[:, 0:1] == block), jnp.concatenate([start, inverse], axis=1))


def index_kernel(
    other_idx, rhs_hbm, diag_hbm, idx_hbm, rhs, diag, targets, labels, selector, idx, sems
):
    _, chip, vec = here()
    index = pltpu.make_async_copy(idx_hbm, idx, sems.at[2])
    index.start()
    copies = [
        pltpu.make_async_copy(rhs_hbm, rhs, sems.at[0]),
        pltpu.make_async_copy(diag_hbm, diag, sems.at[1]),
    ]
    for copy in copies:
        copy.start()
    row = lax.broadcasted_iota(jnp.int32, (2 * CHIPS, CHIPS * SENT), 0)
    place = lax.broadcasted_iota(jnp.int32, (2 * CHIPS, CHIPS * SENT), 1)
    line = SENT * (row & (CHIPS - 1)) + ROWS + jnp.where(row < CHIPS, 0, 1)
    selector[...] = hot_of(place == line)
    targets[PAD + OWN :, :] = scenario_targets(other_idx[...])
    index.wait()
    want = scenario_targets(idx[...])
    targets[0:PAD, :] = want
    targets[PAD : PAD + OWN, :] = lax.broadcasted_iota(jnp.int32, (OWN, WIDTH), 0) + vec * OWN
    lane = lax.broadcasted_iota(jnp.int32, (ROWS, WIDTH), 1)
    rows = lax.broadcasted_iota(jnp.int32, (ROWS, WIDTH), 0)
    mine = rows == (lane - SENT * chip) & (WIDTH - 1)
    column = want[0:ROWS, :]
    for line, values in enumerate((column >> 8, column & 255)):
        labels[line : line + 1, :] = column_sum(jnp.where(mine, values, 0).astype(F32))
    for copy in copies:
        copy.wait()


def fetch_kernel(near, targets, keep, give):
    want = jnp.concatenate([targets[0:PAD, 0:1], targets[PAD + OWN :, 0:1]], axis=0)
    place = lax.broadcasted_iota(jnp.int32, (1, PLANE * HALF), 1)
    block = place + HALF * ((place * 1366) >> 16) + HALF * lax.axis_index("core")
    starts = range(0, PLANE * OWN, OWN)
    start = jnp.concatenate([near[k : k + HALF, :] for k in starts], axis=0)
    inverse = jnp.concatenate([near[k + HALF : k + OWN, :] for k in starts], axis=0)
    found = dot_nn(hot_of(want == block), jnp.concatenate([start, inverse], axis=1))
    keep[...] = found[0:PAD, :]
    give[...] = found[PAD:, :].astype(BF16)


def lower_kernel(upper, lower):
    lower[0, :, :] = jnp.zeros((WIDTH, LOWER * WIDTH), BF16)
    lower[1, :, 0:WIDTH] = jnp.zeros((WIDTH, WIDTH), BF16)
    for d in range(ROWS):
        for band in range(1, UPPER):
            if d + band < ROWS:
                at = (LOWER - band) * WIDTH
                block = upper[d, :, band * WIDTH : (band + 1) * WIDTH]
                lower[d + band, :, at : at + WIDTH] = block.T


def first_kernel(keep, got, labels, own, cost, upper, lower, msg_out, us_out, inv_out):
    chip = here()[1]
    total = keep[...] + got[...].astype(F32)
    us = total[:, 0:WIDTH]
    us_out[...], inv_out[...] = us, total[:, WIDTH:]
    lifted = scenario_lift(us, upper, lower)
    r = own[...]
    ru = r * (r * (1.0 / cost[...]))
    lane = lax.broadcasted_iota(jnp.int32, (1, WIDTH), 1)
    turned = (lane - SENT * chip) & (WIDTH - 1)
    parts = []
    for k, line in enumerate(products(us, lifted, ru, ru)):
        high, low = split(jnp.sum(line, axis=1, keepdims=True))
        line = labels[k : k + 1, :]
        parts.append(jnp.where(turned == ROWS, high, jnp.where(turned == ROWS + 1, low, line)))
    write_message(msg_out, lifted, parts)


def give_and_keep(found, keep, give):
    keep[...] = found[0 : PAD + OWN, :]
    give[0:PAD, :] = found[PAD + OWN :, :]
    give[PAD:, :] = found[PAD : PAD + OWN, :]


def label_sum(part, targets, selector, hot, keep, give):
    want = targets[...]
    ends = dot_nn(selector[...], part[...])
    first, second = ends[0:CHIPS, :], ends[CHIPS:, :]
    message = lax.broadcasted_iota(jnp.int32, (CHIPS, WIDTH), 0) * SENT
    lane = lax.broadcasted_iota(jnp.int32, (CHIPS, WIDTH), 1)
    turned = (lane - message) & (WIDTH - 1)
    inner = [
        column_sum(jnp.where((turned >= ROWS) & (turned < SENT), e, 0.0)) for e in (first, second)
    ]
    labels = jnp.where(turned < ROWS, first * 256.0 + second, 0.0)
    at_chunk = (message + turned) >> 7
    for chunk in range(CHIPS * SENT // WIDTH):
        start = WIDTH * chunk
        found = column_sum(jnp.where(at_chunk == chunk, labels, 0.0)).astype(jnp.int32)
        place = lax.broadcasted_iota(jnp.int32, (1, WIDTH), 1) + start
        slot = place - SENT * ((place * 2521) >> 16)
        block = jnp.where(slot < ROWS, found, slot - ROWS + GAMMA)
        hot[:, start : start + WIDTH] = hot_of(want == block)
    give_and_keep(dot_nn(hot[...], part[...]), keep, give)
    for ref in (keep, give):
        for k in range(2):
            ref[ROWS + k : ROWS + k + 1, :] = inner[k]


def message_sum(part, hot, keep, give):
    give_and_keep(dot_nn(hot[...], part[...]), keep, give)


def advance(total, us, inv_s, ps, u, cost, q, d, x, r, gamma_old, alpha_old):
    gamma = jnp.sum(total[ROWS : ROWS + 1, :], axis=1, keepdims=True)
    delta = jnp.sum(total[ROWS + 1 : ROWS + 2, :], axis=1, keepdims=True)
    if gamma_old is None:
        alpha = gamma / delta
    else:
        beta = gamma / gamma_old
        alpha = gamma / (delta - beta * gamma / alpha_old)
    s = cost * u + total[PAD:, :]
    if gamma_old is None:
        d, q = u, s
    else:
        d, q = u + beta * d, s + beta * q
    x = alpha * d if x is None else x + alpha * d
    r = r - alpha * q
    if us is not None:
        rows = lax.broadcasted_iota(jnp.int32, (PAD, WIDTH), 0)
        own = jnp.where(rows < ROWS, us + inv_s * total[0:PAD, :], 0.0)
        ps = own if ps is None else own + beta * ps
        us = us - alpha * ps
    return gamma, alpha, us, ps, d, q, x, r


def second_kernel(
    keep, got, us, inv_s, own, cost, upper, lower,
    msg_out, us_out, ps_out, scal_out, d_out, q_out, x_out, r_out,
):
    total = keep[...] + got[...]
    d = cost[...]
    inv = 1.0 / d
    r = own[...]
    gamma, alpha, u_s, p_s, dn, qn, xn, rn = advance(
        total, us[...], inv_s[...], None, inv * r, d, None, None, None, r, None, None
    )
    us_out[...], ps_out[...] = u_s, p_s
    d_out[...], q_out[...], x_out[...], r_out[...] = dn, qn, xn, rn
    scal_out[0:1, :] = jnp.broadcast_to(gamma, (1, WIDTH))
    scal_out[1:2, :] = jnp.broadcast_to(alpha, (1, WIDTH))
    next_message(msg_out, u_s, inv * rn, rn, d, upper, lower)


def third_kernel(
    keep, got, us, ps, inv_s, scal, d, q, x, r, cost, upper, lower,
    msg_out, scal_out, d_out, q_out, x_out, r_out,
):
    total = keep[...] + got[...]
    c = cost[...]
    inv = 1.0 / c
    gamma, alpha, u_s, p_s, dn, qn, xn, rn = advance(
        total, us[...], inv_s[...], ps[...], inv * r[...], c, q[...], d[...], x[...], r[...],
        scal[0:1, 0:1], scal[1:2, 0:1],
    )
    d_out[...], q_out[...], x_out[...], r_out[...] = dn, qn, xn, rn
    scal_out[0:1, :] = jnp.broadcast_to(gamma, (1, WIDTH))
    scal_out[1:2, :] = jnp.broadcast_to(alpha, (1, WIDTH))
    next_message(msg_out, u_s, inv * rn, rn, c, upper, lower)


def last_kernel(keep, got, scal, d, q, x, r, cost, x_out, r_out):
    total = keep[...] + got[...]
    c = cost[...]
    found = advance(
        total, None, None, None, r[...] / c, c, q[...], d[...], x[...], r[...],
        scal[0:1, 0:1], scal[1:2, 0:1],
    )
    x_out[...], r_out[...] = found[6], found[7]


def call(kernel, shapes, *args, weights=(), scratch=(), sems=0, hbm_out=False):
    vmem = pl.BlockSpec(memory_space=pltpu.VMEM)
    specs = [vmem] * len(args) + [pl.BlockSpec(memory_space=pltpu.HBM)] * len(weights)
    scratch = [pltpu.VMEM(s, t) for s, t in scratch]
    if sems:
        scratch.append(pltpu.SemaphoreType.DMA((sems,)))
    return pl.pallas_call(
        kernel,
        out_shape=[(pltpu.HBM if hbm_out else jax.ShapeDtypeStruct)(s, t) for s, t in shapes],
        in_specs=specs,
        out_specs=[pl.BlockSpec(memory_space=pltpu.HBM) if hbm_out else vmem] * len(shapes),
        scratch_shapes=scratch,
        compiler_params=pltpu.CompilerParams(vmem_limit_bytes=32 * 1024 * 1024),
    )(*args, *weights)


def in_hbm(*arrays):
    return [pltpu.with_memory_space_constraint(a, pltpu.HBM) for a in arrays]


def other_core(values):
    return lax.ppermute(values, "core", [(0, 1), (1, 0)])


def to_all(sent):
    sent = sent.reshape(CHIPS, SENT // 2, 2, WIDTH)
    near = lax.all_to_all(sent, ("x", "z", "y"), 0, 0, tiled=True)
    return near.reshape(CHIPS * SENT, WIDTH)


def shards(rhs, diag, couple, couple_idx, factor, pattern):
    scen, own, msg = ((PAD, WIDTH), F32), ((OWN, WIDTH), F32), ((CHIPS * SENT, WIDTH), BF16)
    scal, sums = ((2, WIDTH), F32), ((PAD + OWN, WIDTH), F32)
    hots = ((PAD + OWN + PAD, CHIPS * SENT), BF16)
    aims = ((PAD + OWN + PAD, WIDTH), jnp.int32)
    selectors = ((2 * CHIPS, CHIPS * SENT), BF16)
    first = lax.axis_index("core") * HALF
    inverse = 1.0 / lax.dynamic_slice_in_dim(diag, first, HALF, 0)
    start = lax.dynamic_slice_in_dim(rhs, first, HALF, 0) * inverse
    sent = jnp.concatenate([start.astype(BF16), inverse.astype(BF16)], axis=0)
    sent = jnp.broadcast_to(sent[None], (PLANE, OWN, WIDTH))
    near = lax.all_to_all(sent, ("z", "y"), 0, 0, tiled=True)
    near = near.reshape(PLANE * OWN, WIDTH)
    other_idx = other_core(couple_idx)
    triple, wide = (ROWS, 3, WIDTH, WIDTH), (ROWS, WIDTH, 3 * WIDTH)
    bands, below = [((ROWS, WIDTH, n * WIDTH), BF16) for n in (UPPER, LOWER)]
    upper = call(
        normal_kernel, [bands], sems=10,
        weights=in_hbm(pattern[0].T, couple[0], factor[0]),
        scratch=[
            ((2, ROWS), jnp.int32), ((ROWS, WIDTH, WIDTH), BF16), (triple, BF16),
            (triple, BF16), (wide, BF16),
        ],
    )[0]
    r, cost, targets, labels, selector = call(
        index_kernel, [own, own, aims, scal, selectors],
        other_idx, weights=in_hbm(rhs, diag, couple_idx),
        scratch=[((1, ROWS), jnp.int32)], sems=3,
    )
    near, upper, r, cost, targets, labels, selector = lax.optimization_barrier(
        (near, upper, r, cost, targets, labels, selector)
    )
    pair = (PAD, 2 * WIDTH)
    keep, give = call(fetch_kernel, [(pair, F32), (pair, BF16)], near, targets)
    lower = call(lower_kernel, [below], upper)[0]
    sent, us, inv_s = call(
        first_kernel, [msg, scen, scen], keep, other_core(give), labels, r, cost, upper, lower
    )

    near = to_all(sent)
    hot, keep, give = call(label_sum, [hots, sums, sums], near, targets, selector)
    sent, us, ps, sc, d, q, x, r = call(
        second_kernel, [msg, scen, scen, scal, own, own, own, own],
        keep, other_core(give), us, inv_s, r, cost, upper, lower,
    )
    near = to_all(sent)
    keep, give = call(message_sum, [sums, sums], near, hot)
    sent, sc, d, q, x, r = call(
        third_kernel, [msg, scal, own, own, own, own],
        keep, other_core(give), us, ps, inv_s, sc, d, q, x, r, cost, upper, lower,
    )
    near = to_all(sent)
    keep, give = call(message_sum, [sums, sums], near, hot)
    return call(last_kernel, [own, own], keep, other_core(give), sc, d, q, x, r, cost)


def solution(mesh):
    fine = Mesh(np.array(mesh.devices).reshape(4, 2, 4, 4), ("x", "core", "z", "y"))
    vec, scen = ("z", "y"), ("x", "core", "z", "y")
    in_specs = (
        P(vec, None),
        P(vec, None),
        P(scen, None, None, None),
        P(scen, None),
        P(scen, None, None, None, None),
        P(scen, None, None),
    )
    out_specs = (P(vec, None), P(vec, None))
    return jax.shard_map(shards, mesh=fine, in_specs=in_specs, out_specs=out_specs, check_vma=False)
```

```python
import jax
import jax.numpy as jnp
import numpy as np
from jax import lax
from jax.experimental import pallas as pl
from jax.experimental.pallas import tpu as pltpu
from jax.sharding import Mesh
from jax.sharding import PartitionSpec as P

ROWS = 24
PAD = 32
SENT = 26
OWN = 96
HALF = OWN // 2
WIDTH = 128
CHIPS = 64
PLANE = 16
UPPER, LOWER = 3, 2
COPIES = 8
GAMMA, DELTA = 4000, 4001
F32, BF16 = jnp.float32, jnp.bfloat16


def dot_nn(a, b):
    return lax.dot_general(a, b, (((1,), (0,)), ((), ())), preferred_element_type=F32)


def dot_nt(a, b):
    return lax.dot_general(a, b, (((1,), (1,)), ((), ())), preferred_element_type=F32)


def split(values):
    high = values.astype(BF16).astype(F32)
    return high, values - high


def hot_of(mask):
    return mask.astype(F32).astype(BF16)


def only_row(values, r):
    rows = lax.broadcasted_iota(jnp.int32, (PAD, WIDTH), 0)
    return jnp.where(rows == r, values, 0.0).astype(BF16)


def scenario_lift(y, upper, lower):
    rows = lax.broadcasted_iota(jnp.int32, (PAD, WIDTH), 0)
    exact = y.astype(BF16).astype(F32)
    columns = jnp.concatenate([exact] * (WIDTH // PAD), axis=0).T
    spread = jnp.zeros((PAD, UPPER * WIDTH), F32)
    below = [jnp.zeros((PAD, WIDTH), F32) for band in range(LOWER)]
    for r in range(0, ROWS, 2):
        pair = jnp.concatenate([only_row(y, r), only_row(y, r + 1)], axis=1)
        spread += dot_nn(pair, upper[r : r + 2].reshape(2 * WIDTH, UPPER * WIDTH))
        for d in (r, r + 1):
            for band in range(LOWER):
                c = d + band - LOWER
                if c >= 0:
                    block = lower[d, :, band * WIDTH : (band + 1) * WIDTH].astype(F32)
                    line = column_sum(block * columns[:, d : d + 1])
                    below[band] = jnp.where(rows == c, line, below[band])
    lifted = spread[:, 0:WIDTH] + below[0] + below[1]
    for band in range(1, UPPER):
        lifted += pltpu.roll(spread[:, band * WIDTH : (band + 1) * WIDTH], band, 0)
    return lifted


def write_message(msg_out, lifted, lines):
    row = lax.broadcasted_iota(jnp.int32, (COPIES * SENT, PAD), 0)
    column = lax.broadcasted_iota(jnp.int32, (COPIES * SENT, PAD), 1)
    again = hot_of(row - SENT * ((row * 2521) >> 16) == column)
    block = dot_nn(again, lifted.astype(BF16))
    row = lax.broadcasted_iota(jnp.int32, (COPIES * SENT, WIDTH), 0)
    row = row - SENT * ((row * 2521) >> 16)
    for place, line in enumerate(lines):
        block = jnp.where(row == ROWS + place, line, block)
    block = block.astype(BF16)
    for start in range(0, CHIPS * SENT, COPIES * SENT):
        msg_out[start : start + COPIES * SENT, :] = block


def column_sum(values):
    return jnp.sum(values, axis=0, keepdims=True)


def products(us, lifted, ru, cuu):
    return column_sum(ru) * 0.125, column_sum(cuu) * 0.125 + column_sum(us * lifted)


def folded(values):
    lane = lax.broadcasted_iota(jnp.int32, (1, WIDTH), 1)
    high, low = split(values + pltpu.roll(values, WIDTH // 2, 1))
    return jnp.where(lane < WIDTH // 2, high, low)


def next_message(msg_out, us, u, r, cost, upper, lower):
    lifted = scenario_lift(us, upper, lower)
    write_message(msg_out, lifted, [folded(v) for v in products(us, lifted, r * u, cost * u * u)])


def as_column(row):
    square = (ROWS, ROWS)
    same = lax.broadcasted_iota(jnp.int32, square, 0) == lax.broadcasted_iota(jnp.int32, square, 1)
    found = jnp.where(same, jnp.broadcast_to(row, square), 0).astype(F32)
    return jnp.broadcast_to(jnp.sum(found, axis=1, keepdims=True), (ROWS, WIDTH))


def scenario_targets(idx):
    rows = lax.broadcasted_iota(jnp.int32, (PAD - ROWS, WIDTH), 0)
    rest = jnp.where(rows < 2, rows + GAMMA, -9)
    return jnp.concatenate([as_column(idx).astype(jnp.int32), rest], axis=0)


def here():
    vec = lax.axis_index("z") * 4 + lax.axis_index("y")
    return lax.axis_index("core"), lax.axis_index("x") * PLANE + vec, vec


def copy_parts(source, target, sems, first, parts):
    step = source.shape[0] // parts
    copies = []
    for part in range(parts):
        rows = pl.ds(part * step, step)
        copies.append(
            pltpu.make_async_copy(source.at[rows], target.at[rows], sems.at[first + part])
        )
    return copies


def normal_kernel(
    pattern_hbm, couple_hbm, factor_hbm, upper, pattern, couple, factor, prod, flip, sems
):
    couples = copy_parts(couple_hbm, couple, sems, 0, 3)
    factors = copy_parts(factor_hbm, factor, sems, 3, 6)
    for part in range(3):
        for copy in (couples[part], factors[2 * part], factors[2 * part + 1]):
            copy.start()
    copy = pltpu.make_async_copy(pattern_hbm, pattern, sems.at[9])
    copy.start()
    copy.wait()
    side = [as_column(pattern[k : k + 1, :]) for k in range(2)]
    zeros = jnp.zeros((WIDTH, WIDTH), BF16)

    def product_row(r):
        for k in range(3):
            c = r + k - 1
            if not 0 <= c < ROWS:
                continue
            block = dot_nn(factor[r, k], couple[c])
            if k != 1:
                block = block * side[k // 2][r : r + 1, :]
            block = block.astype(BF16)
            prod[r, k] = block
            flip[c, :, (2 - k) * WIDTH : (3 - k) * WIDTH] = block.T

    def normal_row(d):
        for band in range(UPPER):
            c = d + band
            at = slice(band * WIDTH, (band + 1) * WIDTH)
            if c >= ROWS:
                upper[d, :, at] = zeros
                continue
            terms = [r for r in (d - 1, d, d + 1) if 0 <= r < ROWS and abs(r - c) <= 1]
            first = terms[0] - d + 1
            left = flip[d, :, first * WIDTH : (first + len(terms)) * WIDTH]
            right = jnp.concatenate([prod[r, c - r + 1] for r in terms], axis=0)
            upper[d, :, at] = dot_nn(left, right).astype(BF16)

    for copy in couples[:2] + factors[:2]:
        copy.wait()
    for r in range(8):
        product_row(r)
    for copy in couples[2:] + factors[2:4]:
        copy.wait()
    for r in range(8, 16):
        product_row(r)
    for d in range(7):
        normal_row(d)
    for copy in factors[4:]:
        copy.wait()
    for r in range(16, 24):
        product_row(r)
    for d in range(7, 12):
        normal_row(d)
    for d in range(12, 18):
        normal_row(d)
    for d in range(18, 24):
        normal_row(d)


def fetched(part, which, want):
    place = lax.broadcasted_iota(jnp.int32, (1, PLANE * HALF), 1)
    block = place + HALF * ((place * 1366) >> 16) + HALF * which
    starts = range(0, PLANE * OWN, OWN)
    start = jnp.concatenate([part[k : k + HALF, :] for k in starts], axis=0)
    inverse = jnp.concatenate([part[k + HALF : k + OWN, :] for k in starts], axis=0)
    return dot_nn(hot_of(want[:, 0:1] == block), jnp.concatenate([start, inverse], axis=1))


def index_kernel(
    other_idx, rhs_hbm, diag_hbm, idx_hbm, rhs, diag, targets, labels, selector, idx, sems
):
    _, chip, vec = here()
    index = pltpu.make_async_copy(idx_hbm, idx, sems.at[2])
    index.start()
    copies = [
        pltpu.make_async_copy(rhs_hbm, rhs, sems.at[0]),
        pltpu.make_async_copy(diag_hbm, diag, sems.at[1]),
    ]
    for copy in copies:
        copy.start()
    row = lax.broadcasted_iota(jnp.int32, (2 * CHIPS, CHIPS * SENT), 0)
    place = lax.broadcasted_iota(jnp.int32, (2 * CHIPS, CHIPS * SENT), 1)
    line = SENT * (row & (CHIPS - 1)) + ROWS + jnp.where(row < CHIPS, 0, 1)
    selector[...] = hot_of(place == line)
    targets[PAD + OWN :, :] = scenario_targets(other_idx[...])
    index.wait()
    want = scenario_targets(idx[...])
    targets[0:PAD, :] = want
    targets[PAD : PAD + OWN, :] = lax.broadcasted_iota(jnp.int32, (OWN, WIDTH), 0) + vec * OWN
    lane = lax.broadcasted_iota(jnp.int32, (ROWS, WIDTH), 1)
    rows = lax.broadcasted_iota(jnp.int32, (ROWS, WIDTH), 0)
    mine = rows == (lane - SENT * chip) & (WIDTH - 1)
    column = want[0:ROWS, :]
    for line, values in enumerate((column >> 8, column & 255)):
        labels[line : line + 1, :] = column_sum(jnp.where(mine, values, 0).astype(F32))
    for copy in copies:
        copy.wait()


def fetch_kernel(near, targets, keep, give):
    want = jnp.concatenate([targets[0:PAD, 0:1], targets[PAD + OWN :, 0:1]], axis=0)
    place = lax.broadcasted_iota(jnp.int32, (1, PLANE * HALF), 1)
    block = place + HALF * ((place * 1366) >> 16) + HALF * lax.axis_index("core")
    starts = range(0, PLANE * OWN, OWN)
    start = jnp.concatenate([near[k : k + HALF, :] for k in starts], axis=0)
    inverse = jnp.concatenate([near[k + HALF : k + OWN, :] for k in starts], axis=0)
    found = dot_nn(hot_of(want == block), jnp.concatenate([start, inverse], axis=1))
    keep[...] = found[0:PAD, :]
    give[...] = found[PAD:, :].astype(BF16)


def lower_kernel(upper, lower):
    lower[0, :, :] = jnp.zeros((WIDTH, LOWER * WIDTH), BF16)
    lower[1, :, 0:WIDTH] = jnp.zeros((WIDTH, WIDTH), BF16)
    for d in range(ROWS):
        for band in range(1, UPPER):
            if d + band < ROWS:
                at = (LOWER - band) * WIDTH
                block = upper[d, :, band * WIDTH : (band + 1) * WIDTH]
                lower[d + band, :, at : at + WIDTH] = block.T


def first_kernel(keep, got, labels, own, cost, upper, lower, msg_out, us_out, inv_out):
    chip = here()[1]
    total = keep[...] + got[...].astype(F32)
    us = total[:, 0:WIDTH]
    us_out[...], inv_out[...] = us, total[:, WIDTH:]
    lifted = scenario_lift(us, upper, lower)
    r = own[...]
    ru = r * (r * (1.0 / cost[...]))
    lane = lax.broadcasted_iota(jnp.int32, (1, WIDTH), 1)
    turned = (lane - SENT * chip) & (WIDTH - 1)
    parts = []
    for k, line in enumerate(products(us, lifted, ru, ru)):
        high, low = split(jnp.sum(line, axis=1, keepdims=True))
        line = labels[k : k + 1, :]
        parts.append(jnp.where(turned == ROWS, high, jnp.where(turned == ROWS + 1, low, line)))
    write_message(msg_out, lifted, parts)


def give_and_keep(found, keep, give):
    keep[...] = found[0 : PAD + OWN, :]
    give[0:PAD, :] = found[PAD + OWN :, :]
    give[PAD:, :] = found[PAD : PAD + OWN, :]


def label_sum(part, targets, selector, hot, keep, give):
    want = targets[...]
    ends = dot_nn(selector[...], part[...])
    first, second = ends[0:CHIPS, :], ends[CHIPS:, :]
    message = lax.broadcasted_iota(jnp.int32, (CHIPS, WIDTH), 0) * SENT
    lane = lax.broadcasted_iota(jnp.int32, (CHIPS, WIDTH), 1)
    turned = (lane - message) & (WIDTH - 1)
    inner = [
        column_sum(jnp.where((turned >= ROWS) & (turned < SENT), e, 0.0)) for e in (first, second)
    ]
    labels = jnp.where(turned < ROWS, first * 256.0 + second, 0.0)
    at_chunk = (message + turned) >> 7
    for chunk in range(CHIPS * SENT // WIDTH):
        start = WIDTH * chunk
        found = column_sum(jnp.where(at_chunk == chunk, labels, 0.0)).astype(jnp.int32)
        place = lax.broadcasted_iota(jnp.int32, (1, WIDTH), 1) + start
        slot = place - SENT * ((place * 2521) >> 16)
        block = jnp.where(slot < ROWS, found, slot - ROWS + GAMMA)
        hot[:, start : start + WIDTH] = hot_of(want == block)
    give_and_keep(dot_nn(hot[...], part[...]), keep, give)
    for ref in (keep, give):
        for k in range(2):
            ref[ROWS + k : ROWS + k + 1, :] = inner[k]


def message_sum(part, hot, keep, give):
    give_and_keep(dot_nn(hot[...], part[...]), keep, give)


def advance(total, us, inv_s, ps, u, cost, q, d, x, r, per_gamma, per_alpha):
    gamma = jnp.sum(total[ROWS : ROWS + 1, :], axis=1, keepdims=True)
    delta = jnp.sum(total[ROWS + 1 : ROWS + 2, :], axis=1, keepdims=True)
    if per_gamma is None:
        alpha = gamma / delta
    else:
        beta = gamma * per_gamma
        alpha = gamma / (delta - beta * (gamma * per_alpha))
    s = cost * u + total[PAD:, :]
    if per_gamma is None:
        d, q = u, s
    else:
        d, q = u + beta * d, s + beta * q
    x = alpha * d if x is None else x + alpha * d
    r = r - alpha * q
    if us is not None:
        rows = lax.broadcasted_iota(jnp.int32, (PAD, WIDTH), 0)
        own = jnp.where(rows < ROWS, us + inv_s * total[0:PAD, :], 0.0)
        ps = own if ps is None else own + beta * ps
        us = us - alpha * ps
    return gamma, alpha, us, ps, d, q, x, r


def second_kernel(
    keep, got, us, inv_s, own, cost, upper, lower,
    msg_out, us_out, ps_out, scal_out, d_out, q_out, x_out, r_out,
):
    total = keep[...] + got[...]
    d = cost[...]
    inv = 1.0 / d
    r = own[...]
    gamma, alpha, u_s, p_s, dn, qn, xn, rn = advance(
        total, us[...], inv_s[...], None, inv * r, d, None, None, None, r, None, None
    )
    us_out[...], ps_out[...] = u_s, p_s
    d_out[...], q_out[...], x_out[...], r_out[...] = dn, qn, xn, rn
    scal_out[0:1, :] = jnp.broadcast_to(1.0 / gamma, (1, WIDTH))
    scal_out[1:2, :] = jnp.broadcast_to(1.0 / alpha, (1, WIDTH))
    next_message(msg_out, u_s, inv * rn, rn, d, upper, lower)


def third_kernel(
    keep, got, us, ps, inv_s, scal, d, q, x, r, cost, upper, lower,
    msg_out, scal_out, d_out, q_out, x_out, r_out,
):
    total = keep[...] + got[...]
    c = cost[...]
    inv = 1.0 / c
    gamma, alpha, u_s, p_s, dn, qn, xn, rn = advance(
        total, us[...], inv_s[...], ps[...], inv * r[...], c, q[...], d[...], x[...], r[...],
        scal[0:1, 0:1], scal[1:2, 0:1],
    )
    d_out[...], q_out[...], x_out[...], r_out[...] = dn, qn, xn, rn
    scal_out[0:1, :] = jnp.broadcast_to(1.0 / gamma, (1, WIDTH))
    scal_out[1:2, :] = jnp.broadcast_to(1.0 / alpha, (1, WIDTH))
    next_message(msg_out, u_s, inv * rn, rn, c, upper, lower)


def last_kernel(keep, got, scal, d, q, x, r, cost, x_out, r_out):
    total = keep[...] + got[...]
    c = cost[...]
    found = advance(
        total, None, None, None, r[...] / c, c, q[...], d[...], x[...], r[...],
        scal[0:1, 0:1], scal[1:2, 0:1],
    )
    x_out[...], r_out[...] = found[6], found[7]


def call(kernel, shapes, *args, weights=(), scratch=(), sems=0, hbm_out=False):
    vmem = pl.BlockSpec(memory_space=pltpu.VMEM)
    specs = [vmem] * len(args) + [pl.BlockSpec(memory_space=pltpu.HBM)] * len(weights)
    scratch = [pltpu.VMEM(s, t) for s, t in scratch]
    if sems:
        scratch.append(pltpu.SemaphoreType.DMA((sems,)))
    return pl.pallas_call(
        kernel,
        out_shape=[(pltpu.HBM if hbm_out else jax.ShapeDtypeStruct)(s, t) for s, t in shapes],
        in_specs=specs,
        out_specs=[pl.BlockSpec(memory_space=pltpu.HBM) if hbm_out else vmem] * len(shapes),
        scratch_shapes=scratch,
        compiler_params=pltpu.CompilerParams(vmem_limit_bytes=32 * 1024 * 1024),
    )(*args, *weights)


def in_hbm(*arrays):
    return [pltpu.with_memory_space_constraint(a, pltpu.HBM) for a in arrays]


def other_core(values):
    return lax.ppermute(values, "core", [(0, 1), (1, 0)])


def to_all(sent):
    sent = sent.reshape(CHIPS, SENT // 2, 2, WIDTH)
    near = lax.all_to_all(sent, ("x", "z", "y"), 0, 0, tiled=True)
    return near.reshape(CHIPS * SENT, WIDTH)


def shards(rhs, diag, couple, couple_idx, factor, pattern):
    scen, own, msg = ((PAD, WIDTH), F32), ((OWN, WIDTH), F32), ((CHIPS * SENT, WIDTH), BF16)
    scal, sums = ((2, WIDTH), F32), ((PAD + OWN, WIDTH), F32)
    hots = ((PAD + OWN + PAD, CHIPS * SENT), BF16)
    aims = ((PAD + OWN + PAD, WIDTH), jnp.int32)
    selectors = ((2 * CHIPS, CHIPS * SENT), BF16)
    first = lax.axis_index("core") * HALF
    inverse = 1.0 / lax.dynamic_slice_in_dim(diag, first, HALF, 0)
    start = lax.dynamic_slice_in_dim(rhs, first, HALF, 0) * inverse
    sent = jnp.concatenate([start.astype(BF16), inverse.astype(BF16)], axis=0)
    sent = jnp.broadcast_to(sent[None], (PLANE, OWN, WIDTH))
    near = lax.all_to_all(sent, ("z", "y"), 0, 0, tiled=True)
    near = near.reshape(PLANE * OWN, WIDTH)
    other_idx = other_core(couple_idx)
    triple, wide = (ROWS, 3, WIDTH, WIDTH), (ROWS, WIDTH, 3 * WIDTH)
    bands, below = [((ROWS, WIDTH, n * WIDTH), BF16) for n in (UPPER, LOWER)]
    upper = call(
        normal_kernel, [bands], sems=10,
        weights=in_hbm(pattern[0].T, couple[0], factor[0]),
        scratch=[
            ((2, ROWS), jnp.int32), ((ROWS, WIDTH, WIDTH), BF16), (triple, BF16),
            (triple, BF16), (wide, BF16),
        ],
    )[0]
    r, cost, targets, labels, selector = call(
        index_kernel, [own, own, aims, scal, selectors],
        other_idx, weights=in_hbm(rhs, diag, couple_idx),
        scratch=[((1, ROWS), jnp.int32)], sems=3,
    )
    near, upper, r, cost, targets, labels, selector = lax.optimization_barrier(
        (near, upper, r, cost, targets, labels, selector)
    )
    pair = (PAD, 2 * WIDTH)
    keep, give = call(fetch_kernel, [(pair, F32), (pair, BF16)], near, targets)
    lower = call(lower_kernel, [below], upper)[0]
    sent, us, inv_s = call(
        first_kernel, [msg, scen, scen], keep, other_core(give), labels, r, cost, upper, lower
    )

    near = to_all(sent)
    hot, keep, give = call(label_sum, [hots, sums, sums], near, targets, selector)
    sent, us, ps, sc, d, q, x, r = call(
        second_kernel, [msg, scen, scen, scal, own, own, own, own],
        keep, other_core(give), us, inv_s, r, cost, upper, lower,
    )
    near = to_all(sent)
    keep, give = call(message_sum, [sums, sums], near, hot)
    sent, sc, d, q, x, r = call(
        third_kernel, [msg, scal, own, own, own, own],
        keep, other_core(give), us, ps, inv_s, sc, d, q, x, r, cost, upper, lower,
    )
    near = to_all(sent)
    keep, give = call(message_sum, [sums, sums], near, hot)
    return call(last_kernel, [own, own], keep, other_core(give), sc, d, q, x, r, cost)


def solution(mesh):
    fine = Mesh(np.array(mesh.devices).reshape(4, 2, 4, 4), ("x", "core", "z", "y"))
    vec, scen = ("z", "y"), ("x", "core", "z", "y")
    in_specs = (
        P(vec, None),
        P(vec, None),
        P(scen, None, None, None),
        P(scen, None),
        P(scen, None, None, None, None),
        P(scen, None, None),
    )
    out_specs = (P(vec, None), P(vec, None))
    return jax.shard_map(shards, mesh=fine, in_specs=in_specs, out_specs=out_specs, check_vma=False)
```

```python
import jax
import jax.numpy as jnp
import numpy as np
from jax import lax
from jax.experimental import pallas as pl
from jax.experimental.pallas import tpu as pltpu
from jax.sharding import Mesh
from jax.sharding import PartitionSpec as P

ROWS = 24
PAD = 32
SENT = 26
OWN = 96
HALF = OWN // 2
WIDTH = 128
CHIPS = 64
PLANE = 16
UPPER, LOWER = 3, 2
COPIES = 8
GAMMA, DELTA = 4000, 4001
F32, BF16 = jnp.float32, jnp.bfloat16


def dot_nn(a, b):
    return lax.dot_general(a, b, (((1,), (0,)), ((), ())), preferred_element_type=F32)


def dot_nt(a, b):
    return lax.dot_general(a, b, (((1,), (1,)), ((), ())), preferred_element_type=F32)


def split(values):
    high = values.astype(BF16).astype(F32)
    return high, values - high


def hot_of(mask):
    return mask.astype(F32).astype(BF16)


def only_row(values, r):
    rows = lax.broadcasted_iota(jnp.int32, values.shape, 0)
    return jnp.where(rows == r, values, 0.0).astype(BF16)


def scenario_lift(y, upper, lower):
    rows = lax.broadcasted_iota(jnp.int32, (PAD, WIDTH), 0)
    exact = y.astype(BF16).astype(F32)
    columns = jnp.concatenate([exact] * (WIDTH // PAD), axis=0).T
    half = PAD // 2
    spread = [jnp.zeros((half, UPPER * WIDTH), F32) for group in range(2)]
    below = [jnp.zeros((PAD, WIDTH), F32) for band in range(LOWER)]
    for r in range(0, ROWS, 2):
        group = r // half
        some = y[group * half : (group + 1) * half, :]
        pair = jnp.concatenate([only_row(some, r % half), only_row(some, r % half + 1)], axis=1)
        spread[group] += dot_nn(pair, upper[r : r + 2].reshape(2 * WIDTH, UPPER * WIDTH))
        for d in (r, r + 1):
            for band in range(LOWER):
                c = d + band - LOWER
                if c >= 0:
                    block = lower[d, :, band * WIDTH : (band + 1) * WIDTH].astype(F32)
                    line = column_sum(block * columns[:, d : d + 1])
                    below[band] = jnp.where(rows == c, line, below[band])
    spread = jnp.concatenate(spread, axis=0)
    lifted = spread[:, 0:WIDTH] + below[0] + below[1]
    for band in range(1, UPPER):
        lifted += pltpu.roll(spread[:, band * WIDTH : (band + 1) * WIDTH], band, 0)
    return lifted


def write_message(msg_out, lifted, lines):
    row = lax.broadcasted_iota(jnp.int32, (COPIES * SENT, PAD), 0)
    column = lax.broadcasted_iota(jnp.int32, (COPIES * SENT, PAD), 1)
    again = hot_of(row - SENT * ((row * 2521) >> 16) == column)
    block = dot_nn(again, lifted.astype(BF16))
    row = lax.broadcasted_iota(jnp.int32, (COPIES * SENT, WIDTH), 0)
    row = row - SENT * ((row * 2521) >> 16)
    for place, line in enumerate(lines):
        block = jnp.where(row == ROWS + place, line, block)
    block = block.astype(BF16)
    for start in range(0, CHIPS * SENT, COPIES * SENT):
        msg_out[start : start + COPIES * SENT, :] = block


def column_sum(values):
    return jnp.sum(values, axis=0, keepdims=True)


def products(us, lifted, ru, cuu):
    return column_sum(ru) * 0.125, column_sum(cuu) * 0.125 + column_sum(us * lifted)


def folded(values):
    lane = lax.broadcasted_iota(jnp.int32, (1, WIDTH), 1)
    high, low = split(values + pltpu.roll(values, WIDTH // 2, 1))
    return jnp.where(lane < WIDTH // 2, high, low)


def next_message(msg_out, us, u, r, cost, upper, lower):
    lifted = scenario_lift(us, upper, lower)
    write_message(msg_out, lifted, [folded(v) for v in products(us, lifted, r * u, cost * u * u)])


def as_column(row):
    square = (ROWS, ROWS)
    same = lax.broadcasted_iota(jnp.int32, square, 0) == lax.broadcasted_iota(jnp.int32, square, 1)
    found = jnp.where(same, jnp.broadcast_to(row, square), 0).astype(F32)
    return jnp.broadcast_to(jnp.sum(found, axis=1, keepdims=True), (ROWS, WIDTH))


def scenario_targets(idx):
    rows = lax.broadcasted_iota(jnp.int32, (PAD - ROWS, WIDTH), 0)
    rest = jnp.where(rows < 2, rows + GAMMA, -9)
    return jnp.concatenate([as_column(idx).astype(jnp.int32), rest], axis=0)


def here():
    vec = lax.axis_index("z") * 4 + lax.axis_index("y")
    return lax.axis_index("core"), lax.axis_index("x") * PLANE + vec, vec


def copy_parts(source, target, sems, first, parts):
    step = source.shape[0] // parts
    copies = []
    for part in range(parts):
        rows = pl.ds(part * step, step)
        copies.append(
            pltpu.make_async_copy(source.at[rows], target.at[rows], sems.at[first + part])
        )
    return copies


def normal_kernel(
    pattern_hbm, couple_hbm, factor_hbm, upper, pattern, couple, factor, prod, flip, sems
):
    couples = copy_parts(couple_hbm, couple, sems, 0, 3)
    factors = copy_parts(factor_hbm, factor, sems, 3, 6)
    for part in range(3):
        for copy in (couples[part], factors[2 * part], factors[2 * part + 1]):
            copy.start()
    copy = pltpu.make_async_copy(pattern_hbm, pattern, sems.at[9])
    copy.start()
    copy.wait()
    side = [as_column(pattern[k : k + 1, :]) for k in range(2)]
    zeros = jnp.zeros((WIDTH, WIDTH), BF16)

    def product_row(r):
        for k in range(3):
            c = r + k - 1
            if not 0 <= c < ROWS:
                continue
            block = dot_nn(factor[r, k], couple[c])
            if k != 1:
                block = block * side[k // 2][r : r + 1, :]
            block = block.astype(BF16)
            prod[r, k] = block
            flip[c, :, (2 - k) * WIDTH : (3 - k) * WIDTH] = block.T

    def normal_row(d):
        for band in range(UPPER):
            c = d + band
            at = slice(band * WIDTH, (band + 1) * WIDTH)
            if c >= ROWS:
                upper[d, :, at] = zeros
                continue
            terms = [r for r in (d - 1, d, d + 1) if 0 <= r < ROWS and abs(r - c) <= 1]
            first = terms[0] - d + 1
            left = flip[d, :, first * WIDTH : (first + len(terms)) * WIDTH]
            right = jnp.concatenate([prod[r, c - r + 1] for r in terms], axis=0)
            upper[d, :, at] = dot_nn(left, right).astype(BF16)

    for copy in couples[:2] + factors[:2]:
        copy.wait()
    for r in range(8):
        product_row(r)
    for copy in couples[2:] + factors[2:4]:
        copy.wait()
    for r in range(8, 16):
        product_row(r)
    for d in range(7):
        normal_row(d)
    for copy in factors[4:]:
        copy.wait()
    for r in range(16, 24):
        product_row(r)
    for d in range(7, 12):
        normal_row(d)
    for d in range(12, 18):
        normal_row(d)
    for d in range(18, 24):
        normal_row(d)


def fetched(part, which, want):
    place = lax.broadcasted_iota(jnp.int32, (1, PLANE * HALF), 1)
    block = place + HALF * ((place * 1366) >> 16) + HALF * which
    starts = range(0, PLANE * OWN, OWN)
    start = jnp.concatenate([part[k : k + HALF, :] for k in starts], axis=0)
    inverse = jnp.concatenate([part[k + HALF : k + OWN, :] for k in starts], axis=0)
    return dot_nn(hot_of(want[:, 0:1] == block), jnp.concatenate([start, inverse], axis=1))


def index_kernel(
    other_idx, rhs_hbm, diag_hbm, idx_hbm, rhs, diag, targets, labels, selector, idx, sems
):
    _, chip, vec = here()
    index = pltpu.make_async_copy(idx_hbm, idx, sems.at[2])
    index.start()
    copies = [
        pltpu.make_async_copy(rhs_hbm, rhs, sems.at[0]),
        pltpu.make_async_copy(diag_hbm, diag, sems.at[1]),
    ]
    for copy in copies:
        copy.start()
    row = lax.broadcasted_iota(jnp.int32, (2 * CHIPS, CHIPS * SENT), 0)
    place = lax.broadcasted_iota(jnp.int32, (2 * CHIPS, CHIPS * SENT), 1)
    line = SENT * (row & (CHIPS - 1)) + ROWS + jnp.where(row < CHIPS, 0, 1)
    selector[...] = hot_of(place == line)
    targets[PAD + OWN :, :] = scenario_targets(other_idx[...])
    index.wait()
    want = scenario_targets(idx[...])
    targets[0:PAD, :] = want
    targets[PAD : PAD + OWN, :] = lax.broadcasted_iota(jnp.int32, (OWN, WIDTH), 0) + vec * OWN
    lane = lax.broadcasted_iota(jnp.int32, (ROWS, WIDTH), 1)
    rows = lax.broadcasted_iota(jnp.int32, (ROWS, WIDTH), 0)
    mine = rows == (lane - SENT * chip) & (WIDTH - 1)
    column = want[0:ROWS, :]
    for line, values in enumerate((column >> 8, column & 255)):
        labels[line : line + 1, :] = column_sum(jnp.where(mine, values, 0).astype(F32))
    for copy in copies:
        copy.wait()


def fetch_kernel(near, targets, keep, give):
    want = jnp.concatenate([targets[0:PAD, 0:1], targets[PAD + OWN :, 0:1]], axis=0)
    place = lax.broadcasted_iota(jnp.int32, (1, PLANE * HALF), 1)
    block = place + HALF * ((place * 1366) >> 16) + HALF * lax.axis_index("core")
    starts = range(0, PLANE * OWN, OWN)
    start = jnp.concatenate([near[k : k + HALF, :] for k in starts], axis=0)
    inverse = jnp.concatenate([near[k + HALF : k + OWN, :] for k in starts], axis=0)
    found = dot_nn(hot_of(want == block), jnp.concatenate([start, inverse], axis=1))
    keep[...] = found[0:PAD, :]
    give[...] = found[PAD:, :].astype(BF16)


def lower_kernel(upper, lower):
    lower[0, :, :] = jnp.zeros((WIDTH, LOWER * WIDTH), BF16)
    lower[1, :, 0:WIDTH] = jnp.zeros((WIDTH, WIDTH), BF16)
    for d in range(ROWS):
        for band in range(1, UPPER):
            if d + band < ROWS:
                at = (LOWER - band) * WIDTH
                block = upper[d, :, band * WIDTH : (band + 1) * WIDTH]
                lower[d + band, :, at : at + WIDTH] = block.T


def first_kernel(keep, got, labels, own, cost, upper, lower, msg_out, us_out, inv_out):
    chip = here()[1]
    total = keep[...] + got[...].astype(F32)
    us = total[:, 0:WIDTH]
    us_out[...], inv_out[...] = us, total[:, WIDTH:]
    lifted = scenario_lift(us, upper, lower)
    r = own[...]
    ru = r * (r * (1.0 / cost[...]))
    lane = lax.broadcasted_iota(jnp.int32, (1, WIDTH), 1)
    turned = (lane - SENT * chip) & (WIDTH - 1)
    parts = []
    for k, line in enumerate(products(us, lifted, ru, ru)):
        high, low = split(jnp.sum(line, axis=1, keepdims=True))
        line = labels[k : k + 1, :]
        parts.append(jnp.where(turned == ROWS, high, jnp.where(turned == ROWS + 1, low, line)))
    write_message(msg_out, lifted, parts)


def give_and_keep(found, keep, give):
    keep[...] = found[0 : PAD + OWN, :]
    give[0:PAD, :] = found[PAD + OWN :, :]
    give[PAD:, :] = found[PAD : PAD + OWN, :]


def label_sum(part, targets, selector, hot, keep, give):
    want = targets[...]
    ends = dot_nn(selector[...], part[...])
    first, second = ends[0:CHIPS, :], ends[CHIPS:, :]
    message = lax.broadcasted_iota(jnp.int32, (CHIPS, WIDTH), 0) * SENT
    lane = lax.broadcasted_iota(jnp.int32, (CHIPS, WIDTH), 1)
    turned = (lane - message) & (WIDTH - 1)
    inner = [
        column_sum(jnp.where((turned >= ROWS) & (turned < SENT), e, 0.0)) for e in (first, second)
    ]
    labels = jnp.where(turned < ROWS, first * 256.0 + second, 0.0)
    at_chunk = (message + turned) >> 7
    for chunk in range(CHIPS * SENT // WIDTH):
        start = WIDTH * chunk
        found = column_sum(jnp.where(at_chunk == chunk, labels, 0.0)).astype(jnp.int32)
        place = lax.broadcasted_iota(jnp.int32, (1, WIDTH), 1) + start
        slot = place - SENT * ((place * 2521) >> 16)
        block = jnp.where(slot < ROWS, found, slot - ROWS + GAMMA)
        hot[:, start : start + WIDTH] = hot_of(want == block)
    give_and_keep(dot_nn(hot[...], part[...]), keep, give)
    for ref in (keep, give):
        for k in range(2):
            ref[ROWS + k : ROWS + k + 1, :] = inner[k]


def message_sum(part, hot, keep, give):
    give_and_keep(dot_nn(hot[...], part[...]), keep, give)


def last_sum(part, hot, half):
    half[...] = dot_nn(hot[PAD // 2 : PAD + OWN, :], part[...])


def advance(total, us, inv_s, ps, u, cost, q, d, x, r, per_gamma, per_alpha):
    gamma = jnp.sum(total[ROWS : ROWS + 1, :], axis=1, keepdims=True)
    delta = jnp.sum(total[ROWS + 1 : ROWS + 2, :], axis=1, keepdims=True)
    if per_gamma is None:
        alpha = gamma / delta
    else:
        beta = gamma * per_gamma
        alpha = gamma / (delta - beta * (gamma * per_alpha))
    s = cost * u + total[PAD:, :]
    if per_gamma is None:
        d, q = u, s
    else:
        d, q = u + beta * d, s + beta * q
    x = alpha * d if x is None else x + alpha * d
    r = r - alpha * q
    if us is not None:
        rows = lax.broadcasted_iota(jnp.int32, (PAD, WIDTH), 0)
        own = jnp.where(rows < ROWS, us + inv_s * total[0:PAD, :], 0.0)
        ps = own if ps is None else own + beta * ps
        us = us - alpha * ps
    return gamma, alpha, us, ps, d, q, x, r


def second_kernel(
    keep, got, us, inv_s, own, cost, upper, lower,
    msg_out, us_out, ps_out, scal_out, d_out, q_out, x_out, r_out,
):
    total = keep[...] + got[...]
    d = cost[...]
    inv = 1.0 / d
    r = own[...]
    gamma, alpha, u_s, p_s, dn, qn, xn, rn = advance(
        total, us[...], inv_s[...], None, inv * r, d, None, None, None, r, None, None
    )
    us_out[...], ps_out[...] = u_s, p_s
    d_out[...], q_out[...], x_out[...], r_out[...] = dn, qn, xn, rn
    scal_out[0:1, :] = jnp.broadcast_to(1.0 / gamma, (1, WIDTH))
    scal_out[1:2, :] = jnp.broadcast_to(1.0 / alpha, (1, WIDTH))
    next_message(msg_out, u_s, inv * rn, rn, d, upper, lower)


def third_kernel(
    keep, got, us, ps, inv_s, scal, d, q, x, r, cost, upper, lower,
    msg_out, scal_out, d_out, q_out, x_out, r_out,
):
    total = keep[...] + got[...]
    c = cost[...]
    inv = 1.0 / c
    gamma, alpha, u_s, p_s, dn, qn, xn, rn = advance(
        total, us[...], inv_s[...], ps[...], inv * r[...], c, q[...], d[...], x[...], r[...],
        scal[0:1, 0:1], scal[1:2, 0:1],
    )
    d_out[...], q_out[...], x_out[...], r_out[...] = dn, qn, xn, rn
    scal_out[0:1, :] = jnp.broadcast_to(1.0 / gamma, (1, WIDTH))
    scal_out[1:2, :] = jnp.broadcast_to(1.0 / alpha, (1, WIDTH))
    next_message(msg_out, u_s, inv * rn, rn, c, upper, lower)


def last_kernel(half, got, scal, d, q, x, r, cost, x_out, r_out):
    total = jnp.concatenate([jnp.zeros((PAD // 2, WIDTH), F32), half[...] + got[...]], axis=0)
    c = cost[...]
    found = advance(
        total, None, None, None, r[...] / c, c, q[...], d[...], x[...], r[...],
        scal[0:1, 0:1], scal[1:2, 0:1],
    )
    x_out[...], r_out[...] = found[6], found[7]


def call(kernel, shapes, *args, weights=(), scratch=(), sems=0, hbm_out=False):
    vmem = pl.BlockSpec(memory_space=pltpu.VMEM)
    specs = [vmem] * len(args) + [pl.BlockSpec(memory_space=pltpu.HBM)] * len(weights)
    scratch = [pltpu.VMEM(s, t) for s, t in scratch]
    if sems:
        scratch.append(pltpu.SemaphoreType.DMA((sems,)))
    return pl.pallas_call(
        kernel,
        out_shape=[(pltpu.HBM if hbm_out else jax.ShapeDtypeStruct)(s, t) for s, t in shapes],
        in_specs=specs,
        out_specs=[pl.BlockSpec(memory_space=pltpu.HBM) if hbm_out else vmem] * len(shapes),
        scratch_shapes=scratch,
        compiler_params=pltpu.CompilerParams(vmem_limit_bytes=32 * 1024 * 1024),
    )(*args, *weights)


def in_hbm(*arrays):
    return [pltpu.with_memory_space_constraint(a, pltpu.HBM) for a in arrays]


def other_core(values):
    return lax.ppermute(values, "core", [(0, 1), (1, 0)])


def to_all(sent):
    sent = sent.reshape(CHIPS, SENT // 2, 2, WIDTH)
    near = lax.all_to_all(sent, ("x", "z", "y"), 0, 0, tiled=True)
    return near.reshape(CHIPS * SENT, WIDTH)


def shards(rhs, diag, couple, couple_idx, factor, pattern):
    scen, own, msg = ((PAD, WIDTH), F32), ((OWN, WIDTH), F32), ((CHIPS * SENT, WIDTH), BF16)
    scal, sums = ((2, WIDTH), F32), ((PAD + OWN, WIDTH), F32)
    hots = ((PAD + OWN + PAD, CHIPS * SENT), BF16)
    aims = ((PAD + OWN + PAD, WIDTH), jnp.int32)
    selectors = ((2 * CHIPS, CHIPS * SENT), BF16)
    first = lax.axis_index("core") * HALF
    inverse = 1.0 / lax.dynamic_slice_in_dim(diag, first, HALF, 0)
    start = lax.dynamic_slice_in_dim(rhs, first, HALF, 0) * inverse
    sent = jnp.concatenate([start.astype(BF16), inverse.astype(BF16)], axis=0)
    sent = jnp.broadcast_to(sent[None], (PLANE, OWN, WIDTH))
    near = lax.all_to_all(sent, ("z", "y"), 0, 0, tiled=True)
    near = near.reshape(PLANE * OWN, WIDTH)
    other_idx = other_core(couple_idx)
    triple, wide = (ROWS, 3, WIDTH, WIDTH), (ROWS, WIDTH, 3 * WIDTH)
    bands, below = [((ROWS, WIDTH, n * WIDTH), BF16) for n in (UPPER, LOWER)]
    upper = call(
        normal_kernel, [bands], sems=10,
        weights=in_hbm(pattern[0].T, couple[0], factor[0]),
        scratch=[
            ((2, ROWS), jnp.int32), ((ROWS, WIDTH, WIDTH), BF16), (triple, BF16),
            (triple, BF16), (wide, BF16),
        ],
    )[0]
    r, cost, targets, labels, selector = call(
        index_kernel, [own, own, aims, scal, selectors],
        other_idx, weights=in_hbm(rhs, diag, couple_idx),
        scratch=[((1, ROWS), jnp.int32)], sems=3,
    )
    near, upper, r, cost, targets, labels, selector = lax.optimization_barrier(
        (near, upper, r, cost, targets, labels, selector)
    )
    pair = (PAD, 2 * WIDTH)
    keep, give = call(fetch_kernel, [(pair, F32), (pair, BF16)], near, targets)
    lower = call(lower_kernel, [below], upper)[0]
    sent, us, inv_s = call(
        first_kernel, [msg, scen, scen], keep, other_core(give), labels, r, cost, upper, lower
    )

    near = to_all(sent)
    hot, keep, give = call(label_sum, [hots, sums, sums], near, targets, selector)
    sent, us, ps, sc, d, q, x, r = call(
        second_kernel, [msg, scen, scen, scal, own, own, own, own],
        keep, other_core(give), us, inv_s, r, cost, upper, lower,
    )
    near = to_all(sent)
    keep, give = call(message_sum, [sums, sums], near, hot)
    sent, sc, d, q, x, r = call(
        third_kernel, [msg, scal, own, own, own, own],
        keep, other_core(give), us, ps, inv_s, sc, d, q, x, r, cost, upper, lower,
    )
    near = to_all(sent)
    half = call(last_sum, [((PAD // 2 + OWN, WIDTH), F32)], near, hot)[0]
    return call(last_kernel, [own, own], half, other_core(half), sc, d, q, x, r, cost)


def solution(mesh):
    fine = Mesh(np.array(mesh.devices).reshape(4, 2, 4, 4), ("x", "core", "z", "y"))
    vec, scen = ("z", "y"), ("x", "core", "z", "y")
    in_specs = (
        P(vec, None),
        P(vec, None),
        P(scen, None, None, None),
        P(scen, None),
        P(scen, None, None, None, None),
        P(scen, None, None),
    )
    out_specs = (P(vec, None), P(vec, None))
    return jax.shard_map(shards, mesh=fine, in_specs=in_specs, out_specs=out_specs, check_vma=False)
```

```python
import jax
import jax.numpy as jnp
import numpy as np
from jax import lax
from jax.experimental import pallas as pl
from jax.experimental.pallas import tpu as pltpu
from jax.sharding import Mesh
from jax.sharding import PartitionSpec as P

ROWS = 24
PAD = 32
SENT = 26
OWN = 96
HALF = OWN // 2
WIDTH = 128
CHIPS = 64
PLANE = 16
UPPER, LOWER = 3, 2
COPIES = 8
GAMMA, DELTA = 4000, 4001
F32, BF16 = jnp.float32, jnp.bfloat16


def dot_nn(a, b):
    return lax.dot_general(a, b, (((1,), (0,)), ((), ())), preferred_element_type=F32)


def dot_nt(a, b):
    return lax.dot_general(a, b, (((1,), (1,)), ((), ())), preferred_element_type=F32)


def split(values):
    high = values.astype(BF16).astype(F32)
    return high, values - high


def hot_of(mask):
    return mask.astype(F32).astype(BF16)


def only_row(values, r):
    rows = lax.broadcasted_iota(jnp.int32, values.shape, 0)
    return jnp.where(rows == r, values, 0.0).astype(BF16)


def scenario_lift(y, upper, lower):
    rows = lax.broadcasted_iota(jnp.int32, (PAD, WIDTH), 0)
    exact = y.astype(BF16).astype(F32)
    columns = jnp.concatenate([exact] * (WIDTH // PAD), axis=0).T
    half = PAD // 2
    spread = [jnp.zeros((half, UPPER * WIDTH), F32) for group in range(2)]
    below = [jnp.zeros((PAD, WIDTH), F32) for band in range(LOWER)]
    for r in range(0, ROWS, 2):
        group = r // half
        some = y[group * half : (group + 1) * half, :]
        pair = jnp.concatenate([only_row(some, r % half), only_row(some, r % half + 1)], axis=1)
        spread[group] += dot_nn(pair, upper[r : r + 2].reshape(2 * WIDTH, UPPER * WIDTH))
        for d in (r, r + 1):
            for band in range(LOWER):
                c = d + band - LOWER
                if c >= 0:
                    block = lower[d, :, band * WIDTH : (band + 1) * WIDTH].astype(F32)
                    line = column_sum(block * columns[:, d : d + 1])
                    below[band] = jnp.where(rows == c, line, below[band])
    spread = jnp.concatenate(spread, axis=0)
    lifted = spread[:, 0:WIDTH] + below[0] + below[1]
    for band in range(1, UPPER):
        lifted += pltpu.roll(spread[:, band * WIDTH : (band + 1) * WIDTH], band, 0)
    return lifted


def write_message(msg_out, lifted, lines):
    row = lax.broadcasted_iota(jnp.int32, (COPIES * SENT, PAD), 0)
    column = lax.broadcasted_iota(jnp.int32, (COPIES * SENT, PAD), 1)
    again = hot_of(row - SENT * ((row * 2521) >> 16) == column)
    block = dot_nn(again, lifted.astype(BF16))
    row = lax.broadcasted_iota(jnp.int32, (COPIES * SENT, WIDTH), 0)
    row = row - SENT * ((row * 2521) >> 16)
    for place, line in enumerate(lines):
        block = jnp.where(row == ROWS + place, line, block)
    block = block.astype(BF16)
    for start in range(0, CHIPS * SENT, COPIES * SENT):
        msg_out[start : start + COPIES * SENT, :] = block


def column_sum(values):
    return jnp.sum(values, axis=0, keepdims=True)


def products(us, lifted, ru, cuu):
    return column_sum(ru) * 0.125, column_sum(cuu) * 0.125 + column_sum(us * lifted)


def folded(values):
    lane = lax.broadcasted_iota(jnp.int32, (1, WIDTH), 1)
    high, low = split(values + pltpu.roll(values, WIDTH // 2, 1))
    return jnp.where(lane < WIDTH // 2, high, low)


def next_message(msg_out, us, u, r, cost, upper, lower):
    lifted = scenario_lift(us, upper, lower)
    write_message(msg_out, lifted, [folded(v) for v in products(us, lifted, r * u, cost * u * u)])


def as_column(row):
    square = (ROWS, ROWS)
    same = lax.broadcasted_iota(jnp.int32, square, 0) == lax.broadcasted_iota(jnp.int32, square, 1)
    found = jnp.where(same, jnp.broadcast_to(row, square), 0).astype(F32)
    return jnp.broadcast_to(jnp.sum(found, axis=1, keepdims=True), (ROWS, WIDTH))


def scenario_targets(idx):
    rows = lax.broadcasted_iota(jnp.int32, (PAD - ROWS, WIDTH), 0)
    rest = jnp.where(rows < 2, rows + GAMMA, -9)
    return jnp.concatenate([as_column(idx).astype(jnp.int32), rest], axis=0)


def here():
    vec = lax.axis_index("z") * 4 + lax.axis_index("y")
    chip = lax.axis_index("x") * PLANE + lax.axis_index("y") * 4 + lax.axis_index("z")
    return lax.axis_index("core"), chip, vec


def copy_parts(source, target, sems, first, parts):
    step = source.shape[0] // parts
    copies = []
    for part in range(parts):
        rows = pl.ds(part * step, step)
        copies.append(
            pltpu.make_async_copy(source.at[rows], target.at[rows], sems.at[first + part])
        )
    return copies


def normal_kernel(
    pattern_hbm, couple_hbm, factor_hbm, upper, pattern, couple, factor, prod, flip, sems
):
    couples = copy_parts(couple_hbm, couple, sems, 0, 3)
    factors = copy_parts(factor_hbm, factor, sems, 3, 6)
    for part in range(3):
        for copy in (couples[part], factors[2 * part], factors[2 * part + 1]):
            copy.start()
    copy = pltpu.make_async_copy(pattern_hbm, pattern, sems.at[9])
    copy.start()
    copy.wait()
    side = [as_column(pattern[k : k + 1, :]) for k in range(2)]
    zeros = jnp.zeros((WIDTH, WIDTH), BF16)

    def product_row(r):
        for k in range(3):
            c = r + k - 1
            if not 0 <= c < ROWS:
                continue
            block = dot_nn(factor[r, k], couple[c])
            if k != 1:
                block = block * side[k // 2][r : r + 1, :]
            block = block.astype(BF16)
            prod[r, k] = block
            flip[c, :, (2 - k) * WIDTH : (3 - k) * WIDTH] = block.T

    def normal_row(d):
        for band in range(UPPER):
            c = d + band
            at = slice(band * WIDTH, (band + 1) * WIDTH)
            if c >= ROWS:
                upper[d, :, at] = zeros
                continue
            terms = [r for r in (d - 1, d, d + 1) if 0 <= r < ROWS and abs(r - c) <= 1]
            first = terms[0] - d + 1
            left = flip[d, :, first * WIDTH : (first + len(terms)) * WIDTH]
            right = jnp.concatenate([prod[r, c - r + 1] for r in terms], axis=0)
            upper[d, :, at] = dot_nn(left, right).astype(BF16)

    for copy in couples[:2] + factors[:2]:
        copy.wait()
    for r in range(8):
        product_row(r)
    for copy in couples[2:] + factors[2:4]:
        copy.wait()
    for r in range(8, 16):
        product_row(r)
    for d in range(7):
        normal_row(d)
    for copy in factors[4:]:
        copy.wait()
    for r in range(16, 24):
        product_row(r)
    for d in range(7, 12):
        normal_row(d)
    for d in range(12, 18):
        normal_row(d)
    for d in range(18, 24):
        normal_row(d)


def fetched(part, which, want):
    place = lax.broadcasted_iota(jnp.int32, (1, PLANE * HALF), 1)
    block = place + HALF * ((place * 1366) >> 16) + HALF * which
    starts = range(0, PLANE * OWN, OWN)
    start = jnp.concatenate([part[k : k + HALF, :] for k in starts], axis=0)
    inverse = jnp.concatenate([part[k + HALF : k + OWN, :] for k in starts], axis=0)
    return dot_nn(hot_of(want[:, 0:1] == block), jnp.concatenate([start, inverse], axis=1))


def index_kernel(
    other_idx, rhs_hbm, diag_hbm, idx_hbm, rhs, diag, targets, labels, selector, idx, sems
):
    _, chip, vec = here()
    index = pltpu.make_async_copy(idx_hbm, idx, sems.at[2])
    index.start()
    copies = [
        pltpu.make_async_copy(rhs_hbm, rhs, sems.at[0]),
        pltpu.make_async_copy(diag_hbm, diag, sems.at[1]),
    ]
    for copy in copies:
        copy.start()
    row = lax.broadcasted_iota(jnp.int32, (2 * CHIPS, CHIPS * SENT), 0)
    place = lax.broadcasted_iota(jnp.int32, (2 * CHIPS, CHIPS * SENT), 1)
    line = SENT * (row & (CHIPS - 1)) + ROWS + jnp.where(row < CHIPS, 0, 1)
    selector[...] = hot_of(place == line)
    targets[PAD + OWN :, :] = scenario_targets(other_idx[...])
    index.wait()
    want = scenario_targets(idx[...])
    targets[0:PAD, :] = want
    targets[PAD : PAD + OWN, :] = lax.broadcasted_iota(jnp.int32, (OWN, WIDTH), 0) + vec * OWN
    lane = lax.broadcasted_iota(jnp.int32, (ROWS, WIDTH), 1)
    rows = lax.broadcasted_iota(jnp.int32, (ROWS, WIDTH), 0)
    mine = rows == (lane - SENT * chip) & (WIDTH - 1)
    column = want[0:ROWS, :]
    for line, values in enumerate((column >> 8, column & 255)):
        labels[line : line + 1, :] = column_sum(jnp.where(mine, values, 0).astype(F32))
    for copy in copies:
        copy.wait()


def fetch_kernel(near, targets, keep, give):
    want = jnp.concatenate([targets[0:PAD, 0:1], targets[PAD + OWN :, 0:1]], axis=0)
    place = lax.broadcasted_iota(jnp.int32, (1, PLANE * HALF), 1)
    block = place + HALF * ((place * 1366) >> 16) + HALF * lax.axis_index("core")
    starts = range(0, PLANE * OWN, OWN)
    start = jnp.concatenate([near[k : k + HALF, :] for k in starts], axis=0)
    inverse = jnp.concatenate([near[k + HALF : k + OWN, :] for k in starts], axis=0)
    found = dot_nn(hot_of(want == block), jnp.concatenate([start, inverse], axis=1))
    keep[...] = found[0:PAD, :]
    give[...] = found[PAD:, :].astype(BF16)


def lower_kernel(upper, lower):
    lower[0, :, :] = jnp.zeros((WIDTH, LOWER * WIDTH), BF16)
    lower[1, :, 0:WIDTH] = jnp.zeros((WIDTH, WIDTH), BF16)
    for d in range(ROWS):
        for band in range(1, UPPER):
            if d + band < ROWS:
                at = (LOWER - band) * WIDTH
                block = upper[d, :, band * WIDTH : (band + 1) * WIDTH]
                lower[d + band, :, at : at + WIDTH] = block.T


def first_kernel(keep, got, labels, own, cost, upper, lower, msg_out, us_out, inv_out):
    chip = here()[1]
    total = keep[...] + got[...].astype(F32)
    us = total[:, 0:WIDTH]
    us_out[...], inv_out[...] = us, total[:, WIDTH:]
    lifted = scenario_lift(us, upper, lower)
    r = own[...]
    ru = r * (r * (1.0 / cost[...]))
    lane = lax.broadcasted_iota(jnp.int32, (1, WIDTH), 1)
    turned = (lane - SENT * chip) & (WIDTH - 1)
    parts = []
    for k, line in enumerate(products(us, lifted, ru, ru)):
        high, low = split(jnp.sum(line, axis=1, keepdims=True))
        line = labels[k : k + 1, :]
        parts.append(jnp.where(turned == ROWS, high, jnp.where(turned == ROWS + 1, low, line)))
    write_message(msg_out, lifted, parts)


def give_and_keep(found, keep, give):
    keep[...] = found[0 : PAD + OWN, :]
    give[0:PAD, :] = found[PAD + OWN :, :]
    give[PAD:, :] = found[PAD : PAD + OWN, :]


def label_sum(part, targets, selector, hot, keep, give):
    want = targets[...]
    ends = dot_nn(selector[...], part[...])
    first, second = ends[0:CHIPS, :], ends[CHIPS:, :]
    message = lax.broadcasted_iota(jnp.int32, (CHIPS, WIDTH), 0) * SENT
    lane = lax.broadcasted_iota(jnp.int32, (CHIPS, WIDTH), 1)
    turned = (lane - message) & (WIDTH - 1)
    inner = [
        column_sum(jnp.where((turned >= ROWS) & (turned < SENT), e, 0.0)) for e in (first, second)
    ]
    labels = jnp.where(turned < ROWS, first * 256.0 + second, 0.0)
    at_chunk = (message + turned) >> 7
    for chunk in range(CHIPS * SENT // WIDTH):
        start = WIDTH * chunk
        found = column_sum(jnp.where(at_chunk == chunk, labels, 0.0)).astype(jnp.int32)
        place = lax.broadcasted_iota(jnp.int32, (1, WIDTH), 1) + start
        slot = place - SENT * ((place * 2521) >> 16)
        block = jnp.where(slot < ROWS, found, slot - ROWS + GAMMA)
        hot[:, start : start + WIDTH] = hot_of(want == block)
    give_and_keep(dot_nn(hot[...], part[...]), keep, give)
    for ref in (keep, give):
        for k in range(2):
            ref[ROWS + k : ROWS + k + 1, :] = inner[k]


def message_sum(part, hot, keep, give):
    give_and_keep(dot_nn(hot[...], part[...]), keep, give)


def last_sum(part, hot, half):
    half[...] = dot_nn(hot[PAD // 2 : PAD + OWN, :], part[...])


def advance(total, us, inv_s, ps, u, cost, q, d, x, r, per_gamma, per_alpha):
    gamma = jnp.sum(total[ROWS : ROWS + 1, :], axis=1, keepdims=True)
    delta = jnp.sum(total[ROWS + 1 : ROWS + 2, :], axis=1, keepdims=True)
    if per_gamma is None:
        alpha = gamma / delta
    else:
        beta = gamma * per_gamma
        alpha = gamma / (delta - beta * (gamma * per_alpha))
    s = cost * u + total[PAD:, :]
    if per_gamma is None:
        d, q = u, s
    else:
        d, q = u + beta * d, s + beta * q
    x = alpha * d if x is None else x + alpha * d
    r = r - alpha * q
    if us is not None:
        rows = lax.broadcasted_iota(jnp.int32, (PAD, WIDTH), 0)
        own = jnp.where(rows < ROWS, us + inv_s * total[0:PAD, :], 0.0)
        ps = own if ps is None else own + beta * ps
        us = us - alpha * ps
    return gamma, alpha, us, ps, d, q, x, r


def second_kernel(
    keep, got, us, inv_s, own, cost, upper, lower,
    msg_out, us_out, ps_out, scal_out, d_out, q_out, x_out, r_out,
):
    total = keep[...] + got[...]
    d = cost[...]
    inv = 1.0 / d
    r = own[...]
    gamma, alpha, u_s, p_s, dn, qn, xn, rn = advance(
        total, us[...], inv_s[...], None, inv * r, d, None, None, None, r, None, None
    )
    us_out[...], ps_out[...] = u_s, p_s
    d_out[...], q_out[...], x_out[...], r_out[...] = dn, qn, xn, rn
    scal_out[0:1, :] = jnp.broadcast_to(1.0 / gamma, (1, WIDTH))
    scal_out[1:2, :] = jnp.broadcast_to(1.0 / alpha, (1, WIDTH))
    next_message(msg_out, u_s, inv * rn, rn, d, upper, lower)


def third_kernel(
    keep, got, us, ps, inv_s, scal, d, q, x, r, cost, upper, lower,
    msg_out, scal_out, d_out, q_out, x_out, r_out, u_out,
):
    total = keep[...] + got[...]
    c = cost[...]
    inv = 1.0 / c
    gamma, alpha, u_s, p_s, dn, qn, xn, rn = advance(
        total, us[...], inv_s[...], ps[...], inv * r[...], c, q[...], d[...], x[...], r[...],
        scal[0:1, 0:1], scal[1:2, 0:1],
    )
    d_out[...], q_out[...], x_out[...], r_out[...] = dn, qn, xn, rn
    scal_out[0:1, :] = jnp.broadcast_to(1.0 / gamma, (1, WIDTH))
    scal_out[1:2, :] = jnp.broadcast_to(1.0 / alpha, (1, WIDTH))
    un = inv * rn
    u_out[...] = un
    next_message(msg_out, u_s, un, rn, c, upper, lower)


def last_kernel(half, got, scal, d, q, x, r, u, cost, x_out, r_out):
    total = jnp.concatenate([jnp.zeros((PAD // 2, WIDTH), F32), half[...] + got[...]], axis=0)
    c = cost[...]
    found = advance(
        total, None, None, None, u[...], c, q[...], d[...], x[...], r[...],
        scal[0:1, 0:1], scal[1:2, 0:1],
    )
    x_out[...], r_out[...] = found[6], found[7]


def call(kernel, shapes, *args, weights=(), scratch=(), sems=0, hbm_out=False):
    vmem = pl.BlockSpec(memory_space=pltpu.VMEM)
    specs = [vmem] * len(args) + [pl.BlockSpec(memory_space=pltpu.HBM)] * len(weights)
    scratch = [pltpu.VMEM(s, t) for s, t in scratch]
    if sems:
        scratch.append(pltpu.SemaphoreType.DMA((sems,)))
    return pl.pallas_call(
        kernel,
        out_shape=[(pltpu.HBM if hbm_out else jax.ShapeDtypeStruct)(s, t) for s, t in shapes],
        in_specs=specs,
        out_specs=[pl.BlockSpec(memory_space=pltpu.HBM) if hbm_out else vmem] * len(shapes),
        scratch_shapes=scratch,
        compiler_params=pltpu.CompilerParams(vmem_limit_bytes=32 * 1024 * 1024),
    )(*args, *weights)


def in_hbm(*arrays):
    return [pltpu.with_memory_space_constraint(a, pltpu.HBM) for a in arrays]


def other_core(values):
    return lax.ppermute(values, "core", [(0, 1), (1, 0)])


def to_all(sent):
    sent = sent.reshape(CHIPS, SENT // 2, 2, WIDTH)
    near = lax.all_to_all(sent, ("x", "y", "z"), 0, 0, tiled=True)
    return near.reshape(CHIPS * SENT, WIDTH)


def shards(rhs, diag, couple, couple_idx, factor, pattern):
    scen, own, msg = ((PAD, WIDTH), F32), ((OWN, WIDTH), F32), ((CHIPS * SENT, WIDTH), BF16)
    scal, sums = ((2, WIDTH), F32), ((PAD + OWN, WIDTH), F32)
    hots = ((PAD + OWN + PAD, CHIPS * SENT), BF16)
    aims = ((PAD + OWN + PAD, WIDTH), jnp.int32)
    selectors = ((2 * CHIPS, CHIPS * SENT), BF16)
    first = lax.axis_index("core") * HALF
    inverse = 1.0 / lax.dynamic_slice_in_dim(diag, first, HALF, 0)
    start = lax.dynamic_slice_in_dim(rhs, first, HALF, 0) * inverse
    sent = jnp.concatenate([start.astype(BF16), inverse.astype(BF16)], axis=0)
    sent = jnp.broadcast_to(sent[None], (PLANE, OWN, WIDTH))
    near = lax.all_to_all(sent, ("z", "y"), 0, 0, tiled=True)
    near = near.reshape(PLANE * OWN, WIDTH)
    other_idx = other_core(couple_idx)
    triple, wide = (ROWS, 3, WIDTH, WIDTH), (ROWS, WIDTH, 3 * WIDTH)
    bands, below = [((ROWS, WIDTH, n * WIDTH), BF16) for n in (UPPER, LOWER)]
    upper = call(
        normal_kernel, [bands], sems=10,
        weights=in_hbm(pattern[0].T, couple[0], factor[0]),
        scratch=[
            ((2, ROWS), jnp.int32), ((ROWS, WIDTH, WIDTH), BF16), (triple, BF16),
            (triple, BF16), (wide, BF16),
        ],
    )[0]
    r, cost, targets, labels, selector = call(
        index_kernel, [own, own, aims, scal, selectors],
        other_idx, weights=in_hbm(rhs, diag, couple_idx),
        scratch=[((1, ROWS), jnp.int32)], sems=3,
    )
    near, upper, r, cost, targets, labels, selector = lax.optimization_barrier(
        (near, upper, r, cost, targets, labels, selector)
    )
    pair = (PAD, 2 * WIDTH)
    keep, give = call(fetch_kernel, [(pair, F32), (pair, BF16)], near, targets)
    lower = call(lower_kernel, [below], upper)[0]
    sent, us, inv_s = call(
        first_kernel, [msg, scen, scen], keep, other_core(give), labels, r, cost, upper, lower
    )

    near = to_all(sent)
    hot, keep, give = call(label_sum, [hots, sums, sums], near, targets, selector)
    sent, us, ps, sc, d, q, x, r = call(
        second_kernel, [msg, scen, scen, scal, own, own, own, own],
        keep, other_core(give), us, inv_s, r, cost, upper, lower,
    )
    near = to_all(sent)
    keep, give = call(message_sum, [sums, sums], near, hot)
    sent, sc, d, q, x, r, u = call(
        third_kernel, [msg, scal, own, own, own, own, own],
        keep, other_core(give), us, ps, inv_s, sc, d, q, x, r, cost, upper, lower,
    )
    near = to_all(sent)
    half = call(last_sum, [((PAD // 2 + OWN, WIDTH), F32)], near, hot)[0]
    return call(last_kernel, [own, own], half, other_core(half), sc, d, q, x, r, u, cost)


def solution(mesh):
    fine = Mesh(np.array(mesh.devices).reshape(4, 2, 4, 4), ("x", "core", "z", "y"))
    vec, scen = ("z", "y"), ("x", "core", "z", "y")
    in_specs = (
        P(vec, None),
        P(vec, None),
        P(scen, None, None, None),
        P(scen, None),
        P(scen, None, None, None, None),
        P(scen, None, None),
    )
    out_specs = (P(vec, None), P(vec, None))
    return jax.shard_map(shards, mesh=fine, in_specs=in_specs, out_specs=out_specs, check_vma=False)
```

```python
import jax
import jax.numpy as jnp
import numpy as np
from jax import lax
from jax.experimental import pallas as pl
from jax.experimental.pallas import tpu as pltpu
from jax.sharding import Mesh
from jax.sharding import PartitionSpec as P

ROWS = 24
PAD = 32
SENT = 26
OWN = 96
HALF = OWN // 2
WIDTH = 128
CHIPS = 64
PLANE = 16
UPPER, LOWER = 3, 2
COPIES = 8
GAMMA, DELTA = 4000, 4001
F32, BF16 = jnp.float32, jnp.bfloat16


def dot_nn(a, b):
    return lax.dot_general(a, b, (((1,), (0,)), ((), ())), preferred_element_type=F32)


def dot_nt(a, b):
    return lax.dot_general(a, b, (((1,), (1,)), ((), ())), preferred_element_type=F32)


def split(values):
    high = values.astype(BF16).astype(F32)
    return high, values - high


def hot_of(mask):
    return mask.astype(F32).astype(BF16)


def only_row(values, r):
    rows = lax.broadcasted_iota(jnp.int32, values.shape, 0)
    return jnp.where(rows == r, values, 0.0).astype(BF16)


def scenario_lift(y, upper, lower):
    rows = lax.broadcasted_iota(jnp.int32, (PAD, WIDTH), 0)
    exact = y.astype(BF16).astype(F32)
    columns = jnp.concatenate([exact] * (WIDTH // PAD), axis=0).T
    half = PAD // 2
    spread = [jnp.zeros((half, UPPER * WIDTH), F32) for group in range(2)]
    below = [jnp.zeros((PAD, WIDTH), F32) for band in range(LOWER)]
    for r in range(0, ROWS, 2):
        group = r // half
        some = y[group * half : (group + 1) * half, :]
        pair = jnp.concatenate([only_row(some, r % half), only_row(some, r % half + 1)], axis=1)
        spread[group] += dot_nn(pair, upper[r : r + 2].reshape(2 * WIDTH, UPPER * WIDTH))
        for d in (r, r + 1):
            for band in range(LOWER):
                c = d + band - LOWER
                if c >= 0:
                    block = lower[d, :, band * WIDTH : (band + 1) * WIDTH].astype(F32)
                    line = column_sum(block * columns[:, d : d + 1])
                    below[band] = jnp.where(rows == c, line, below[band])
    spread = jnp.concatenate(spread, axis=0)
    lifted = spread[:, 0:WIDTH] + below[0] + below[1]
    for band in range(1, UPPER):
        lifted += pltpu.roll(spread[:, band * WIDTH : (band + 1) * WIDTH], band, 0)
    return lifted


def write_message(msg_out, lifted, lines):
    row = lax.broadcasted_iota(jnp.int32, (COPIES * SENT, PAD), 0)
    column = lax.broadcasted_iota(jnp.int32, (COPIES * SENT, PAD), 1)
    again = hot_of(row - SENT * ((row * 2521) >> 16) == column)
    block = dot_nn(again, lifted.astype(BF16))
    row = lax.broadcasted_iota(jnp.int32, (COPIES * SENT, WIDTH), 0)
    row = row - SENT * ((row * 2521) >> 16)
    for place, line in enumerate(lines):
        block = jnp.where(row == ROWS + place, line, block)
    block = block.astype(BF16)
    for start in range(0, CHIPS * SENT, COPIES * SENT):
        msg_out[start : start + COPIES * SENT, :] = block


def column_sum(values):
    return jnp.sum(values, axis=0, keepdims=True)


def products(us, lifted, ru, cuu):
    return column_sum(ru) * 0.125, column_sum(cuu) * 0.125 + column_sum(us * lifted)


def folded(values):
    lane = lax.broadcasted_iota(jnp.int32, (1, WIDTH), 1)
    high, low = split(values + pltpu.roll(values, WIDTH // 2, 1))
    return jnp.where(lane < WIDTH // 2, high, low)


def next_message(msg_out, us, u, r, cost, upper, lower):
    lifted = scenario_lift(us, upper, lower)
    write_message(msg_out, lifted, [folded(v) for v in products(us, lifted, r * u, cost * u * u)])


def as_column(row):
    square = (ROWS, ROWS)
    same = lax.broadcasted_iota(jnp.int32, square, 0) == lax.broadcasted_iota(jnp.int32, square, 1)
    found = jnp.where(same, jnp.broadcast_to(row, square), 0).astype(F32)
    return jnp.broadcast_to(jnp.sum(found, axis=1, keepdims=True), (ROWS, WIDTH))


def scenario_targets(idx):
    rows = lax.broadcasted_iota(jnp.int32, (PAD - ROWS, WIDTH), 0)
    rest = jnp.where(rows < 2, rows + GAMMA, -9)
    return jnp.concatenate([as_column(idx).astype(jnp.int32), rest], axis=0)


def here():
    vec = lax.axis_index("z") * 4 + lax.axis_index("y")
    chip = lax.axis_index("x") * PLANE + lax.axis_index("y") * 4 + lax.axis_index("z")
    return lax.axis_index("core"), chip, vec


def copy_parts(source, target, sems, first, parts):
    step = source.shape[0] // parts
    copies = []
    for part in range(parts):
        rows = pl.ds(part * step, step)
        copies.append(
            pltpu.make_async_copy(source.at[rows], target.at[rows], sems.at[first + part])
        )
    return copies


def normal_kernel(
    pattern_hbm, couple_hbm, factor_hbm, upper, pattern, couple, factor, prod, flip, sems
):
    couples = copy_parts(couple_hbm, couple, sems, 0, 3)
    factors = copy_parts(factor_hbm, factor, sems, 3, 6)
    for part in range(3):
        for copy in (couples[part], factors[2 * part], factors[2 * part + 1]):
            copy.start()
    copy = pltpu.make_async_copy(pattern_hbm, pattern, sems.at[9])
    copy.start()
    copy.wait()
    side = [as_column(pattern[k : k + 1, :]) for k in range(2)]
    zeros = jnp.zeros((WIDTH, WIDTH), BF16)

    def product_row(r):
        for k in range(3):
            c = r + k - 1
            if not 0 <= c < ROWS:
                continue
            block = dot_nn(factor[r, k], couple[c])
            if k != 1:
                block = block * side[k // 2][r : r + 1, :]
            block = block.astype(BF16)
            prod[r, k] = block
            flip[c, :, (2 - k) * WIDTH : (3 - k) * WIDTH] = block.T

    def normal_row(d):
        for band in range(UPPER):
            c = d + band
            at = slice(band * WIDTH, (band + 1) * WIDTH)
            if c >= ROWS:
                upper[d, :, at] = zeros
                continue
            terms = [r for r in (d - 1, d, d + 1) if 0 <= r < ROWS and abs(r - c) <= 1]
            first = terms[0] - d + 1
            left = flip[d, :, first * WIDTH : (first + len(terms)) * WIDTH]
            right = jnp.concatenate([prod[r, c - r + 1] for r in terms], axis=0)
            upper[d, :, at] = dot_nn(left, right).astype(BF16)

    for copy in couples[:2] + factors[:2]:
        copy.wait()
    for r in range(8):
        product_row(r)
    for copy in couples[2:] + factors[2:4]:
        copy.wait()
    for r in range(8, 16):
        product_row(r)
    for d in range(7):
        normal_row(d)
    for copy in factors[4:]:
        copy.wait()
    for r in range(16, 24):
        product_row(r)
    for d in range(7, 12):
        normal_row(d)
    for d in range(12, 18):
        normal_row(d)
    for d in range(18, 24):
        normal_row(d)


def fetched(part, which, want):
    place = lax.broadcasted_iota(jnp.int32, (1, PLANE * HALF), 1)
    block = place + HALF * ((place * 1366) >> 16) + HALF * which
    starts = range(0, PLANE * OWN, OWN)
    start = jnp.concatenate([part[k : k + HALF, :] for k in starts], axis=0)
    inverse = jnp.concatenate([part[k + HALF : k + OWN, :] for k in starts], axis=0)
    return dot_nn(hot_of(want[:, 0:1] == block), jnp.concatenate([start, inverse], axis=1))


def index_kernel(
    other_idx, rhs_hbm, diag_hbm, idx_hbm, rhs, diag, inv, targets, labels, selector, idx, sems
):
    _, chip, vec = here()
    index = pltpu.make_async_copy(idx_hbm, idx, sems.at[2])
    index.start()
    copies = [
        pltpu.make_async_copy(rhs_hbm, rhs, sems.at[0]),
        pltpu.make_async_copy(diag_hbm, diag, sems.at[1]),
    ]
    for copy in copies:
        copy.start()
    row = lax.broadcasted_iota(jnp.int32, (2 * CHIPS, CHIPS * SENT), 0)
    place = lax.broadcasted_iota(jnp.int32, (2 * CHIPS, CHIPS * SENT), 1)
    line = SENT * (row & (CHIPS - 1)) + ROWS + jnp.where(row < CHIPS, 0, 1)
    selector[...] = hot_of(place == line)
    targets[PAD + OWN :, :] = scenario_targets(other_idx[...])
    index.wait()
    want = scenario_targets(idx[...])
    targets[0:PAD, :] = want
    targets[PAD : PAD + OWN, :] = lax.broadcasted_iota(jnp.int32, (OWN, WIDTH), 0) + vec * OWN
    lane = lax.broadcasted_iota(jnp.int32, (ROWS, WIDTH), 1)
    rows = lax.broadcasted_iota(jnp.int32, (ROWS, WIDTH), 0)
    mine = rows == (lane - SENT * chip) & (WIDTH - 1)
    column = want[0:ROWS, :]
    for line, values in enumerate((column >> 8, column & 255)):
        labels[line : line + 1, :] = column_sum(jnp.where(mine, values, 0).astype(F32))
    for copy in copies:
        copy.wait()
    inv[...] = 1.0 / diag[...]


def fetch_kernel(near, targets, keep, give):
    want = jnp.concatenate([targets[0:PAD, 0:1], targets[PAD + OWN :, 0:1]], axis=0)
    place = lax.broadcasted_iota(jnp.int32, (1, PLANE * HALF), 1)
    block = place + HALF * ((place * 1366) >> 16) + HALF * lax.axis_index("core")
    starts = range(0, PLANE * OWN, OWN)
    start = jnp.concatenate([near[k : k + HALF, :] for k in starts], axis=0)
    inverse = jnp.concatenate([near[k + HALF : k + OWN, :] for k in starts], axis=0)
    found = dot_nn(hot_of(want == block), jnp.concatenate([start, inverse], axis=1))
    keep[...] = found[0:PAD, :]
    give[...] = found[PAD:, :].astype(BF16)


def lower_kernel(upper, lower):
    lower[0, :, :] = jnp.zeros((WIDTH, LOWER * WIDTH), BF16)
    lower[1, :, 0:WIDTH] = jnp.zeros((WIDTH, WIDTH), BF16)
    for d in range(ROWS):
        for band in range(1, UPPER):
            if d + band < ROWS:
                at = (LOWER - band) * WIDTH
                block = upper[d, :, band * WIDTH : (band + 1) * WIDTH]
                lower[d + band, :, at : at + WIDTH] = block.T


def first_kernel(keep, got, labels, own, inv, upper, lower, msg_out, us_out, inv_out):
    chip = here()[1]
    total = keep[...] + got[...].astype(F32)
    us = total[:, 0:WIDTH]
    us_out[...], inv_out[...] = us, total[:, WIDTH:]
    lifted = scenario_lift(us, upper, lower)
    r = own[...]
    ru = r * (r * inv[...])
    lane = lax.broadcasted_iota(jnp.int32, (1, WIDTH), 1)
    turned = (lane - SENT * chip) & (WIDTH - 1)
    parts = []
    for k, line in enumerate(products(us, lifted, ru, ru)):
        high, low = split(jnp.sum(line, axis=1, keepdims=True))
        line = labels[k : k + 1, :]
        parts.append(jnp.where(turned == ROWS, high, jnp.where(turned == ROWS + 1, low, line)))
    write_message(msg_out, lifted, parts)


def give_and_keep(found, keep, give):
    keep[...] = found[0 : PAD + OWN, :]
    give[0:PAD, :] = found[PAD + OWN :, :]
    give[PAD:, :] = found[PAD : PAD + OWN, :]


def label_sum(part, targets, selector, hot, keep, give):
    want = targets[...]
    ends = dot_nn(selector[...], part[...])
    first, second = ends[0:CHIPS, :], ends[CHIPS:, :]
    message = lax.broadcasted_iota(jnp.int32, (CHIPS, WIDTH), 0) * SENT
    lane = lax.broadcasted_iota(jnp.int32, (CHIPS, WIDTH), 1)
    turned = (lane - message) & (WIDTH - 1)
    inner = [
        column_sum(jnp.where((turned >= ROWS) & (turned < SENT), e, 0.0)) for e in (first, second)
    ]
    labels = jnp.where(turned < ROWS, first * 256.0 + second, 0.0)
    at_chunk = (message + turned) >> 7
    for chunk in range(CHIPS * SENT // WIDTH):
        start = WIDTH * chunk
        found = column_sum(jnp.where(at_chunk == chunk, labels, 0.0)).astype(jnp.int32)
        place = lax.broadcasted_iota(jnp.int32, (1, WIDTH), 1) + start
        slot = place - SENT * ((place * 2521) >> 16)
        block = jnp.where(slot < ROWS, found, slot - ROWS + GAMMA)
        hot[:, start : start + WIDTH] = hot_of(want == block)
    give_and_keep(dot_nn(hot[...], part[...]), keep, give)
    for ref in (keep, give):
        for k in range(2):
            ref[ROWS + k : ROWS + k + 1, :] = inner[k]


def message_sum(part, hot, keep, give):
    give_and_keep(dot_nn(hot[...], part[...]), keep, give)


def last_sum(part, hot, half):
    half[...] = dot_nn(hot[PAD // 2 : PAD + OWN, :], part[...])


def advance(total, us, inv_s, ps, u, cost, q, d, x, r, per_gamma, per_alpha):
    gamma = jnp.sum(total[ROWS : ROWS + 1, :], axis=1, keepdims=True)
    delta = jnp.sum(total[ROWS + 1 : ROWS + 2, :], axis=1, keepdims=True)
    if per_gamma is None:
        alpha = gamma / delta
    else:
        beta = gamma * per_gamma
        alpha = gamma / (delta - beta * (gamma * per_alpha))
    s = cost * u + total[PAD:, :]
    if per_gamma is None:
        d, q = u, s
    else:
        d, q = u + beta * d, s + beta * q
    x = alpha * d if x is None else x + alpha * d
    r = r - alpha * q
    if us is not None:
        rows = lax.broadcasted_iota(jnp.int32, (PAD, WIDTH), 0)
        own = jnp.where(rows < ROWS, us + inv_s * total[0:PAD, :], 0.0)
        ps = own if ps is None else own + beta * ps
        us = us - alpha * ps
    return gamma, alpha, us, ps, d, q, x, r


def second_kernel(
    keep, got, us, inv_s, own, cost, inverse, upper, lower,
    msg_out, us_out, ps_out, scal_out, d_out, q_out, x_out, r_out,
):
    total = keep[...] + got[...]
    d = cost[...]
    inv = inverse[...]
    r = own[...]
    gamma, alpha, u_s, p_s, dn, qn, xn, rn = advance(
        total, us[...], inv_s[...], None, inv * r, d, None, None, None, r, None, None
    )
    us_out[...], ps_out[...] = u_s, p_s
    d_out[...], q_out[...], x_out[...], r_out[...] = dn, qn, xn, rn
    scal_out[0:1, :] = jnp.broadcast_to(1.0 / gamma, (1, WIDTH))
    scal_out[1:2, :] = jnp.broadcast_to(1.0 / alpha, (1, WIDTH))
    next_message(msg_out, u_s, inv * rn, rn, d, upper, lower)


def third_kernel(
    keep, got, us, ps, inv_s, scal, d, q, x, r, cost, inverse, upper, lower,
    msg_out, scal_out, d_out, q_out, x_out, r_out, u_out,
):
    total = keep[...] + got[...]
    c = cost[...]
    inv = inverse[...]
    gamma, alpha, u_s, p_s, dn, qn, xn, rn = advance(
        total, us[...], inv_s[...], ps[...], inv * r[...], c, q[...], d[...], x[...], r[...],
        scal[0:1, 0:1], scal[1:2, 0:1],
    )
    d_out[...], q_out[...], x_out[...], r_out[...] = dn, qn, xn, rn
    scal_out[0:1, :] = jnp.broadcast_to(1.0 / gamma, (1, WIDTH))
    scal_out[1:2, :] = jnp.broadcast_to(1.0 / alpha, (1, WIDTH))
    un = inv * rn
    u_out[...] = un
    next_message(msg_out, u_s, un, rn, c, upper, lower)


def last_kernel(half, got, scal, d, q, x, r, u, cost, x_out, r_out):
    total = jnp.concatenate([jnp.zeros((PAD // 2, WIDTH), F32), half[...] + got[...]], axis=0)
    c = cost[...]
    found = advance(
        total, None, None, None, u[...], c, q[...], d[...], x[...], r[...],
        scal[0:1, 0:1], scal[1:2, 0:1],
    )
    x_out[...], r_out[...] = found[6], found[7]


def call(kernel, shapes, *args, weights=(), scratch=(), sems=0, hbm_out=False):
    vmem = pl.BlockSpec(memory_space=pltpu.VMEM)
    specs = [vmem] * len(args) + [pl.BlockSpec(memory_space=pltpu.HBM)] * len(weights)
    scratch = [pltpu.VMEM(s, t) for s, t in scratch]
    if sems:
        scratch.append(pltpu.SemaphoreType.DMA((sems,)))
    return pl.pallas_call(
        kernel,
        out_shape=[(pltpu.HBM if hbm_out else jax.ShapeDtypeStruct)(s, t) for s, t in shapes],
        in_specs=specs,
        out_specs=[pl.BlockSpec(memory_space=pltpu.HBM) if hbm_out else vmem] * len(shapes),
        scratch_shapes=scratch,
        compiler_params=pltpu.CompilerParams(vmem_limit_bytes=32 * 1024 * 1024),
    )(*args, *weights)


def in_hbm(*arrays):
    return [pltpu.with_memory_space_constraint(a, pltpu.HBM) for a in arrays]


def other_core(values):
    return lax.ppermute(values, "core", [(0, 1), (1, 0)])


def to_all(sent):
    sent = sent.reshape(CHIPS, SENT // 2, 2, WIDTH)
    near = lax.all_to_all(sent, ("x", "y", "z"), 0, 0, tiled=True)
    return near.reshape(CHIPS * SENT, WIDTH)


def shards(rhs, diag, couple, couple_idx, factor, pattern):
    scen, own, msg = ((PAD, WIDTH), F32), ((OWN, WIDTH), F32), ((CHIPS * SENT, WIDTH), BF16)
    scal, sums = ((2, WIDTH), F32), ((PAD + OWN, WIDTH), F32)
    hots = ((PAD + OWN + PAD, CHIPS * SENT), BF16)
    aims = ((PAD + OWN + PAD, WIDTH), jnp.int32)
    selectors = ((2 * CHIPS, CHIPS * SENT), BF16)
    first = lax.axis_index("core") * HALF
    inverse = 1.0 / lax.dynamic_slice_in_dim(diag, first, HALF, 0)
    start = lax.dynamic_slice_in_dim(rhs, first, HALF, 0) * inverse
    sent = jnp.concatenate([start.astype(BF16), inverse.astype(BF16)], axis=0)
    sent = jnp.broadcast_to(sent[None], (PLANE, OWN, WIDTH))
    near = lax.all_to_all(sent, ("z", "y"), 0, 0, tiled=True)
    near = near.reshape(PLANE * OWN, WIDTH)
    other_idx = other_core(couple_idx)
    triple, wide = (ROWS, 3, WIDTH, WIDTH), (ROWS, WIDTH, 3 * WIDTH)
    bands, below = [((ROWS, WIDTH, n * WIDTH), BF16) for n in (UPPER, LOWER)]
    upper = call(
        normal_kernel, [bands], sems=10,
        weights=in_hbm(pattern[0].T, couple[0], factor[0]),
        scratch=[
            ((2, ROWS), jnp.int32), ((ROWS, WIDTH, WIDTH), BF16), (triple, BF16),
            (triple, BF16), (wide, BF16),
        ],
    )[0]
    r, cost, inv, targets, labels, selector = call(
        index_kernel, [own, own, own, aims, scal, selectors],
        other_idx, weights=in_hbm(rhs, diag, couple_idx),
        scratch=[((1, ROWS), jnp.int32)], sems=3,
    )
    near, upper, r, cost, inv, targets, labels, selector = lax.optimization_barrier(
        (near, upper, r, cost, inv, targets, labels, selector)
    )
    pair = (PAD, 2 * WIDTH)
    keep, give = call(fetch_kernel, [(pair, F32), (pair, BF16)], near, targets)
    lower = call(lower_kernel, [below], upper)[0]
    sent, us, inv_s = call(
        first_kernel, [msg, scen, scen], keep, other_core(give), labels, r, inv, upper, lower
    )

    near = to_all(sent)
    hot, keep, give = call(label_sum, [hots, sums, sums], near, targets, selector)
    sent, us, ps, sc, d, q, x, r = call(
        second_kernel, [msg, scen, scen, scal, own, own, own, own],
        keep, other_core(give), us, inv_s, r, cost, inv, upper, lower,
    )
    near = to_all(sent)
    keep, give = call(message_sum, [sums, sums], near, hot)
    sent, sc, d, q, x, r, u = call(
        third_kernel, [msg, scal, own, own, own, own, own],
        keep, other_core(give), us, ps, inv_s, sc, d, q, x, r, cost, inv, upper, lower,
    )
    near = to_all(sent)
    half = call(last_sum, [((PAD // 2 + OWN, WIDTH), F32)], near, hot)[0]
    return call(last_kernel, [own, own], half, other_core(half), sc, d, q, x, r, u, cost)


def solution(mesh):
    fine = Mesh(np.array(mesh.devices).reshape(4, 2, 4, 4), ("x", "core", "z", "y"))
    vec, scen = ("z", "y"), ("x", "core", "z", "y")
    in_specs = (
        P(vec, None),
        P(vec, None),
        P(scen, None, None, None),
        P(scen, None),
        P(scen, None, None, None, None),
        P(scen, None, None),
    )
    out_specs = (P(vec, None), P(vec, None))
    return jax.shard_map(shards, mesh=fine, in_specs=in_specs, out_specs=out_specs, check_vma=False)
```

```python
import jax
import jax.numpy as jnp
import numpy as np
from jax import lax
from jax.experimental import pallas as pl
from jax.experimental.pallas import tpu as pltpu
from jax.sharding import Mesh
from jax.sharding import PartitionSpec as P

ROWS = 24
PAD = 32
SENT = 26
OWN = 96
HALF = OWN // 2
WIDTH = 128
CHIPS = 64
PLANE = 16
UPPER, LOWER = 3, 2
COPIES = 8
GAMMA, DELTA = 4000, 4001
F32, BF16 = jnp.float32, jnp.bfloat16


def dot_nn(a, b):
    return lax.dot_general(a, b, (((1,), (0,)), ((), ())), preferred_element_type=F32)


def dot_nt(a, b):
    return lax.dot_general(a, b, (((1,), (1,)), ((), ())), preferred_element_type=F32)


def split(values):
    high = values.astype(BF16).astype(F32)
    return high, values - high


def hot_of(mask):
    return mask.astype(F32).astype(BF16)


def only_row(values, r):
    rows = lax.broadcasted_iota(jnp.int32, values.shape, 0)
    return jnp.where(rows == r, values, 0.0).astype(BF16)


def scenario_lift(y, upper, lower):
    rows = lax.broadcasted_iota(jnp.int32, (PAD, WIDTH), 0)
    exact = y.astype(BF16).astype(F32)
    columns = jnp.concatenate([exact] * (WIDTH // PAD), axis=0).T
    half = PAD // 4
    spread = [jnp.zeros((half, UPPER * WIDTH), F32) for group in range(4)]
    below = [jnp.zeros((PAD, WIDTH), F32) for band in range(LOWER)]
    for r in range(0, ROWS, 2):
        group = r // half
        some = y[group * half : (group + 1) * half, :]
        pair = jnp.concatenate([only_row(some, r % half), only_row(some, r % half + 1)], axis=1)
        spread[group] += dot_nn(pair, upper[r : r + 2].reshape(2 * WIDTH, UPPER * WIDTH))
        for d in (r, r + 1):
            for band in range(LOWER):
                c = d + band - LOWER
                if c >= 0:
                    block = lower[d, :, band * WIDTH : (band + 1) * WIDTH].astype(F32)
                    line = column_sum(block * columns[:, d : d + 1])
                    below[band] = jnp.where(rows == c, line, below[band])
    spread = jnp.concatenate(spread, axis=0)
    lifted = spread[:, 0:WIDTH] + below[0] + below[1]
    for band in range(1, UPPER):
        lifted += pltpu.roll(spread[:, band * WIDTH : (band + 1) * WIDTH], band, 0)
    return lifted


def write_message(msg_out, lifted, lines):
    row = lax.broadcasted_iota(jnp.int32, (COPIES * SENT, PAD), 0)
    column = lax.broadcasted_iota(jnp.int32, (COPIES * SENT, PAD), 1)
    again = hot_of(row - SENT * ((row * 2521) >> 16) == column)
    block = dot_nn(again, lifted.astype(BF16))
    row = lax.broadcasted_iota(jnp.int32, (COPIES * SENT, WIDTH), 0)
    row = row - SENT * ((row * 2521) >> 16)
    for place, line in enumerate(lines):
        block = jnp.where(row == ROWS + place, line, block)
    block = block.astype(BF16)
    for start in range(0, CHIPS * SENT, COPIES * SENT):
        msg_out[start : start + COPIES * SENT, :] = block


def column_sum(values):
    return jnp.sum(values, axis=0, keepdims=True)


def products(us, lifted, ru, cuu):
    return column_sum(ru) * 0.125, column_sum(cuu) * 0.125 + column_sum(us * lifted)


def folded(values):
    lane = lax.broadcasted_iota(jnp.int32, (1, WIDTH), 1)
    high, low = split(values + pltpu.roll(values, WIDTH // 2, 1))
    return jnp.where(lane < WIDTH // 2, high, low)


def next_message(msg_out, us, u, r, cost, upper, lower):
    lifted = scenario_lift(us, upper, lower)
    write_message(msg_out, lifted, [folded(v) for v in products(us, lifted, r * u, cost * u * u)])


def as_column(row):
    square = (ROWS, ROWS)
    same = lax.broadcasted_iota(jnp.int32, square, 0) == lax.broadcasted_iota(jnp.int32, square, 1)
    found = jnp.where(same, jnp.broadcast_to(row, square), 0).astype(F32)
    return jnp.broadcast_to(jnp.sum(found, axis=1, keepdims=True), (ROWS, WIDTH))


def scenario_targets(idx):
    rows = lax.broadcasted_iota(jnp.int32, (PAD - ROWS, WIDTH), 0)
    rest = jnp.where(rows < 2, rows + GAMMA, -9)
    return jnp.concatenate([as_column(idx).astype(jnp.int32), rest], axis=0)


def here():
    vec = lax.axis_index("z") * 4 + lax.axis_index("y")
    chip = lax.axis_index("x") * PLANE + lax.axis_index("y") * 4 + lax.axis_index("z")
    return lax.axis_index("core"), chip, vec


def copy_parts(source, target, sems, first, parts):
    step = source.shape[0] // parts
    copies = []
    for part in range(parts):
        rows = pl.ds(part * step, step)
        copies.append(
            pltpu.make_async_copy(source.at[rows], target.at[rows], sems.at[first + part])
        )
    return copies


def normal_kernel(
    pattern_hbm, couple_hbm, factor_hbm, upper, pattern, couple, factor, prod, flip, sems
):
    couples = copy_parts(couple_hbm, couple, sems, 0, 3)
    factors = copy_parts(factor_hbm, factor, sems, 3, 6)
    for part in range(3):
        for copy in (couples[part], factors[2 * part], factors[2 * part + 1]):
            copy.start()
    copy = pltpu.make_async_copy(pattern_hbm, pattern, sems.at[9])
    copy.start()
    copy.wait()
    side = [as_column(pattern[k : k + 1, :]) for k in range(2)]
    zeros = jnp.zeros((WIDTH, WIDTH), BF16)

    def product_row(r):
        for k in range(3):
            c = r + k - 1
            if not 0 <= c < ROWS:
                continue
            block = dot_nn(factor[r, k], couple[c])
            if k != 1:
                block = block * side[k // 2][r : r + 1, :]
            block = block.astype(BF16)
            prod[r, k] = block
            flip[c, :, (2 - k) * WIDTH : (3 - k) * WIDTH] = block.T

    def normal_row(d):
        for band in range(UPPER):
            c = d + band
            at = slice(band * WIDTH, (band + 1) * WIDTH)
            if c >= ROWS:
                upper[d, :, at] = zeros
                continue
            terms = [r for r in (d - 1, d, d + 1) if 0 <= r < ROWS and abs(r - c) <= 1]
            first = terms[0] - d + 1
            left = flip[d, :, first * WIDTH : (first + len(terms)) * WIDTH]
            right = jnp.concatenate([prod[r, c - r + 1] for r in terms], axis=0)
            upper[d, :, at] = dot_nn(left, right).astype(BF16)

    for copy in couples[:2] + factors[:2]:
        copy.wait()
    for r in range(8):
        product_row(r)
    for copy in couples[2:] + factors[2:4]:
        copy.wait()
    for r in range(8, 16):
        product_row(r)
    for d in range(7):
        normal_row(d)
    for copy in factors[4:]:
        copy.wait()
    for r in range(16, 24):
        product_row(r)
    for d in range(7, 12):
        normal_row(d)
    for d in range(12, 18):
        normal_row(d)
    for d in range(18, 24):
        normal_row(d)


def fetched(part, which, want):
    place = lax.broadcasted_iota(jnp.int32, (1, PLANE * HALF), 1)
    block = place + HALF * ((place * 1366) >> 16) + HALF * which
    starts = range(0, PLANE * OWN, OWN)
    start = jnp.concatenate([part[k : k + HALF, :] for k in starts], axis=0)
    inverse = jnp.concatenate([part[k + HALF : k + OWN, :] for k in starts], axis=0)
    return dot_nn(hot_of(want[:, 0:1] == block), jnp.concatenate([start, inverse], axis=1))


def index_kernel(
    other_idx, rhs_hbm, diag_hbm, idx_hbm, rhs, diag, targets, labels, selector, idx, sems
):
    _, chip, vec = here()
    index = pltpu.make_async_copy(idx_hbm, idx, sems.at[2])
    index.start()
    copies = [
        pltpu.make_async_copy(rhs_hbm, rhs, sems.at[0]),
        pltpu.make_async_copy(diag_hbm, diag, sems.at[1]),
    ]
    for copy in copies:
        copy.start()
    row = lax.broadcasted_iota(jnp.int32, (2 * CHIPS, CHIPS * SENT), 0)
    place = lax.broadcasted_iota(jnp.int32, (2 * CHIPS, CHIPS * SENT), 1)
    line = SENT * (row & (CHIPS - 1)) + ROWS + jnp.where(row < CHIPS, 0, 1)
    selector[...] = hot_of(place == line)
    targets[PAD + OWN :, :] = scenario_targets(other_idx[...])
    index.wait()
    want = scenario_targets(idx[...])
    targets[0:PAD, :] = want
    targets[PAD : PAD + OWN, :] = lax.broadcasted_iota(jnp.int32, (OWN, WIDTH), 0) + vec * OWN
    lane = lax.broadcasted_iota(jnp.int32, (ROWS, WIDTH), 1)
    rows = lax.broadcasted_iota(jnp.int32, (ROWS, WIDTH), 0)
    mine = rows == (lane - SENT * chip) & (WIDTH - 1)
    column = want[0:ROWS, :]
    for line, values in enumerate((column >> 8, column & 255)):
        labels[line : line + 1, :] = column_sum(jnp.where(mine, values, 0).astype(F32))
    for copy in copies:
        copy.wait()


def fetch_kernel(near, targets, keep, give):
    want = jnp.concatenate([targets[0:PAD, 0:1], targets[PAD + OWN :, 0:1]], axis=0)
    place = lax.broadcasted_iota(jnp.int32, (1, PLANE * HALF), 1)
    block = place + HALF * ((place * 1366) >> 16) + HALF * lax.axis_index("core")
    starts = range(0, PLANE * OWN, OWN)
    start = jnp.concatenate([near[k : k + HALF, :] for k in starts], axis=0)
    inverse = jnp.concatenate([near[k + HALF : k + OWN, :] for k in starts], axis=0)
    found = dot_nn(hot_of(want == block), jnp.concatenate([start, inverse], axis=1))
    keep[...] = found[0:PAD, :]
    give[...] = found[PAD:, :].astype(BF16)


def lower_kernel(upper, lower):
    lower[0, :, :] = jnp.zeros((WIDTH, LOWER * WIDTH), BF16)
    lower[1, :, 0:WIDTH] = jnp.zeros((WIDTH, WIDTH), BF16)
    for d in range(ROWS):
        for band in range(1, UPPER):
            if d + band < ROWS:
                at = (LOWER - band) * WIDTH
                block = upper[d, :, band * WIDTH : (band + 1) * WIDTH]
                lower[d + band, :, at : at + WIDTH] = block.T


def first_kernel(keep, got, labels, own, cost, upper, lower, msg_out, us_out, inv_out):
    chip = here()[1]
    total = keep[...] + got[...].astype(F32)
    us = total[:, 0:WIDTH]
    us_out[...], inv_out[...] = us, total[:, WIDTH:]
    lifted = scenario_lift(us, upper, lower)
    r = own[...]
    ru = r * (r * (1.0 / cost[...]))
    lane = lax.broadcasted_iota(jnp.int32, (1, WIDTH), 1)
    turned = (lane - SENT * chip) & (WIDTH - 1)
    parts = []
    for k, line in enumerate(products(us, lifted, ru, ru)):
        high, low = split(jnp.sum(line, axis=1, keepdims=True))
        line = labels[k : k + 1, :]
        parts.append(jnp.where(turned == ROWS, high, jnp.where(turned == ROWS + 1, low, line)))
    write_message(msg_out, lifted, parts)


def give_and_keep(found, keep, give):
    keep[...] = found[0 : PAD + OWN, :]
    give[0:PAD, :] = found[PAD + OWN :, :]
    give[PAD:, :] = found[PAD : PAD + OWN, :]


def label_sum(part, targets, selector, hot, keep, give):
    want = targets[...]
    ends = dot_nn(selector[...], part[...])
    first, second = ends[0:CHIPS, :], ends[CHIPS:, :]
    message = lax.broadcasted_iota(jnp.int32, (CHIPS, WIDTH), 0) * SENT
    lane = lax.broadcasted_iota(jnp.int32, (CHIPS, WIDTH), 1)
    turned = (lane - message) & (WIDTH - 1)
    inner = [
        column_sum(jnp.where((turned >= ROWS) & (turned < SENT), e, 0.0)) for e in (first, second)
    ]
    labels = jnp.where(turned < ROWS, first * 256.0 + second, 0.0)
    at_chunk = (message + turned) >> 7
    for chunk in range(CHIPS * SENT // WIDTH):
        start = WIDTH * chunk
        found = column_sum(jnp.where(at_chunk == chunk, labels, 0.0)).astype(jnp.int32)
        place = lax.broadcasted_iota(jnp.int32, (1, WIDTH), 1) + start
        slot = place - SENT * ((place * 2521) >> 16)
        block = jnp.where(slot < ROWS, found, slot - ROWS + GAMMA)
        hot[:, start : start + WIDTH] = hot_of(want == block)
    give_and_keep(dot_nn(hot[...], part[...]), keep, give)
    for ref in (keep, give):
        for k in range(2):
            ref[ROWS + k : ROWS + k + 1, :] = inner[k]


def message_sum(part, hot, keep, give):
    give_and_keep(dot_nn(hot[...], part[...]), keep, give)


def last_sum(part, hot, half):
    half[...] = dot_nn(hot[PAD // 2 : PAD + OWN, :], part[...])


def advance(total, us, inv_s, ps, u, cost, q, d, x, r, per_gamma, per_alpha):
    gamma = jnp.sum(total[ROWS : ROWS + 1, :], axis=1, keepdims=True)
    delta = jnp.sum(total[ROWS + 1 : ROWS + 2, :], axis=1, keepdims=True)
    if per_gamma is None:
        alpha = gamma / delta
    else:
        beta = gamma * per_gamma
        alpha = gamma / (delta - beta * (gamma * per_alpha))
    s = cost * u + total[PAD:, :]
    if per_gamma is None:
        d, q = u, s
    else:
        d, q = u + beta * d, s + beta * q
    x = alpha * d if x is None else x + alpha * d
    r = r - alpha * q
    if us is not None:
        rows = lax.broadcasted_iota(jnp.int32, (PAD, WIDTH), 0)
        own = jnp.where(rows < ROWS, us + inv_s * total[0:PAD, :], 0.0)
        ps = own if ps is None else own + beta * ps
        us = us - alpha * ps
    return gamma, alpha, us, ps, d, q, x, r


def second_kernel(
    keep, got, us, inv_s, own, cost, upper, lower,
    msg_out, us_out, ps_out, scal_out, d_out, q_out, x_out, r_out,
):
    total = keep[...] + got[...]
    d = cost[...]
    inv = 1.0 / d
    r = own[...]
    gamma, alpha, u_s, p_s, dn, qn, xn, rn = advance(
        total, us[...], inv_s[...], None, inv * r, d, None, None, None, r, None, None
    )
    us_out[...], ps_out[...] = u_s, p_s
    d_out[...], q_out[...], x_out[...], r_out[...] = dn, qn, xn, rn
    scal_out[0:1, :] = jnp.broadcast_to(1.0 / gamma, (1, WIDTH))
    scal_out[1:2, :] = jnp.broadcast_to(1.0 / alpha, (1, WIDTH))
    next_message(msg_out, u_s, inv * rn, rn, d, upper, lower)


def third_kernel(
    keep, got, us, ps, inv_s, scal, d, q, x, r, cost, upper, lower,
    msg_out, scal_out, d_out, q_out, x_out, r_out, u_out,
):
    total = keep[...] + got[...]
    c = cost[...]
    inv = 1.0 / c
    gamma, alpha, u_s, p_s, dn, qn, xn, rn = advance(
        total, us[...], inv_s[...], ps[...], inv * r[...], c, q[...], d[...], x[...], r[...],
        scal[0:1, 0:1], scal[1:2, 0:1],
    )
    d_out[...], q_out[...], x_out[...], r_out[...] = dn, qn, xn, rn
    scal_out[0:1, :] = jnp.broadcast_to(1.0 / gamma, (1, WIDTH))
    scal_out[1:2, :] = jnp.broadcast_to(1.0 / alpha, (1, WIDTH))
    un = inv * rn
    u_out[...] = un
    next_message(msg_out, u_s, un, rn, c, upper, lower)


def last_kernel(half, got, scal, d, q, x, r, u, cost, x_out, r_out):
    total = jnp.concatenate([jnp.zeros((PAD // 2, WIDTH), F32), half[...] + got[...]], axis=0)
    c = cost[...]
    found = advance(
        total, None, None, None, u[...], c, q[...], d[...], x[...], r[...],
        scal[0:1, 0:1], scal[1:2, 0:1],
    )
    x_out[...], r_out[...] = found[6], found[7]


def call(kernel, shapes, *args, weights=(), scratch=(), sems=0, hbm_out=False):
    vmem = pl.BlockSpec(memory_space=pltpu.VMEM)
    specs = [vmem] * len(args) + [pl.BlockSpec(memory_space=pltpu.HBM)] * len(weights)
    scratch = [pltpu.VMEM(s, t) for s, t in scratch]
    if sems:
        scratch.append(pltpu.SemaphoreType.DMA((sems,)))
    return pl.pallas_call(
        kernel,
        out_shape=[(pltpu.HBM if hbm_out else jax.ShapeDtypeStruct)(s, t) for s, t in shapes],
        in_specs=specs,
        out_specs=[pl.BlockSpec(memory_space=pltpu.HBM) if hbm_out else vmem] * len(shapes),
        scratch_shapes=scratch,
        compiler_params=pltpu.CompilerParams(vmem_limit_bytes=32 * 1024 * 1024),
    )(*args, *weights)


def in_hbm(*arrays):
    return [pltpu.with_memory_space_constraint(a, pltpu.HBM) for a in arrays]


def other_core(values):
    return lax.ppermute(values, "core", [(0, 1), (1, 0)])


def to_all(sent):
    sent = sent.reshape(CHIPS, SENT // 2, 2, WIDTH)
    near = lax.all_to_all(sent, ("x", "y", "z"), 0, 0, tiled=True)
    return near.reshape(CHIPS * SENT, WIDTH)


def shards(rhs, diag, couple, couple_idx, factor, pattern):
    scen, own, msg = ((PAD, WIDTH), F32), ((OWN, WIDTH), F32), ((CHIPS * SENT, WIDTH), BF16)
    scal, sums = ((2, WIDTH), F32), ((PAD + OWN, WIDTH), F32)
    hots = ((PAD + OWN + PAD, CHIPS * SENT), BF16)
    aims = ((PAD + OWN + PAD, WIDTH), jnp.int32)
    selectors = ((2 * CHIPS, CHIPS * SENT), BF16)
    first = lax.axis_index("core") * HALF
    inverse = 1.0 / lax.dynamic_slice_in_dim(diag, first, HALF, 0)
    start = lax.dynamic_slice_in_dim(rhs, first, HALF, 0) * inverse
    sent = jnp.concatenate([start.astype(BF16), inverse.astype(BF16)], axis=0)
    sent = jnp.broadcast_to(sent[None], (PLANE, OWN, WIDTH))
    near = lax.all_to_all(sent, ("z", "y"), 0, 0, tiled=True)
    near = near.reshape(PLANE * OWN, WIDTH)
    other_idx = other_core(couple_idx)
    triple, wide = (ROWS, 3, WIDTH, WIDTH), (ROWS, WIDTH, 3 * WIDTH)
    bands, below = [((ROWS, WIDTH, n * WIDTH), BF16) for n in (UPPER, LOWER)]
    upper = call(
        normal_kernel, [bands], sems=10,
        weights=in_hbm(pattern[0].T, couple[0], factor[0]),
        scratch=[
            ((2, ROWS), jnp.int32), ((ROWS, WIDTH, WIDTH), BF16), (triple, BF16),
            (triple, BF16), (wide, BF16),
        ],
    )[0]
    r, cost, targets, labels, selector = call(
        index_kernel, [own, own, aims, scal, selectors],
        other_idx, weights=in_hbm(rhs, diag, couple_idx),
        scratch=[((1, ROWS), jnp.int32)], sems=3,
    )
    near, upper, r, cost, targets, labels, selector = lax.optimization_barrier(
        (near, upper, r, cost, targets, labels, selector)
    )
    pair = (PAD, 2 * WIDTH)
    keep, give = call(fetch_kernel, [(pair, F32), (pair, BF16)], near, targets)
    lower = call(lower_kernel, [below], upper)[0]
    sent, us, inv_s = call(
        first_kernel, [msg, scen, scen], keep, other_core(give), labels, r, cost, upper, lower
    )

    near = to_all(sent)
    hot, keep, give = call(label_sum, [hots, sums, sums], near, targets, selector)
    sent, us, ps, sc, d, q, x, r = call(
        second_kernel, [msg, scen, scen, scal, own, own, own, own],
        keep, other_core(give), us, inv_s, r, cost, upper, lower,
    )
    near = to_all(sent)
    keep, give = call(message_sum, [sums, sums], near, hot)
    sent, sc, d, q, x, r, u = call(
        third_kernel, [msg, scal, own, own, own, own, own],
        keep, other_core(give), us, ps, inv_s, sc, d, q, x, r, cost, upper, lower,
    )
    near = to_all(sent)
    half = call(last_sum, [((PAD // 2 + OWN, WIDTH), F32)], near, hot)[0]
    return call(last_kernel, [own, own], half, other_core(half), sc, d, q, x, r, u, cost)


def solution(mesh):
    fine = Mesh(np.array(mesh.devices).reshape(4, 2, 4, 4), ("x", "core", "z", "y"))
    vec, scen = ("z", "y"), ("x", "core", "z", "y")
    in_specs = (
        P(vec, None),
        P(vec, None),
        P(scen, None, None, None),
        P(scen, None),
        P(scen, None, None, None, None),
        P(scen, None, None),
    )
    out_specs = (P(vec, None), P(vec, None))
    return jax.shard_map(shards, mesh=fine, in_specs=in_specs, out_specs=out_specs, check_vma=False)
```
